32 devices in a mesh: dp: 8 (over z, x), fsdp: 4 (over y, core).
Axes of the slice: x: 2, y: 2, z: 4, core: 2. Of those that a mesh axis runs over, the one named last changes fastest.
Arguments:
- hidden: bfloat16 [8192, 4, 1024], P(('dp', 'fsdp')), may hold values from -108 to 108
- head: bfloat16 [4, 1024, 1024], P('fsdp', 'dp'), may hold values from -14 to 14
- gain: bfloat16 [4, 1024], P('fsdp', 'dp'), may hold values from 0.5 to 1.5
- targets: int32 [8192, 4], P('dp', 'fsdp'), may hold values from 0 to 1023
- lengths: int32 [8], replicated, may hold values from 256 to 1024, as said below
Outputs:
- loss: float32 [], replicated
- grad_hidden: bfloat16 [8192, 4, 1024], P(('dp', 'fsdp'))
- grad_head: float32 [4, 1024, 1024], P('fsdp', 'dp')
The draws below stay inside these ranges and needn't reach their ends.
Inputs may be any that keep to these rules, and one draw needn't show every extreme that they name: `lengths`: each dialogue has at least 256 valid frames, and some dialogue has all 1024.
All inputs are finite; a program needn't handle non-finite values.
Results may differ from the reference program's by a relative error of at most 0.015.
Values may be sent and summed in bfloat16 or wider, within the bound.
No kernel may reach another device: no remote copies, remote signals or barrier semaphores. Data moves between devices by JAX's collectives and lax.ppermute only.
A program may use at most 64 MiB of HBM per device.

```python
import math
import jax
import jax.numpy as jnp
from jax import lax

E = 1024
CARD = 1024
LEN = 1024
POS = 4
DIALOGS = 8
FRAMES = 8192


def shared_parts(key):
    row_weights = jnp.exp(jax.random.uniform(jax.random.fold_in(key, 2), (E,), jnp.float32, math.log(0.3), math.log(3.0)))
    return row_weights


def draw_hidden(key, part):
    base = key
    key = jax.random.fold_in(key, 11)
    first, second, third = jax.random.split(key, 3)
    row_weights = shared_parts(base)
    row_scale = jnp.exp(jax.random.uniform(second, (FRAMES, POS, 1), jnp.float32, math.log(0.3), math.log(3.0)))
    col_scale = jnp.exp(jax.random.uniform(third, (1, 1, E), jnp.float32, math.log(0.3), math.log(3.0)))
    frame = jnp.arange(FRAMES, dtype=jnp.int32)
    odd_dialog = frame // LEN % 2 == 1
    emphasis = jnp.where(odd_dialog[:, None, None], row_weights[None, None, :], 1.0)
    values = jax.random.truncated_normal(first, -4.0, 4.0, (FRAMES, POS, E), jnp.float32) * row_scale * col_scale * emphasis
    return values.astype(jnp.bfloat16)


def draw_head(key, part):
    base = key
    key = jax.random.fold_in(key, 23)
    first, second = jax.random.split(key, 2)
    row_weights = shared_parts(base)
    scale = 2.2 / math.sqrt(E)
    col_scale = jnp.exp(jax.random.uniform(second, (1, 1, CARD), jnp.float32, math.log(0.4), math.log(2.5)))
    rows = row_weights[None, :, None]
    values = jax.random.truncated_normal(first, -4.0, 4.0, (POS, E, CARD), jnp.float32) * scale * col_scale * rows
    return values.astype(jnp.bfloat16)


def draw_lengths(key, part):
    key = jax.random.fold_in(key, 37)
    order = jnp.arange(DIALOGS, dtype=jnp.int32)
    rising = LEN // 4 + order * (LEN - LEN // 4) // (DIALOGS - 1)
    jitter = jax.random.randint(key, (DIALOGS,), 0, LEN // 16 + 1)
    values = jnp.maximum(rising - jitter, LEN // 4)
    values = jnp.where(order == 0, LEN // 4, values)
    values = jnp.where(order == DIALOGS - 1, LEN, values)
    return values.astype(jnp.int32)


def plant(values, own_key, smallest, top_value):
    shape = values.shape
    spot = [jax.random.randint(jax.random.fold_in(own_key, axis), (), 0, shape[axis]) for axis in range(len(shape))]
    values = values.at[tuple(spot)].set(smallest)
    longest = shape.index(max(shape))
    spot[longest] = (spot[longest] + 1) % shape[longest]
    return values.at[tuple(spot)].set(top_value)


def setup_inputs(seed: int = 0) -> dict:
    key_of = jax.random.split(jax.random.key(seed), 6)
    hidden = draw_hidden(jax.random.fold_in(key_of[5], 71), 0)
    head = draw_head(jax.random.fold_in(key_of[5], 71), 0)
    gain = jnp.clip(1.0 + 0.1 * jax.random.normal(key_of[2], (POS, E), jnp.float32), 0.5, 1.5).astype(jnp.bfloat16)
    targets = plant(jax.random.randint(key_of[3], (FRAMES, POS), 0, CARD), jax.random.fold_in(key_of[3], 1), 0, CARD - 1).astype(jnp.int32)
    lengths = draw_lengths(jax.random.fold_in(key_of[5], 71), 0)
    return dict(hidden=hidden, head=head, gain=gain, targets=targets, lengths=lengths)


EPS = 1e-05

def reference(hidden, head, gain, targets, lengths):
    frames_all = hidden.reshape(DIALOGS, LEN, POS, E)
    labels_all = targets.reshape(DIALOGS, LEN, POS)
    head_wide = head.astype(jnp.float32)
    gain_wide = gain.astype(jnp.float32)
    classes = jnp.arange(CARD, dtype=jnp.int32)
    slots = jnp.arange(LEN, dtype=jnp.int32)

    def step(carry, inputs):
        grad_sum, loss_sum = carry
        rows, labels, length = inputs
        widened = rows.astype(jnp.float32)
        inverse = lax.rsqrt(lax.optimization_barrier(jnp.mean(widened * widened, axis=-1, keepdims=True)) + EPS)
        normed = (widened * inverse * gain_wide[None, :, :]).astype(jnp.bfloat16)
        normed_wide = lax.optimization_barrier(normed).astype(jnp.float32)
        logits = jnp.einsum('fke,kec->fkc', normed_wide, head_wide)
        top = lax.optimization_barrier(jnp.max(logits, axis=-1, keepdims=True))
        shifted = logits - top
        total = lax.optimization_barrier(jnp.sum(jnp.exp(shifted), axis=-1, keepdims=True))
        log_total = top + jnp.log(total)
        onehot = (labels[:, :, None] == classes[None, None, :]).astype(jnp.float32)
        picked = lax.optimization_barrier(jnp.sum(logits * onehot, axis=-1))
        valid = (slots < length).astype(jnp.float32)
        local = jnp.sum(valid[:, None] * (log_total[:, :, 0] - picked))
        probs = jnp.exp(shifted) / total
        slopes = (valid[:, None, None] * (probs - onehot)).astype(jnp.bfloat16)
        slopes_wide = lax.optimization_barrier(slopes).astype(jnp.float32)
        back = jnp.einsum('fkc,kec->fke', slopes_wide, head_wide)
        weighted = back * gain_wide[None, :, :]
        grad_rows = (inverse * weighted - widened * inverse ** 3 * lax.optimization_barrier(jnp.mean(weighted * widened, axis=-1, keepdims=True))).astype(jnp.bfloat16)
        partial_sum = jnp.einsum('fke,fkc->kec', normed_wide, slopes_wide).astype(jnp.bfloat16)
        partial_sum = lax.optimization_barrier(partial_sum).astype(jnp.float32)
        return ((grad_sum + partial_sum, loss_sum + local), grad_rows)
    init = (jnp.zeros((POS, E, CARD), jnp.float32), jnp.zeros((), jnp.float32))
    (grad_head, loss_sum), grads = lax.scan(step, init, (frames_all, labels_all, lengths))
    loss = loss_sum / (jnp.sum(lengths).astype(jnp.float32) * POS)
    return (loss, grads.reshape(FRAMES, POS, E), grad_head)
```

```python
import jax
import jax.numpy as jnp
from jax import lax
from jax.experimental import pallas as pl
from jax.experimental.pallas import tpu as pltpu
from jax.sharding import PartitionSpec as P

EPS = 1e-05
WIDE = jnp.float32
HALF = jnp.bfloat16
VMEM = pl.BlockSpec(memory_space=pltpu.VMEM)
SMEM = pl.BlockSpec(memory_space=pltpu.SMEM)
ANY = pl.BlockSpec(memory_space=pl.ANY)
PACK_ROWS = 256


def params(mib):
    return pltpu.CompilerParams(vmem_limit_bytes=mib * 1024 * 1024)


def cost(flops, moved):
    return pl.CostEstimate(flops=flops, bytes_accessed=moved, transcendentals=0)


def unpack(hidden):
    frames, positions, width = hidden.shape
    chunk = PACK_ROWS // positions
    rows = chunk * positions

    def body(hidden_ref, out_ref):
        r = lax.broadcasted_iota(jnp.int32, (rows, rows), 0)
        c = lax.broadcasted_iota(jnp.int32, (rows, rows), 1)
        pick = (lax.rem(r, chunk) == lax.div(c, positions)) & (lax.rem(c, positions) == lax.div(r, chunk))
        flat = hidden_ref[...].reshape(rows, width)
        moved = jnp.dot(pick.astype(HALF), flat, preferred_element_type=WIDE).astype(HALF)
        out_ref[...] = moved.reshape(positions, chunk, width)

    out = pl.pallas_call(
        body,
        grid=(frames // chunk,),
        in_specs=[pl.BlockSpec((chunk, positions, width), lambda i: (i, 0, 0))],
        out_specs=pl.BlockSpec((positions, chunk, width), lambda i: (0, i, 0)),
        out_shape=jax.ShapeDtypeStruct((positions, frames, width), HALF),
        cost_estimate=cost(2 * frames * rows * positions * width, 4 * hidden.size),
        compiler_params=params(24),
        name="unpack",
    )(hidden)
    return out.reshape(positions * frames, width)


def pack(flat, positions):
    width = flat.shape[1]
    frames = flat.shape[0] // positions
    chunk = PACK_ROWS // positions
    rows = chunk * positions

    def body(flat_ref, out_ref):
        r = lax.broadcasted_iota(jnp.int32, (rows, rows), 0)
        c = lax.broadcasted_iota(jnp.int32, (rows, rows), 1)
        pick = (lax.rem(c, chunk) == lax.div(r, positions)) & (lax.rem(r, positions) == lax.div(c, chunk))
        block = flat_ref[...].reshape(rows, width)
        moved = jnp.dot(pick.astype(HALF), block, preferred_element_type=WIDE).astype(HALF)
        out_ref[...] = moved.reshape(chunk, positions, width)

    return pl.pallas_call(
        body,
        grid=(frames // chunk,),
        in_specs=[pl.BlockSpec((positions, chunk, width), lambda i: (0, i, 0))],
        out_specs=pl.BlockSpec((chunk, positions, width), lambda i: (i, 0, 0)),
        out_shape=jax.ShapeDtypeStruct((frames, positions, width), HALF),
        cost_estimate=cost(2 * frames * rows * positions * width, 4 * flat.size),
        compiler_params=params(24),
        name="pack",
    )(flat.reshape(positions, frames, width))


def forward(lengths, labels, gains, stream, pieces, blocks):
    frames, width = stream.shape
    height = frames // blocks
    depth, classes = pieces[0].shape
    n_dp = len(pieces)

    def body(*refs):
        length_ref, label_ref, gain_ref, stream_ref = refs[:4]
        piece_refs = refs[4 : 4 + n_dp]
        loss_ref, gain_out, weight_ref, slope_ref = refs[4 + n_dp : 8 + n_dp]
        part_refs = refs[8 + n_dp : 8 + 2 * n_dp]
        rows_ref, normed_ref, partial_ref, sems = refs[8 + 2 * n_dp :]

        dp = lax.axis_index("dp")

        def span(i):
            return pl.ds(pl.multiple_of((dp ^ i) * depth, depth), depth)

        copies = [
            pltpu.make_async_copy(
                stream_ref.at[pl.ds(j * height, height)], rows_ref.at[pl.ds(j * height, height)], sems.at[j]
            )
            for j in range(blocks)
        ]
        copies += [
            pltpu.make_async_copy(piece_refs[i], weight_ref.at[span(i)], sems.at[blocks + i]) for i in range(n_dp)
        ]
        for copy in copies:
            copy.start()
        gain = jnp.concatenate([gain_ref[i : i + 1, :].astype(WIDE) for i in range(n_dp)], axis=1)
        gain_out[...] = gain
        length = length_ref[dp]
        count = length_ref[0]
        for d in range(1, n_dp):
            count = count + length_ref[d]

        for j in range(blocks):
            copies[j].wait()
            values = rows_ref[j * height : (j + 1) * height, :].astype(WIDE)
            inverse = lax.rsqrt(jnp.mean(values * values, axis=1, keepdims=True) + EPS)
            normed_ref[j * height : (j + 1) * height, :] = (values * inverse * gain).astype(HALF)
        for copy in copies[blocks:]:
            copy.wait()
        weights = weight_ref[...]
        loss = jnp.zeros((1, 1), WIDE)
        for j in range(blocks):
            logits = jnp.dot(
                normed_ref[j * height : (j + 1) * height, :], weights, preferred_element_type=WIDE
            )
            label_row = label_ref[:, j * height : (j + 1) * height]
            label = jnp.broadcast_to(label_row, (8, height)).T[:, :1]
            slot = j * height + lax.broadcasted_iota(jnp.int32, (height, 1), 0)
            valid = jnp.where(slot < length, 1.0, 0.0).astype(WIDE)
            top = jnp.max(logits, axis=1, keepdims=True)
            shifted = logits - top
            powers = jnp.exp(shifted)
            total = jnp.sum(powers, axis=1, keepdims=True)
            hit = lax.broadcasted_iota(jnp.int32, (height, classes), 1) == label
            picked = jnp.sum(jnp.where(hit, shifted, 0.0), axis=1, keepdims=True)
            loss = loss + jnp.sum(valid * (jnp.log(total) - picked), axis=0, keepdims=True)
            probs = powers * (1.0 / total)
            slope_ref[j * height : (j + 1) * height, :] = (valid * jnp.where(hit, probs - 1.0, probs)).astype(HALF)
        loss_ref[...] = jnp.broadcast_to(loss / (count.astype(WIDE) * blocks), loss_ref.shape)
        step = min(256, width)
        for at in range(0, width, step):
            partial_ref[at : at + step, :] = lax.dot_general(
                normed_ref[:, at : at + step],
                slope_ref[...],
                (((0,), (0,)), ((), ())),
                preferred_element_type=WIDE,
            ).astype(HALF)
        for i in range(n_dp):
            part_refs[i][...] = partial_ref[span(i), :]

    out = pl.pallas_call(
        body,
        in_specs=[SMEM] + [VMEM] * 2 + [ANY] * (1 + n_dp),
        out_specs=[VMEM] * (4 + n_dp),
        out_shape=[
            jax.ShapeDtypeStruct((8, 128), WIDE),
            jax.ShapeDtypeStruct((1, width), WIDE),
            jax.ShapeDtypeStruct((width, classes), HALF),
            jax.ShapeDtypeStruct((frames, classes), HALF),
        ]
        + [jax.ShapeDtypeStruct((depth, classes), HALF)] * n_dp,
        scratch_shapes=[
            pltpu.VMEM((frames, width), HALF),
            pltpu.VMEM((frames, width), HALF),
            pltpu.VMEM((width, classes), HALF),
            pltpu.SemaphoreType.DMA((blocks + n_dp,)),
        ],
        cost_estimate=cost(4 * frames * width * classes, 6 * width * classes),
        compiler_params=params(28),
        name="forward",
    )(lengths, labels, gains, stream, *pieces)
    return (*out[:4], out[4:])


def backward(gain, weights, stream, slopes, blocks):
    frames, width = stream.shape
    classes = weights.shape[1]
    height = frames // blocks

    def body(gain_ref, weight_ref, stream_ref, slope_ref, out_ref):
        for j in range(blocks):
            rows = slice(j * height, (j + 1) * height)
            values = stream_ref[rows, :].astype(WIDE)
            inverse = lax.rsqrt(jnp.mean(values * values, axis=1, keepdims=True) + EPS)
            back = lax.dot_general(
                slope_ref[rows, :],
                weight_ref[...],
                (((1,), (1,)), ((), ())),
                preferred_element_type=WIDE,
            )
            weighted = back * gain_ref[...]
            scale = inverse * inverse * inverse * jnp.mean(weighted * values, axis=1, keepdims=True)
            out_ref[rows, :] = (inverse * weighted - values * scale).astype(HALF)

    return pl.pallas_call(
        body,
        in_specs=[VMEM] * 4,
        out_specs=VMEM,
        out_shape=jax.ShapeDtypeStruct((frames, width), HALF),
        cost_estimate=cost(2 * frames * width * classes, 6 * frames * width),
        compiler_params=params(24),
        name="backward",
    )(gain, weights, stream, slopes)


def per_device(n_dp, n_fsdp, hidden, head, gain, targets, lengths):
    inner = 2 if n_dp % 2 == 0 else 1
    line = n_dp // inner
    blocks = min(n_fsdp, 4)

    def swap(value, offset):
        return lax.ppermute(value, "dp", [(i, i ^ offset) for i in range(n_dp)])

    def wide(*values):
        total = values[0].astype(WIDE)
        for value in values[1:]:
            total = total + value.astype(WIDE)
        return total

    pieces = [None] * n_dp
    pieces[0] = head[0]
    for j in range(line - 1, 0, -1):
        pieces[j * inner] = swap(head[0], j * inner)
    if inner == 2:
        for j in range(line):
            pieces[j * inner + 1] = swap(pieces[j * inner], 1)

    stream = lax.all_to_all(unpack(hidden), "fsdp", split_axis=0, concat_axis=0, tiled=True)
    gains = lax.all_to_all(
        jnp.broadcast_to(gain, (n_dp, gain.shape[1])), "dp", split_axis=0, concat_axis=0, tiled=True
    )

    loss, gain_row, weights, slopes, parts = forward(lengths, targets.T, gains, stream, pieces, blocks)

    sums = [None] * line
    for j in range(line - 1, -1, -1):
        terms = [parts[j * inner]]
        if inner == 2:
            terms.append(swap(parts[j * inner + 1], 1))
        sums[j] = terms if j == 0 else [swap(wide(*terms).astype(HALF), j * inner)]
    grad_head = wide(*[term for terms in sums for term in terms])

    grads = backward(gain_row, weights, stream, slopes, blocks)
    grads = lax.all_to_all(grads, "fsdp", split_axis=0, concat_axis=0, tiled=True)
    grad_hidden = pack(grads, n_fsdp)

    n = n_dp * n_fsdp
    losses = lax.all_to_all(
        jnp.broadcast_to(loss[:1], (n, 128)), ("dp", "fsdp"), split_axis=0, concat_axis=0, tiled=True
    )
    return jnp.sum(losses[:, 0]), grad_hidden, grad_head[None]


def solution(mesh):
    n_dp, n_fsdp = mesh.shape["dp"], mesh.shape["fsdp"]
    placed = (
        P(("dp", "fsdp"), None, None),
        P("fsdp", "dp", None),
        P("fsdp", "dp"),
        P("dp", "fsdp"),
        P(),
    )
    return jax.shard_map(
        lambda *args: per_device(n_dp, n_fsdp, *args),
        mesh=mesh,
        in_specs=placed,
        out_specs=(P(), P(("dp", "fsdp"), None, None), P("fsdp", "dp", None)),
        check_vma=False,
    )
```

```python
import jax
import jax.numpy as jnp
from jax import lax
from jax.experimental import pallas as pl
from jax.experimental.pallas import tpu as pltpu
from jax.sharding import PartitionSpec as P

EPS = 1e-05
WIDE = jnp.float32
HALF = jnp.bfloat16
VMEM = pl.BlockSpec(memory_space=pltpu.VMEM)
SMEM = pl.BlockSpec(memory_space=pltpu.SMEM)
ANY = pl.BlockSpec(memory_space=pl.ANY)
PACK_ROWS = 256
EXTRA = 8
UNPACK, PACK, NEAR, FAR, BACK_FAR, BACK_NEAR, FOLD, HOLD = 0.01, 0.01, 10, 0.01, 0.01, 0.01, 0.01, 0.01


def params(mib):
    return pltpu.CompilerParams(vmem_limit_bytes=mib * 1024 * 1024)


def cost(gigaflops):
    return pl.CostEstimate(flops=int(gigaflops * 1e9), bytes_accessed=0, transcendentals=0)


def unpack(hidden):
    frames, positions, width = hidden.shape
    chunk = PACK_ROWS // positions
    rows = chunk * positions
    steps = frames // chunk

    def body(hidden_ref, *refs):
        outs, (stage, sems) = refs[:-2], refs[-2:]
        copies = [
            pltpu.make_async_copy(
                hidden_ref.at[pl.ds(i * chunk, chunk)], stage.at[pl.ds(i * chunk, chunk)], sems.at[i]
            )
            for i in range(steps)
        ]
        for copy in copies:
            copy.start()
        me = lax.axis_index("fsdp")
        r = lax.broadcasted_iota(jnp.int32, (rows, rows), 0)
        c = lax.broadcasted_iota(jnp.int32, (rows, rows), 1)
        pick = (lax.rem(r, chunk) == lax.div(c, positions)) & (
            lax.rem(c, positions) == (lax.div(r, chunk) ^ me)
        )
        pick = pick.astype(HALF)
        for i in range(steps):
            copies[i].wait()
            here = slice(i * chunk, (i + 1) * chunk)
            flat = stage[here].reshape(rows, width)
            moved = jnp.dot(pick, flat, preferred_element_type=WIDE).astype(HALF)
            for j in range(positions):
                part = moved[j * chunk : (j + 1) * chunk]
                if j < 2:
                    outs[j][here, :] = part
                else:
                    outs[j // 2 + 1][j % 2, here, :] = part

    return pl.pallas_call(
        body,
        in_specs=[ANY],
        out_specs=[VMEM] * (positions // 2 + 1),
        out_shape=[jax.ShapeDtypeStruct((frames, width), HALF)] * 2
        + [jax.ShapeDtypeStruct((2, frames, width), HALF)] * (positions // 2 - 1),
        scratch_shapes=[pltpu.VMEM(hidden.shape, HALF), pltpu.SemaphoreType.DMA((steps,))],
        cost_estimate=cost(UNPACK),
        compiler_params=params(58),
        name="unpack",
    )(hidden)


def pack(own, side, pairs, relayed):
    frames, width = own.shape
    positions = 2 + 2 * len(pairs)
    chunk = PACK_ROWS // positions
    rows = chunk * positions
    n = len(pairs)

    def body(own_ref, side_ref, *refs):
        me = lax.axis_index("fsdp")
        r = lax.broadcasted_iota(jnp.int32, (rows, rows), 0)
        c = lax.broadcasted_iota(jnp.int32, (rows, rows), 1)
        pick = (lax.rem(c, chunk) == lax.div(r, positions)) & (
            lax.rem(r, positions) == (lax.div(c, chunk) ^ me)
        )
        parts = [own_ref[...], side_ref[...]]
        for i in range(n):
            parts += [refs[i][0], refs[n + i][...]]
        flat = jnp.concatenate(parts, axis=0)
        moved = jnp.dot(pick.astype(HALF), flat, preferred_element_type=WIDE).astype(HALF)
        refs[-1][...] = moved.reshape(chunk, positions, width)

    flat_spec = pl.BlockSpec((chunk, width), lambda i: (i, 0))
    return pl.pallas_call(
        body,
        grid=(frames // chunk,),
        in_specs=[flat_spec] * 2 + [pl.BlockSpec((1, chunk, width), lambda i: (0, i, 0))] * n + [flat_spec] * n,
        out_specs=pl.BlockSpec((chunk, positions, width), lambda i: (i, 0, 0)),
        out_shape=jax.ShapeDtypeStruct((frames, positions, width), HALF),
        cost_estimate=cost(PACK),
        compiler_params=params(24),
        name="pack",
    )(own, side, *pairs, *relayed)


def take(pair, after=()):
    def body(*refs):
        refs[-1][...] = refs[0][1]

    return pl.pallas_call(
        body,
        in_specs=[VMEM] + [ANY] * len(after),
        out_specs=VMEM,
        out_shape=jax.ShapeDtypeStruct(pair.shape[1:], pair.dtype),
        cost_estimate=cost(HOLD),
        compiler_params=params(8),
        name="take",
    )(pair, *after)


def split_rows(value, classes):
    high = value.astype(HALF).astype(WIDE)
    middle = (value - high).astype(HALF).astype(WIDE)
    low = value - high - middle
    row = lax.broadcasted_iota(jnp.int32, (EXTRA, classes), 0)
    terms = jnp.where(row == 0, high, jnp.where(row == 1, middle, jnp.where(row == 2, low, 0.0)))
    return terms.astype(HALF)


def softmax_rows(normed, weights, label_ref, block, length):
    height, classes = normed.shape[0], weights.shape[1]
    logits = jnp.dot(normed, weights, preferred_element_type=WIDE)
    if label_ref.shape[0] == 1:
        label_row = label_ref[:, pl.ds(pl.multiple_of(block * height, height), height)]
    else:
        label_row = label_ref[pl.ds(block, 1), :]
    label = jnp.broadcast_to(label_row, (8, height)).T[:, :1]
    slot = block * height + lax.broadcasted_iota(jnp.int32, (height, 1), 0)
    valid = jnp.where(slot < length, 1.0, 0.0).astype(WIDE)
    top = jnp.max(logits, axis=1, keepdims=True)
    shifted = logits - top
    powers = jnp.exp(shifted)
    total = jnp.sum(powers, axis=1, keepdims=True)
    hit = lax.broadcasted_iota(jnp.int32, (height, classes), 1) == label
    picked = jnp.sum(jnp.where(hit, shifted, 0.0), axis=1, keepdims=True)
    loss = jnp.sum(valid * (jnp.log(total) - picked), axis=0, keepdims=True)
    probs = powers * (1.0 / total)
    return (valid * jnp.where(hit, probs - 1.0, probs)).astype(HALF), loss


def norm_rows(values, gain):
    values = values.astype(WIDE)
    inverse = lax.rsqrt(jnp.mean(values * values, axis=1, keepdims=True) + EPS)
    return (values * inverse * gain).astype(HALF)


def forward_near(lengths, labels, gains, rows, pieces):
    height, width = rows[0].shape
    depth, classes = pieces[0].shape
    n_dp, n_gain, n = len(pieces), len(gains), len(rows)

    def body(*refs):
        length_ref, label_ref = refs[:2]
        gain_refs, refs = refs[2 : 2 + n_gain], refs[2 + n_gain :]
        row_refs, refs = refs[:n], refs[n:]
        piece_refs, refs = refs[:n_dp], refs[n_dp:]
        loss_ref, gain_out, weight_ref, normed_ref, slope_ref, sems = refs
        me, dp = lax.axis_index("fsdp"), lax.axis_index("dp")

        def span(i):
            return pl.ds(pl.multiple_of((dp ^ i) * depth, depth), depth)

        copies = [pltpu.make_async_copy(piece_refs[i], weight_ref.at[span(i)], sems.at[i]) for i in range(n_dp)]
        for copy in copies:
            copy.start()
        if gains[0].shape[1] == width:
            gain_out[...] = gain_refs[0][...].astype(WIDE)
        else:
            lines = jnp.concatenate([ref[...].astype(WIDE) for ref in gain_refs], axis=0)
            for i in range(n_dp):
                gain_out[:, span(i)] = lines[i : i + 1]
        gain = gain_out[...]
        for j in range(n):
            normed_ref[j] = norm_rows(row_refs[j][...], gain)
        for copy in copies:
            copy.wait()
        weights = weight_ref[...]
        loss = jnp.zeros((1, 1), WIDE)
        for j in range(n):
            slopes, part = softmax_rows(normed_ref[j], weights, label_ref, me ^ j, length_ref[dp])
            slope_ref[j] = slopes
            loss = loss + part
        loss_ref[...] = jnp.broadcast_to(loss, loss_ref.shape)

    return pl.pallas_call(
        body,
        in_specs=[SMEM] + [VMEM] * (1 + n_gain + n) + [ANY] * n_dp,
        out_specs=[VMEM] * 5,
        out_shape=[
            jax.ShapeDtypeStruct((8, 128), WIDE),
            jax.ShapeDtypeStruct((1, width), WIDE),
            jax.ShapeDtypeStruct((width, classes), HALF),
            jax.ShapeDtypeStruct((n, height, width), HALF),
            jax.ShapeDtypeStruct((n, height, classes), HALF),
        ],
        scratch_shapes=[pltpu.SemaphoreType.DMA((n_dp,))],
        cost_estimate=cost(NEAR),
        compiler_params=params(20),
        name="forward_near",
    )(lengths, labels, *gains, *rows, *pieces)


def forward_far(lengths, labels, gain, weights, pairs, relayed, normed, slopes, loss, n_dp):
    n = len(pairs)
    n_near, height, width = normed.shape
    classes = weights.shape[1]
    depth = width // n_dp
    blocks = n_near + 2 * n

    def body(*refs):
        length_ref, label_ref, gain_ref, weight_ref = refs[:4]
        pair_refs, side_refs, refs = refs[4 : 4 + n], refs[4 + n : 4 + 2 * n], refs[4 + 2 * n :]
        near_normed, near_slopes, near_loss, loss_ref, slope_ref = refs[:5]
        part_refs, (normed_ref, slopes_ref, partial_ref) = refs[5:-3], refs[-3:]
        me, dp = lax.axis_index("fsdp"), lax.axis_index("dp")
        gain, weights = gain_ref[...], weight_ref[...]
        count = length_ref[0]
        for d in range(1, n_dp):
            count = count + length_ref[d]
        for j in range(n_near):
            normed_ref[j * height : (j + 1) * height, :] = near_normed[j]
            slopes_ref[j * height : (j + 1) * height, :] = near_slopes[j]
        loss = near_loss[:1, :1]
        for j in range(2 * n):
            at = slice((n_near + j) * height, (n_near + j + 1) * height)
            normed_ref[at, :] = norm_rows(side_refs[j // 2][...] if j % 2 else pair_refs[j // 2][0], gain)
        for j in range(2 * n):
            at = slice((n_near + j) * height, (n_near + j + 1) * height)
            new, part = softmax_rows(normed_ref[at, :], weights, label_ref, me ^ (n_near + j), length_ref[dp])
            slope_ref[j] = new
            slopes_ref[at, :] = new
            loss = loss + part
        loss = jnp.broadcast_to(loss / (count.astype(WIDE) * blocks), (1, classes))
        loss_ref[...] = jnp.broadcast_to(loss, loss_ref.shape)
        step = min(256, width)
        for at in range(0, width, step):
            partial_ref[at : at + step, :] = lax.dot_general(
                normed_ref[:, at : at + step],
                slopes_ref[...],
                (((0,), (0,)), ((), ())),
                preferred_element_type=WIDE,
            ).astype(HALF)
        for i in range(n_dp):
            start = pl.multiple_of((dp ^ i) * depth, depth)
            part_refs[i][:depth, :] = partial_ref[pl.ds(start, depth), :]
        part_refs[n_dp - 1][depth:, :] = split_rows(loss, classes)

    out = pl.pallas_call(
        body,
        in_specs=[SMEM] + [VMEM] * (6 + 2 * n),
        out_specs=[VMEM] * (2 + n_dp),
        out_shape=[
            jax.ShapeDtypeStruct((8, classes), WIDE),
            jax.ShapeDtypeStruct((2 * n, height, classes), HALF),
        ]
        + [jax.ShapeDtypeStruct((depth, classes), HALF)] * (n_dp - 1)
        + [jax.ShapeDtypeStruct((depth + EXTRA, classes), HALF)],
        scratch_shapes=[
            pltpu.VMEM((blocks * height, width), HALF),
            pltpu.VMEM((blocks * height, classes), HALF),
            pltpu.VMEM((width, classes), HALF),
        ],
        cost_estimate=cost(FAR),
        compiler_params=params(24),
        name="forward_far",
    )(lengths, labels, gain, weights, *pairs, *relayed, normed, slopes, loss)
    return out[0], out[1], out[2:]


def grad_rows(values, slopes, weights, gain):
    values = values.astype(WIDE)
    inverse = lax.rsqrt(jnp.mean(values * values, axis=1, keepdims=True) + EPS)
    back = lax.dot_general(slopes, weights, (((1,), (1,)), ((), ())), preferred_element_type=WIDE)
    weighted = back * gain
    scale = inverse * inverse * inverse * jnp.mean(weighted * values, axis=1, keepdims=True)
    return (inverse * weighted - values * scale).astype(HALF)


def backward_far(gain, weights, pairs, relayed, slopes):
    n = len(pairs)
    shape = pairs[0].shape

    def body(gain_ref, weight_ref, slope_ref, *refs):
        for j in range(2 * n):
            values = refs[n + j // 2][...] if j % 2 else refs[j // 2][0]
            refs[2 * n + j // 2][j % 2] = grad_rows(values, slope_ref[j], weight_ref[...], gain_ref[...])

    return pl.pallas_call(
        body,
        in_specs=[VMEM] * (3 + 2 * n),
        out_specs=[VMEM] * n,
        out_shape=[jax.ShapeDtypeStruct(shape, HALF)] * n,
        cost_estimate=cost(BACK_FAR),
        compiler_params=params(20),
        name="backward_far",
    )(gain, weights, slopes, *pairs, *relayed)


def backward_near(gain, weights, rows, slopes, after):
    n = len(rows)

    def body(gain_ref, weight_ref, slope_ref, *refs):
        for j in range(n):
            refs[n + len(after) + j][...] = grad_rows(refs[j][...], slope_ref[j], weight_ref[...], gain_ref[...])

    return pl.pallas_call(
        body,
        in_specs=[VMEM] * (3 + n) + [ANY] * len(after),
        out_specs=[VMEM] * n,
        out_shape=[jax.ShapeDtypeStruct(rows[0].shape, HALF)] * n,
        cost_estimate=cost(BACK_NEAR),
        compiler_params=params(20),
        name="backward_near",
    )(gain, weights, slopes, *rows, *after)


def fold(terms, loss=None, held=(), after=(), last=False):
    depth, classes = terms[0].shape
    n = len(terms)
    n_loss = 0 if loss is None else 1
    carries = n_loss and not last

    def body(*refs):
        ins, loss_in = refs[:n], refs[n : n + n_loss]
        outs = refs[n + n_loss + len(held) + len(after) :]
        total = ins[0][...].astype(WIDE)
        for ref in ins[1:]:
            total = total + ref[:depth, :].astype(WIDE)
        outs[0][:depth, :] = total.astype(outs[0].dtype)
        if n_loss:
            extra = ins[-1][depth:, :].astype(WIDE)
            value = loss_in[0][:1, :] + (extra[:1] + extra[1:2] + extra[2:3])
            outs[1][...] = jnp.broadcast_to(value[:, : outs[1].shape[1]], outs[1].shape)
            if carries:
                outs[0][depth:, :] = split_rows(value, classes)

    shapes = [jax.ShapeDtypeStruct((depth + (EXTRA if carries else 0), classes), WIDE if last else HALF)]
    if n_loss:
        shapes.append(jax.ShapeDtypeStruct((8, 128) if last else loss.shape, WIDE))
    out = pl.pallas_call(
        body,
        in_specs=[VMEM] * (n + n_loss) + [ANY] * (len(held) + len(after)),
        out_specs=[VMEM] * (1 + n_loss) + [ANY] * len(held),
        out_shape=shapes + [jax.ShapeDtypeStruct(h.shape, h.dtype) for h in held],
        input_output_aliases={n + n_loss + i: 1 + n_loss + i for i in range(len(held))},
        cost_estimate=cost(FOLD),
        compiler_params=params(8),
        name="fold",
    )(*terms, *([loss] if n_loss else []), *held, *after)
    return out[0], (out[1] if n_loss else None), out[1 + n_loss :]


def hold(gains, piece, after):
    rows = sum(g.shape[0] for g in gains)

    def body(*refs):
        if gains:
            refs[-2][...] = jnp.concatenate([ref[...] for ref in refs[: len(gains)]], axis=0)

    out = pl.pallas_call(
        body,
        in_specs=[VMEM] * len(gains) + [ANY] * (1 + len(after)),
        out_specs=[VMEM] * bool(gains) + [ANY],
        out_shape=[jax.ShapeDtypeStruct((rows, g.shape[1]), HALF) for g in gains[:1]]
        + [jax.ShapeDtypeStruct(piece.shape, HALF)],
        input_output_aliases={len(gains): len(gains[:1])},
        cost_estimate=cost(HOLD),
        compiler_params=params(8),
        name="hold",
    )(*gains, piece, *after)
    return out[0], out[-1]


def per_device(n_dp, n_fsdp, hidden, head, gain, targets, lengths):
    inner = 2
    line = n_dp // inner
    n_pairs = n_fsdp // 2 - 1

    def swap(value, axis, offset):
        size = n_dp if axis == "dp" else n_fsdp
        return lax.ppermute(value, axis, [(i, i ^ offset) for i in range(size)])

    small = gain.shape[1] % 128 == 0 and line == 4
    gains = [gain, swap(gain, "dp", 1)] if small else [gain]
    pieces = [None] * n_dp
    pieces[0] = head[0]
    for o in sorted(range(1, line), key=lambda o: (bin(o).count("1"), -o)):
        bit = o & -o
        if small and o == 3:
            break
        pieces[o * inner] = swap(pieces[(o ^ bit) * inner], "dp", bit * inner)
    own, side, *pairs = unpack(hidden)
    pairs = [swap(pair, "fsdp", 2 * i + 2) for i, pair in enumerate(pairs)]
    for o in range(line):
        if small and o == 1:
            gain, pieces[2] = hold(gains, pieces[2], [own, pieces[1]])
        if pieces[o * inner] is not None:
            pieces[o * inner + 1] = swap(pieces[o * inner], "dp", 1)
    if small:
        gains = [gain, swap(gain, "dp", 2)]
        gain, side = hold(gains, side, [pieces[4]])
        pieces[6] = hold([], swap(pieces[4], "dp", 2), [pieces[3], pieces[5]])[1]
        pieces[7] = swap(pieces[6], "dp", 1)
        gains = [gain, swap(gain, "dp", 4)]
    else:
        gains = [lax.all_gather(gain, "dp", axis=1, tiled=True)]
    side = swap(side, "fsdp", 1)
    relayed = [swap(take(pair), "fsdp", 1) for pair in pairs]

    height = targets.shape[0] // n_fsdp
    labels = targets.T if height % 128 == 0 else targets.reshape(n_fsdp, height)
    loss, gain_row, weights, normed, near_slopes = forward_near(lengths, labels, gains, [own, side], pieces)
    loss, far_slopes, parts = forward_far(
        lengths, labels, gain_row, weights, pairs, relayed, normed, near_slopes, loss, n_dp
    )

    far = backward_far(gain_row, weights, pairs, relayed, far_slopes)
    near = None
    across = [None] * line
    waiting = list(range(line - 1, -1, -1))
    for o in (waiting.pop(0), waiting.pop(0)):
        across[o] = swap(parts[o * inner + 1], "dp", 1)
    came = [[] for _ in range(line)]
    rides = line - 1
    order = far[-1:]
    for o in range(line - 1, 0, -1):
        held = [parts[waiting[0] * inner + 1]] if waiting else []
        if o == rides:
            piece, loss, held = fold([parts[o * inner], across[o], *came[o]], loss, held, order)
        else:
            piece, _, held = fold([parts[o * inner], *came[o], across[o]], None, held, order)
        if near is None:
            near = backward_near(gain_row, weights, [own, side], near_slopes, [loss])
        bit, order = o & -o, [piece]
        moved = swap(piece, "dp", bit * inner)
        if o == rides:
            rides = o ^ bit
            came[rides] = [*came[rides], moved]
        else:
            came[o ^ bit] = [moved, *came[o ^ bit]]
        if held:
            across[waiting.pop(0)] = swap(held[0], "dp", 1)
    grad_head, loss, _ = fold([parts[0], across[0], *came[0]], loss, last=True)

    far = [swap(pair, "fsdp", 2 * i + 2) for i, pair in enumerate(far)]
    relayed = [swap(take(pair, came[0][-1:]), "fsdp", 1) for pair in far]
    grad_hidden = pack(near[0], swap(near[1], "fsdp", 1), far, relayed)

    bit = n_fsdp // 2
    while bit:
        loss = loss + swap(loss, "fsdp", bit)
        bit //= 2
    return loss[0, 0], grad_hidden, grad_head[None]


def solution(mesh):
    n_dp, n_fsdp = mesh.shape["dp"], mesh.shape["fsdp"]
    placed = (
        P(("dp", "fsdp"), None, None),
        P("fsdp", "dp", None),
        P("fsdp", "dp"),
        P("dp", "fsdp"),
        P(),
    )
    return jax.shard_map(
        lambda *args: per_device(n_dp, n_fsdp, *args),
        mesh=mesh,
        in_specs=placed,
        out_specs=(P(), P(("dp", "fsdp"), None, None), P("fsdp", "dp", None)),
        check_vma=False,
    )
```

```python
import jax
import jax.numpy as jnp
from jax import lax
from jax.experimental import pallas as pl
from jax.experimental.pallas import tpu as pltpu
from jax.sharding import PartitionSpec as P

EPS = 1e-05
WIDE = jnp.float32
HALF = jnp.bfloat16
VMEM = pl.BlockSpec(memory_space=pltpu.VMEM)
SMEM = pl.BlockSpec(memory_space=pltpu.SMEM)
ANY = pl.BlockSpec(memory_space=pl.ANY)
PACK_ROWS = 256
EXTRA = 8
UNPACK, PACK, NEAR, FAR, BACKWARD, FOLD, HOLD, LAST, RELAY = 0.01, 0.01, 3, 0.01, 0.01, 0.01, 0.01, 3, 1.5


def params(mib):
    return pltpu.CompilerParams(vmem_limit_bytes=mib * 1024 * 1024)


def cost(gigaflops):
    return pl.CostEstimate(flops=int(gigaflops * 1e9), bytes_accessed=0, transcendentals=0)


def unpack(hidden):
    frames, positions, width = hidden.shape
    chunk = PACK_ROWS // positions
    rows = chunk * positions
    steps = frames // chunk

    def body(hidden_ref, *refs):
        outs, (stage, sems) = refs[:-2], refs[-2:]
        copies = [
            pltpu.make_async_copy(
                hidden_ref.at[pl.ds(i * chunk, chunk)], stage.at[pl.ds(i * chunk, chunk)], sems.at[i]
            )
            for i in range(steps)
        ]
        for copy in copies:
            copy.start()
        me = lax.axis_index("fsdp")
        r = lax.broadcasted_iota(jnp.int32, (rows, rows), 0)
        c = lax.broadcasted_iota(jnp.int32, (rows, rows), 1)
        pick = (lax.rem(r, chunk) == lax.div(c, positions)) & (
            lax.rem(c, positions) == (lax.div(r, chunk) ^ me)
        )
        pick = pick.astype(HALF)
        for i in range(steps):
            copies[i].wait()
            here = slice(i * chunk, (i + 1) * chunk)
            flat = stage[here].reshape(rows, width)
            moved = jnp.dot(pick, flat, preferred_element_type=WIDE).astype(HALF)
            for j in range(positions):
                part = moved[j * chunk : (j + 1) * chunk]
                outs[j][here, :] = part

    return pl.pallas_call(
        body,
        in_specs=[ANY],
        out_specs=[VMEM] * positions,
        out_shape=[jax.ShapeDtypeStruct((frames, width), HALF)] * positions,
        scratch_shapes=[pltpu.VMEM(hidden.shape, HALF), pltpu.SemaphoreType.DMA((steps,))],
        cost_estimate=cost(UNPACK),
        compiler_params=params(58),
        name="unpack",
    )(hidden)


def pack(parts):
    frames, width = parts[0].shape
    positions = len(parts)
    chunk = PACK_ROWS // positions
    rows = chunk * positions

    def body(*refs):
        me = lax.axis_index("fsdp")
        r = lax.broadcasted_iota(jnp.int32, (rows, rows), 0)
        c = lax.broadcasted_iota(jnp.int32, (rows, rows), 1)
        pick = (lax.rem(c, chunk) == lax.div(r, positions)) & (
            lax.rem(r, positions) == (lax.div(c, chunk) ^ me)
        )
        flat = jnp.concatenate([ref[...] for ref in refs[:-1]], axis=0)
        moved = jnp.dot(pick.astype(HALF), flat, preferred_element_type=WIDE).astype(HALF)
        refs[-1][...] = moved.reshape(chunk, positions, width)

    return pl.pallas_call(
        body,
        grid=(frames // chunk,),
        in_specs=[pl.BlockSpec((chunk, width), lambda i: (i, 0))] * positions,
        out_specs=pl.BlockSpec((chunk, positions, width), lambda i: (i, 0, 0)),
        out_shape=jax.ShapeDtypeStruct((frames, positions, width), HALF),
        cost_estimate=cost(PACK),
        compiler_params=params(24),
        name="pack",
    )(*parts)


def split_rows(value, classes):
    high = value.astype(HALF).astype(WIDE)
    middle = (value - high).astype(HALF).astype(WIDE)
    low = value - high - middle
    row = lax.broadcasted_iota(jnp.int32, (EXTRA, classes), 0)
    terms = jnp.where(row == 0, high, jnp.where(row == 1, middle, jnp.where(row == 2, low, 0.0)))
    return terms.astype(HALF)


def softmax_rows(normed, weights, label_ref, block, length):
    height, classes = normed.shape[0], weights.shape[1]
    logits = jnp.dot(normed, weights, preferred_element_type=WIDE)
    if label_ref.shape[0] == 1:
        label_row = label_ref[:, pl.ds(pl.multiple_of(block * height, height), height)]
    else:
        label_row = label_ref[pl.ds(block, 1), :]
    label = jnp.broadcast_to(label_row, (8, height)).T[:, :1]
    slot = block * height + lax.broadcasted_iota(jnp.int32, (height, 1), 0)
    valid = jnp.where(slot < length, 1.0, 0.0).astype(WIDE)
    top = jnp.max(logits, axis=1, keepdims=True)
    shifted = logits - top
    powers = jnp.exp(shifted)
    total = jnp.sum(powers, axis=1, keepdims=True)
    hit = lax.broadcasted_iota(jnp.int32, (height, classes), 1) == label
    picked = jnp.sum(jnp.where(hit, shifted, 0.0), axis=1, keepdims=True)
    loss = jnp.sum(valid * (jnp.log(total) - picked), axis=0, keepdims=True)
    probs = powers * (1.0 / total)
    return (valid * jnp.where(hit, probs - 1.0, probs)).astype(HALF), loss


def norm_rows(values, gain):
    values = values.astype(WIDE)
    inverse = lax.rsqrt(jnp.mean(values * values, axis=1, keepdims=True) + EPS)
    return (values * inverse * gain).astype(HALF)


def forward_near(lengths, labels, gains, rows, pieces):
    height, width = rows[0].shape
    depth, classes = pieces[0].shape
    n_dp, n_gain, n = len(pieces), len(gains), len(rows)

    def body(*refs):
        length_ref, label_ref = refs[:2]
        gain_refs, refs = refs[2 : 2 + n_gain], refs[2 + n_gain :]
        row_refs, refs = refs[:n], refs[n:]
        piece_refs, refs = refs[:n_dp], refs[n_dp:]
        loss_ref, gain_out, weight_ref, normed_ref, slope_ref, sems = refs
        me, dp = lax.axis_index("fsdp"), lax.axis_index("dp")

        def span(i):
            return pl.ds(pl.multiple_of((dp ^ i) * depth, depth), depth)

        copies = [pltpu.make_async_copy(piece_refs[i], weight_ref.at[span(i)], sems.at[i]) for i in range(n_dp)]
        for copy in copies:
            copy.start()
        if gains[0].shape[1] == width:
            gain_out[...] = gain_refs[0][...].astype(WIDE)
        else:
            lines = jnp.concatenate([ref[...].astype(WIDE) for ref in gain_refs], axis=0)
            for i in range(n_dp):
                gain_out[:, span(i)] = lines[i : i + 1]
        gain = gain_out[...]
        for j in range(n):
            normed_ref[j] = norm_rows(row_refs[j][...], gain)
        for copy in copies:
            copy.wait()
        weights = weight_ref[...]
        loss = jnp.zeros((1, 1), WIDE)
        for j in range(n):
            slopes, part = softmax_rows(normed_ref[j], weights, label_ref, me ^ j, length_ref[dp])
            slope_ref[j] = slopes
            loss = loss + part
        loss_ref[...] = jnp.broadcast_to(loss, loss_ref.shape)

    return pl.pallas_call(
        body,
        in_specs=[SMEM] + [VMEM] * (1 + n_gain + n) + [ANY] * n_dp,
        out_specs=[VMEM] * 5,
        out_shape=[
            jax.ShapeDtypeStruct((8, 128), WIDE),
            jax.ShapeDtypeStruct((1, width), WIDE),
            jax.ShapeDtypeStruct((width, classes), HALF),
            jax.ShapeDtypeStruct((n, height, width), HALF),
            jax.ShapeDtypeStruct((n, height, classes), HALF),
        ],
        scratch_shapes=[pltpu.SemaphoreType.DMA((n_dp,))],
        cost_estimate=cost(NEAR),
        compiler_params=params(20),
        name="forward_near",
    )(lengths, labels, *gains, *rows, *pieces)


def forward_far(lengths, labels, gain, weights, rows, normed, slopes, loss, n_dp):
    n = len(rows)
    n_near, height, width = normed.shape
    classes = weights.shape[1]
    depth = width // n_dp
    blocks = n_near + n

    def body(*refs):
        length_ref, label_ref, gain_ref, weight_ref = refs[:4]
        row_refs, refs = refs[4 : 4 + n], refs[4 + n :]
        near_normed, near_slopes, near_loss, loss_ref, slope_ref = refs[:5]
        part_refs, (normed_ref, slopes_ref, partial_ref) = refs[5:-3], refs[-3:]
        me, dp = lax.axis_index("fsdp"), lax.axis_index("dp")
        gain, weights = gain_ref[...], weight_ref[...]
        count = length_ref[0]
        for d in range(1, n_dp):
            count = count + length_ref[d]
        for j in range(n_near):
            normed_ref[j * height : (j + 1) * height, :] = near_normed[j]
            slopes_ref[j * height : (j + 1) * height, :] = near_slopes[j]
        loss = near_loss[:1, :1]
        for j in range(n):
            at = slice((n_near + j) * height, (n_near + j + 1) * height)
            normed_ref[at, :] = norm_rows(row_refs[j][...], gain)
        for j in range(n):
            at = slice((n_near + j) * height, (n_near + j + 1) * height)
            new, part = softmax_rows(normed_ref[at, :], weights, label_ref, me ^ (n_near + j), length_ref[dp])
            slope_ref[j] = new
            slopes_ref[at, :] = new
            loss = loss + part
        loss = jnp.broadcast_to(loss / (count.astype(WIDE) * blocks), (1, classes))
        loss_ref[...] = jnp.broadcast_to(loss, loss_ref.shape)
        step = min(256, width)
        for at in range(0, width, step):
            partial_ref[at : at + step, :] = lax.dot_general(
                normed_ref[:, at : at + step],
                slopes_ref[...],
                (((0,), (0,)), ((), ())),
                preferred_element_type=WIDE,
            ).astype(HALF)
        for i in range(n_dp):
            start = pl.multiple_of((dp ^ i) * depth, depth)
            part_refs[i][:depth, :] = partial_ref[pl.ds(start, depth), :]
        part_refs[n_dp - 1][depth:, :] = split_rows(loss, classes)

    out = pl.pallas_call(
        body,
        in_specs=[SMEM] + [VMEM] * (6 + n),
        out_specs=[VMEM] * (2 + n_dp),
        out_shape=[
            jax.ShapeDtypeStruct((8, classes), WIDE),
            jax.ShapeDtypeStruct((n, height, classes), HALF),
        ]
        + [jax.ShapeDtypeStruct((depth, classes), HALF)] * (n_dp - 1)
        + [jax.ShapeDtypeStruct((depth + EXTRA, classes), HALF)],
        scratch_shapes=[
            pltpu.VMEM((blocks * height, width), HALF),
            pltpu.VMEM((blocks * height, classes), HALF),
            pltpu.VMEM((width, classes), HALF),
        ],
        cost_estimate=cost(FAR),
        compiler_params=params(24),
        name="forward_far",
    )(lengths, labels, gain, weights, *rows, normed, slopes, loss)
    return out[0], out[1], out[2:]


def grad_rows(values, slopes, weights, gain):
    values = values.astype(WIDE)
    inverse = lax.rsqrt(jnp.mean(values * values, axis=1, keepdims=True) + EPS)
    back = lax.dot_general(slopes, weights, (((1,), (1,)), ((), ())), preferred_element_type=WIDE)
    weighted = back * gain
    scale = inverse * inverse * inverse * jnp.mean(weighted * values, axis=1, keepdims=True)
    return (inverse * weighted - values * scale).astype(HALF)


def backward(gain, weights, rows, slopes, after=()):
    n = len(rows)

    def body(gain_ref, weight_ref, slope_ref, *refs):
        for j in range(n):
            refs[n + len(after) + j][...] = grad_rows(refs[j][...], slope_ref[j], weight_ref[...], gain_ref[...])

    return pl.pallas_call(
        body,
        in_specs=[VMEM] * (3 + n) + [ANY] * len(after),
        out_specs=[VMEM] * n,
        out_shape=[jax.ShapeDtypeStruct(rows[0].shape, HALF)] * n,
        cost_estimate=cost(BACKWARD),
        compiler_params=params(20),
        name="backward",
    )(gain, weights, slopes, *rows, *after)


def fold(terms, loss=None, held=(), after=(), last=False):
    depth, classes = terms[0].shape
    n = len(terms)
    n_loss = 0 if loss is None else 1
    carries = n_loss and not last

    def body(*refs):
        ins, loss_in = refs[:n], refs[n : n + n_loss]
        outs = refs[n + n_loss + len(held) + len(after) :]
        total = ins[0][...].astype(WIDE)
        for ref in ins[1:]:
            total = total + ref[:depth, :].astype(WIDE)
        outs[0][:depth, :] = total.astype(outs[0].dtype)
        if n_loss:
            extra = ins[-1][depth:, :].astype(WIDE)
            value = loss_in[0][:1, :] + (extra[:1] + extra[1:2] + extra[2:3])
            outs[1][...] = jnp.broadcast_to(value[:, : outs[1].shape[1]], outs[1].shape)
            if carries:
                outs[0][depth:, :] = split_rows(value, classes)

    shapes = [jax.ShapeDtypeStruct((depth + (EXTRA if carries else 0), classes), WIDE if last else HALF)]
    if n_loss:
        shapes.append(jax.ShapeDtypeStruct((8, 128) if last else loss.shape, WIDE))
    out = pl.pallas_call(
        body,
        in_specs=[VMEM] * (n + n_loss) + [ANY] * (len(held) + len(after)),
        out_specs=[VMEM] * (1 + n_loss) + [ANY] * len(held),
        out_shape=shapes + [jax.ShapeDtypeStruct(h.shape, h.dtype) for h in held],
        input_output_aliases={n + n_loss + i: 1 + n_loss + i for i in range(len(held))},
        cost_estimate=cost(LAST if last else FOLD),
        compiler_params=params(8),
        name="fold",
    )(*terms, *([loss] if n_loss else []), *held, *after)
    return out[0], (out[1] if n_loss else None), out[1 + n_loss :]


def hold(gains, piece, after, claim=None):
    rows = sum(g.shape[0] for g in gains)

    def body(*refs):
        if gains:
            refs[-2][...] = jnp.concatenate([ref[...] for ref in refs[: len(gains)]], axis=0)

    out = pl.pallas_call(
        body,
        in_specs=[VMEM] * len(gains) + [ANY] * (1 + len(after)),
        out_specs=[VMEM] * bool(gains) + [ANY],
        out_shape=[jax.ShapeDtypeStruct((rows, g.shape[1]), HALF) for g in gains[:1]]
        + [jax.ShapeDtypeStruct(piece.shape, HALF)],
        input_output_aliases={len(gains): len(gains[:1])},
        cost_estimate=cost(claim or HOLD),
        compiler_params=params(8),
        name="hold",
    )(*gains, piece, *after)
    return out[0], out[-1]


def per_device(n_dp, n_fsdp, hidden, head, gain, targets, lengths):
    inner = 2
    line = n_dp // inner

    def swap(value, axis, offset):
        size = n_dp if axis == "dp" else n_fsdp
        return lax.ppermute(value, axis, [(i, i ^ offset) for i in range(size)])

    def exchange(blocks, after, claim=None):
        came = [swap(block, "fsdp", j + 2 & ~1) for j, block in reversed(list(enumerate(blocks)))][::-1]
        return [
            swap(hold([], block, [came[j - 1], *after], claim)[1], "fsdp", 1) if j % 2 else block
            for j, block in enumerate(came)
        ]

    small = gain.shape[1] % 128 == 0 and line == 4
    gains = [gain, swap(gain, "dp", 1)] if small else [gain]
    pieces = [None] * n_dp
    pieces[0] = head[0]
    for o in sorted(range(1, line), key=lambda o: (bin(o).count("1"), -o)):
        bit = o & -o
        if small and o == 3:
            break
        pieces[o * inner] = swap(pieces[(o ^ bit) * inner], "dp", bit * inner)
    own, side, *away = unpack(hidden)
    far = exchange(away, [], RELAY)
    for o in range(line):
        if small and o == 2:
            pieces[4] = hold([], pieces[4], [own])[1]
        if small and o == 1:
            gain, pieces[2] = hold(gains, pieces[2], [own, pieces[1]])
        if pieces[o * inner] is not None:
            pieces[o * inner + 1] = swap(pieces[o * inner], "dp", 1)
    if small:
        gains = [gain, swap(gain, "dp", 2)]
        gain, side = hold(gains, side, [pieces[4]])
        pieces[6] = hold([], swap(pieces[4], "dp", 2), [pieces[3], pieces[5]])[1]
        pieces[7] = swap(pieces[6], "dp", 1)
        gains = [gain, swap(gain, "dp", 4)]
    else:
        gains = [lax.all_gather(gain, "dp", axis=1, tiled=True)]
    side = swap(side, "fsdp", 1)

    height = targets.shape[0] // n_fsdp
    labels = targets.T if height % 128 == 0 else targets.reshape(n_fsdp, height)
    loss, gain_row, weights, normed, near_slopes = forward_near(lengths, labels, gains, [own, side], pieces)
    loss, far_slopes, parts = forward_far(
        lengths, labels, gain_row, weights, far, normed, near_slopes, loss, n_dp
    )

    far = backward(gain_row, weights, far, far_slopes)
    near = None
    across = [None] * line
    waiting = list(range(line - 1, -1, -1))
    for o in (waiting.pop(0), waiting.pop(0)):
        across[o] = swap(parts[o * inner + 1], "dp", 1)
    came = [[] for _ in range(line)]
    rides = line - 1
    order = far[-1:]
    for o in range(line - 1, 0, -1):
        held = [parts[waiting[0] * inner + 1]] if waiting else []
        if o == rides:
            piece, loss, held = fold([parts[o * inner], across[o], *came[o]], loss, held, order)
        else:
            piece, _, held = fold([parts[o * inner], *came[o], across[o]], None, held, order)
        if near is None:
            near = backward(gain_row, weights, [own, side], near_slopes, [loss])
        bit, order = o & -o, [piece]
        moved = swap(piece, "dp", bit * inner)
        if o == rides:
            rides = o ^ bit
            came[rides] = [*came[rides], moved]
        else:
            came[o ^ bit] = [moved, *came[o ^ bit]]
        if held:
            across[waiting.pop(0)] = swap(held[0], "dp", 1)
    grad_head, loss, _ = fold([parts[0], across[0], *came[0]], loss, last=True)

    grad_hidden = pack([near[0], swap(near[1], "fsdp", 1), *exchange(far, order)])

    bit = n_fsdp // 2
    while bit:
        loss = loss + swap(loss, "fsdp", bit)
        bit //= 2
    return loss[0, 0], grad_hidden, grad_head[None]


def solution(mesh):
    n_dp, n_fsdp = mesh.shape["dp"], mesh.shape["fsdp"]
    placed = (
        P(("dp", "fsdp"), None, None),
        P("fsdp", "dp", None),
        P("fsdp", "dp"),
        P("dp", "fsdp"),
        P(),
    )
    return jax.shard_map(
        lambda *args: per_device(n_dp, n_fsdp, *args),
        mesh=mesh,
        in_specs=placed,
        out_specs=(P(), P(("dp", "fsdp"), None, None), P("fsdp", "dp", None)),
        check_vma=False,
    )
```

```python
import jax
import jax.numpy as jnp
from jax import lax
from jax.experimental import pallas as pl
from jax.experimental.pallas import tpu as pltpu
from jax.sharding import PartitionSpec as P

EPS = 1e-05
WIDE = jnp.float32
HALF = jnp.bfloat16
VMEM = pl.BlockSpec(memory_space=pltpu.VMEM)
SMEM = pl.BlockSpec(memory_space=pltpu.SMEM)
ANY = pl.BlockSpec(memory_space=pl.ANY)
PACK_ROWS = 256
EXTRA = 8
UNPACK, PACK, NEAR, FAR, BACKWARD, FOLD, HOLD, LAST, RELAY, FINISH = 0.01, 0.01, 3, 0.01, 0.01, 0.01, 0.01, 3, 1.5, 0.01


def params(mib):
    return pltpu.CompilerParams(vmem_limit_bytes=mib * 1024 * 1024)


def cost(gigaflops):
    return pl.CostEstimate(flops=int(gigaflops * 1e9), bytes_accessed=0, transcendentals=0)


def unpack(hidden):
    frames, positions, width = hidden.shape
    chunk = PACK_ROWS // positions
    rows = chunk * positions
    steps = frames // chunk

    def body(hidden_ref, *refs):
        outs, (stage, sems) = refs[:-2], refs[-2:]
        copies = [
            pltpu.make_async_copy(
                hidden_ref.at[pl.ds(i * chunk, chunk)], stage.at[pl.ds(i * chunk, chunk)], sems.at[i]
            )
            for i in range(steps)
        ]
        for copy in copies:
            copy.start()
        me = lax.axis_index("fsdp")
        r = lax.broadcasted_iota(jnp.int32, (rows, rows), 0)
        c = lax.broadcasted_iota(jnp.int32, (rows, rows), 1)
        pick = (lax.rem(r, chunk) == lax.div(c, positions)) & (
            lax.rem(c, positions) == (lax.div(r, chunk) ^ me)
        )
        pick = pick.astype(HALF)
        for i in range(steps):
            copies[i].wait()
            here = slice(i * chunk, (i + 1) * chunk)
            flat = stage[here].reshape(rows, width)
            moved = jnp.dot(pick, flat, preferred_element_type=WIDE).astype(HALF)
            for j in range(positions):
                part = moved[j * chunk : (j + 1) * chunk]
                outs[j][here, :] = part
        outs[-1][...] = jnp.zeros_like(outs[-1])

    return pl.pallas_call(
        body,
        in_specs=[ANY],
        out_specs=[VMEM] * (positions + 1),
        out_shape=[jax.ShapeDtypeStruct((frames, width), HALF)] * positions
        + [jax.ShapeDtypeStruct((8, 128), WIDE)],
        scratch_shapes=[pltpu.VMEM(hidden.shape, HALF), pltpu.SemaphoreType.DMA((steps,))],
        cost_estimate=cost(UNPACK),
        compiler_params=params(58),
        name="unpack",
    )(hidden)


def pack(parts):
    frames, width = parts[0].shape
    positions = len(parts)
    chunk = PACK_ROWS // positions
    rows = chunk * positions

    def body(*refs):
        me = lax.axis_index("fsdp")
        r = lax.broadcasted_iota(jnp.int32, (rows, rows), 0)
        c = lax.broadcasted_iota(jnp.int32, (rows, rows), 1)
        pick = (lax.rem(c, chunk) == lax.div(r, positions)) & (
            lax.rem(r, positions) == (lax.div(c, chunk) ^ me)
        )
        flat = jnp.concatenate([ref[...] for ref in refs[:-2]], axis=0)
        moved = jnp.dot(pick.astype(HALF), flat, preferred_element_type=WIDE).astype(HALF)
        refs[-2][...] = moved.reshape(chunk, positions, width)
        refs[-1][...] = jnp.zeros_like(refs[-1])

    return pl.pallas_call(
        body,
        grid=(frames // chunk,),
        in_specs=[pl.BlockSpec((chunk, width), lambda i: (i, 0))] * positions,
        out_specs=[pl.BlockSpec((chunk, positions, width), lambda i: (i, 0, 0)), pl.BlockSpec((8, 128), lambda i: (0, 0))],
        out_shape=[jax.ShapeDtypeStruct((frames, positions, width), HALF), jax.ShapeDtypeStruct((8, 128), WIDE)],
        cost_estimate=cost(PACK),
        compiler_params=params(24),
        name="pack",
    )(*parts)


def split_rows(value, classes):
    high = value.astype(HALF).astype(WIDE)
    middle = (value - high).astype(HALF).astype(WIDE)
    low = value - high - middle
    row = lax.broadcasted_iota(jnp.int32, (EXTRA, classes), 0)
    terms = jnp.where(row == 0, high, jnp.where(row == 1, middle, jnp.where(row == 2, low, 0.0)))
    return terms.astype(HALF)


def softmax_rows(normed, weights, label_ref, block, length):
    height, classes = normed.shape[0], weights.shape[1]
    logits = jnp.dot(normed, weights, preferred_element_type=WIDE)
    if label_ref.shape[0] == 1:
        label_row = label_ref[:, pl.ds(pl.multiple_of(block * height, height), height)]
    else:
        label_row = label_ref[pl.ds(block, 1), :]
    label = jnp.broadcast_to(label_row, (8, height)).T[:, :1]
    slot = block * height + lax.broadcasted_iota(jnp.int32, (height, 1), 0)
    valid = jnp.where(slot < length, 1.0, 0.0).astype(WIDE)
    top = jnp.max(logits, axis=1, keepdims=True)
    shifted = logits - top
    powers = jnp.exp(shifted)
    total = jnp.sum(powers, axis=1, keepdims=True)
    hit = lax.broadcasted_iota(jnp.int32, (height, classes), 1) == label
    picked = jnp.sum(jnp.where(hit, shifted, 0.0), axis=1, keepdims=True)
    loss = jnp.sum(valid * (jnp.log(total) - picked), axis=0, keepdims=True)
    probs = powers * (1.0 / total)
    return (valid * jnp.where(hit, probs - 1.0, probs)).astype(HALF), loss


def norm_rows(values, gain):
    values = values.astype(WIDE)
    inverse = lax.rsqrt(jnp.mean(values * values, axis=1, keepdims=True) + EPS)
    return (values * inverse * gain).astype(HALF)


def forward_near(lengths, labels, gains, rows, pieces):
    height, width = rows[0].shape
    depth, classes = pieces[0].shape
    n_dp, n_gain, n = len(pieces), len(gains), len(rows)

    def body(*refs):
        length_ref, label_ref = refs[:2]
        gain_refs, refs = refs[2 : 2 + n_gain], refs[2 + n_gain :]
        row_refs, refs = refs[:n], refs[n:]
        piece_refs, refs = refs[:n_dp], refs[n_dp:]
        loss_ref, gain_out, weight_ref, normed_ref, slope_ref, sems = refs
        me, dp = lax.axis_index("fsdp"), lax.axis_index("dp")

        def span(i):
            return pl.ds(pl.multiple_of((dp ^ i) * depth, depth), depth)

        copies = [pltpu.make_async_copy(piece_refs[i], weight_ref.at[span(i)], sems.at[i]) for i in range(n_dp)]
        for copy in copies:
            copy.start()
        if gains[0].shape[1] == width:
            gain_out[...] = gain_refs[0][...].astype(WIDE)
        else:
            lines = jnp.concatenate([ref[...].astype(WIDE) for ref in gain_refs], axis=0)
            for i in range(n_dp):
                gain_out[:, span(i)] = lines[i : i + 1]
        gain = gain_out[...]
        for j in range(n):
            normed_ref[j] = norm_rows(row_refs[j][...], gain)
        for copy in copies:
            copy.wait()
        weights = weight_ref[...]
        loss = jnp.zeros((1, 1), WIDE)
        for j in range(n):
            slopes, part = softmax_rows(normed_ref[j], weights, label_ref, me ^ j, length_ref[dp])
            slope_ref[j] = slopes
            loss = loss + part
        loss_ref[...] = jnp.broadcast_to(loss, loss_ref.shape)

    return pl.pallas_call(
        body,
        in_specs=[SMEM] + [VMEM] * (1 + n_gain + n) + [ANY] * n_dp,
        out_specs=[VMEM] * 5,
        out_shape=[
            jax.ShapeDtypeStruct((8, 128), WIDE),
            jax.ShapeDtypeStruct((1, width), WIDE),
            jax.ShapeDtypeStruct((width, classes), HALF),
            jax.ShapeDtypeStruct((n, height, width), HALF),
            jax.ShapeDtypeStruct((n, height, classes), HALF),
        ],
        scratch_shapes=[pltpu.SemaphoreType.DMA((n_dp,))],
        cost_estimate=cost(NEAR),
        compiler_params=params(20),
        name="forward_near",
    )(lengths, labels, *gains, *rows, *pieces)


def forward_far(lengths, labels, gain, weights, rows, normed, slopes, loss, n_dp):
    n = len(rows)
    n_near, height, width = normed.shape
    classes = weights.shape[1]
    depth = width // n_dp
    blocks = n_near + n

    def body(*refs):
        length_ref, label_ref, gain_ref, weight_ref = refs[:4]
        row_refs, refs = refs[4 : 4 + n], refs[4 + n :]
        near_normed, near_slopes, near_loss, loss_ref, slope_ref = refs[:5]
        part_refs, (normed_ref, slopes_ref, partial_ref) = refs[5:-3], refs[-3:]
        me, dp = lax.axis_index("fsdp"), lax.axis_index("dp")
        gain, weights = gain_ref[...], weight_ref[...]
        count = length_ref[0]
        for d in range(1, n_dp):
            count = count + length_ref[d]
        for j in range(n_near):
            normed_ref[j * height : (j + 1) * height, :] = near_normed[j]
            slopes_ref[j * height : (j + 1) * height, :] = near_slopes[j]
        loss = near_loss[:1, :1]
        for j in range(n):
            at = slice((n_near + j) * height, (n_near + j + 1) * height)
            normed_ref[at, :] = norm_rows(row_refs[j][...], gain)
        for j in range(n):
            at = slice((n_near + j) * height, (n_near + j + 1) * height)
            new, part = softmax_rows(normed_ref[at, :], weights, label_ref, me ^ (n_near + j), length_ref[dp])
            slope_ref[j] = new
            slopes_ref[at, :] = new
            loss = loss + part
        loss = jnp.broadcast_to(loss / (count.astype(WIDE) * blocks), (1, classes))
        loss_ref[...] = jnp.broadcast_to(loss, loss_ref.shape)
        step = min(256, width)
        for at in range(0, width, step):
            partial_ref[at : at + step, :] = lax.dot_general(
                normed_ref[:, at : at + step],
                slopes_ref[...],
                (((0,), (0,)), ((), ())),
                preferred_element_type=WIDE,
            ).astype(HALF)
        for i in range(n_dp):
            start = pl.multiple_of((dp ^ i) * depth, depth)
            part_refs[i][:depth, :] = partial_ref[pl.ds(start, depth), :]
        part_refs[n_dp - 1][depth:, :] = split_rows(loss, classes)

    out = pl.pallas_call(
        body,
        in_specs=[SMEM] + [VMEM] * (6 + n),
        out_specs=[VMEM] * (2 + n_dp),
        out_shape=[
            jax.ShapeDtypeStruct((8, classes), WIDE),
            jax.ShapeDtypeStruct((n, height, classes), HALF),
        ]
        + [jax.ShapeDtypeStruct((depth, classes), HALF)] * (n_dp - 1)
        + [jax.ShapeDtypeStruct((depth + EXTRA, classes), HALF)],
        scratch_shapes=[
            pltpu.VMEM((blocks * height, width), HALF),
            pltpu.VMEM((blocks * height, classes), HALF),
            pltpu.VMEM((width, classes), HALF),
        ],
        cost_estimate=cost(FAR),
        compiler_params=params(24),
        name="forward_far",
    )(lengths, labels, gain, weights, *rows, normed, slopes, loss)
    return out[0], out[1], out[2:]


def grad_rows(values, slopes, weights, gain):
    values = values.astype(WIDE)
    inverse = lax.rsqrt(jnp.mean(values * values, axis=1, keepdims=True) + EPS)
    back = lax.dot_general(slopes, weights, (((1,), (1,)), ((), ())), preferred_element_type=WIDE)
    weighted = back * gain
    scale = inverse * inverse * inverse * jnp.mean(weighted * values, axis=1, keepdims=True)
    return (inverse * weighted - values * scale).astype(HALF)


def backward(gain, weights, rows, slopes, after=()):
    n = len(rows)

    def body(gain_ref, weight_ref, slope_ref, *refs):
        for j in range(n):
            refs[n + len(after) + j][...] = grad_rows(refs[j][...], slope_ref[j], weight_ref[...], gain_ref[...])

    return pl.pallas_call(
        body,
        in_specs=[VMEM] * (3 + n) + [ANY] * len(after),
        out_specs=[VMEM] * n,
        out_shape=[jax.ShapeDtypeStruct(rows[0].shape, HALF)] * n,
        cost_estimate=cost(BACKWARD),
        compiler_params=params(20),
        name="backward",
    )(gain, weights, slopes, *rows, *after)


def fold(terms, loss=None, held=(), after=(), last=False):
    depth, classes = terms[0].shape
    n = len(terms)
    n_loss = 0 if loss is None else 1
    carries = n_loss and not last

    def body(*refs):
        ins, loss_in = refs[:n], refs[n : n + n_loss]
        outs = refs[n + n_loss + len(held) + len(after) :]
        total = ins[0][...].astype(WIDE)
        for ref in ins[1:]:
            total = total + ref[:depth, :].astype(WIDE)
        outs[0][:depth, :] = total.astype(outs[0].dtype)
        if n_loss:
            extra = ins[-1][depth:, :].astype(WIDE)
            value = loss_in[0][:1, :] + (extra[:1] + extra[1:2] + extra[2:3])
            outs[1][...] = jnp.broadcast_to(value[:, : outs[1].shape[1]], outs[1].shape)
            if carries:
                outs[0][depth:, :] = split_rows(value, classes)

    shapes = [jax.ShapeDtypeStruct((depth + (EXTRA if carries else 0), classes), WIDE if last else HALF)]
    if n_loss:
        shapes.append(jax.ShapeDtypeStruct((8, 128) if last else loss.shape, WIDE))
    out = pl.pallas_call(
        body,
        in_specs=[VMEM] * (n + n_loss) + [ANY] * (len(held) + len(after)),
        out_specs=[VMEM] * (1 + n_loss) + [ANY] * len(held),
        out_shape=shapes + [jax.ShapeDtypeStruct(h.shape, h.dtype) for h in held],
        input_output_aliases={n + n_loss + i: 1 + n_loss + i for i in range(len(held))},
        cost_estimate=cost(LAST if last else FOLD),
        compiler_params=params(8),
        name="fold",
    )(*terms, *([loss] if n_loss else []), *held, *after)
    return out[0], (out[1] if n_loss else None), out[1 + n_loss :]


def hold(gains, piece, after, claim=None):
    rows = sum(g.shape[0] for g in gains)

    def body(*refs):
        if gains:
            refs[-2][...] = jnp.concatenate([ref[...] for ref in refs[: len(gains)]], axis=0)

    out = pl.pallas_call(
        body,
        in_specs=[VMEM] * len(gains) + [ANY] * (1 + len(after)),
        out_specs=[VMEM] * bool(gains) + [ANY],
        out_shape=[jax.ShapeDtypeStruct((rows, g.shape[1]), HALF) for g in gains[:1]]
        + [jax.ShapeDtypeStruct(piece.shape, HALF)],
        input_output_aliases={len(gains): len(gains[:1])},
        cost_estimate=cost(claim or HOLD),
        compiler_params=params(8),
        name="hold",
    )(*gains, piece, *after)
    return out[0], out[-1]


def finish(parts, after):
    def body(*refs):
        total = refs[0][...]
        for ref in refs[1 : len(parts)]:
            total = total + ref[...]
        refs[-1][...] = total[:1, :1]

    return pl.pallas_call(
        body,
        in_specs=[VMEM] * len(parts) + [ANY] * len(after),
        out_specs=VMEM,
        out_shape=jax.ShapeDtypeStruct((1, 1), WIDE),
        cost_estimate=cost(FINISH),
        compiler_params=params(4),
        name="finish",
    )(*parts, *after)


def per_device(n_dp, n_fsdp, hidden, head, gain, targets, lengths):
    inner = 2
    line = n_dp // inner

    def swap(value, axis, offset):
        size = n_dp if axis == "dp" else n_fsdp
        return lax.ppermute(value, axis, [(i, i ^ offset) for i in range(size)])

    def exchange(blocks, after, claim=None):
        came = [swap(block, "fsdp", j + 2 & ~1) for j, block in reversed(list(enumerate(blocks)))][::-1]
        return [
            swap(hold([], block, [came[j - 1], *after], claim)[1], "fsdp", 1) if j % 2 else block
            for j, block in enumerate(came)
        ]

    small = gain.shape[1] % 128 == 0 and line == 4
    gains = [gain, swap(gain, "dp", 1)] if small else [gain]
    pieces = [None] * n_dp
    pieces[0] = head[0]
    for o in sorted(range(1, line), key=lambda o: (bin(o).count("1"), -o)):
        bit = o & -o
        if small and o == 3:
            break
        pieces[o * inner] = swap(pieces[(o ^ bit) * inner], "dp", bit * inner)
    own, side, *away, unpacked = unpack(hidden)
    far = exchange(away, [], RELAY)
    for o in range(line):
        if small and o == 2:
            pieces[4] = hold([], pieces[4], [unpacked])[1]
        if small and o == 1:
            gain, pieces[2] = hold(gains, pieces[2], [pieces[1]])
        if pieces[o * inner] is not None:
            pieces[o * inner + 1] = swap(pieces[o * inner], "dp", 1)
    if small:
        gains = [gain, swap(gain, "dp", 2)]
        gain, side = hold(gains, side, [pieces[4]])
        gains = [gain, swap(gain, "dp", 4)]
        pieces[6] = hold([], swap(pieces[4], "dp", 2), [pieces[3], gains[1], pieces[5]])[1]
        pieces[7] = swap(pieces[6], "dp", 1)
    else:
        gains = [lax.all_gather(gain, "dp", axis=1, tiled=True)]
    side = swap(side, "fsdp", 1)

    height = targets.shape[0] // n_fsdp
    labels = targets.T if height % 128 == 0 else targets.reshape(n_fsdp, height)
    loss, gain_row, weights, normed, near_slopes = forward_near(lengths, labels, gains, [own, side], pieces)
    loss, far_slopes, parts = forward_far(
        lengths, labels, gain_row, weights, far, normed, near_slopes, loss, n_dp
    )

    far = backward(gain_row, weights, far, far_slopes)
    near = None
    across = [None] * line
    waiting = list(range(line - 1, -1, -1))
    for o in (waiting.pop(0), waiting.pop(0)):
        across[o] = swap(parts[o * inner + 1], "dp", 1)
    came = [[] for _ in range(line)]
    rides = line - 1
    order = far[-1:]
    for o in range(line - 1, 0, -1):
        held = [parts[waiting[0] * inner + 1]] if waiting else []
        if o == rides:
            piece, loss, held = fold([parts[o * inner], across[o], *came[o]], loss, held, order)
        else:
            piece, _, held = fold([parts[o * inner], *came[o], across[o]], None, held, order)
        if near is None:
            near = backward(gain_row, weights, [own, side], near_slopes, [loss])
        bit, order = o & -o, [piece]
        moved = swap(piece, "dp", bit * inner)
        if o == rides:
            rides = o ^ bit
            came[rides] = [*came[rides], moved]
        else:
            came[o ^ bit] = [moved, *came[o ^ bit]]
        if held:
            across[waiting.pop(0)] = swap(held[0], "dp", 1)
    grad_head, loss, _ = fold([parts[0], across[0], *came[0]], loss, last=True)

    grad_hidden, packed = pack([near[0], swap(near[1], "fsdp", 1), *exchange(far, order)])

    parts = [loss] + [swap(loss, "fsdp", j) for j in range(1, n_fsdp)]
    return finish(parts, [packed])[0, 0], grad_hidden, grad_head[None]


def solution(mesh):
    n_dp, n_fsdp = mesh.shape["dp"], mesh.shape["fsdp"]
    placed = (
        P(("dp", "fsdp"), None, None),
        P("fsdp", "dp", None),
        P("fsdp", "dp"),
        P("dp", "fsdp"),
        P(),
    )
    return jax.shard_map(
        lambda *args: per_device(n_dp, n_fsdp, *args),
        mesh=mesh,
        in_specs=placed,
        out_specs=(P(), P(("dp", "fsdp"), None, None), P("fsdp", "dp", None)),
        check_vma=False,
    )
```

```python
import jax
import jax.numpy as jnp
from jax import lax
from jax.experimental import pallas as pl
from jax.experimental.pallas import tpu as pltpu
from jax.sharding import PartitionSpec as P

EPS = 1e-05
WIDE = jnp.float32
HALF = jnp.bfloat16
VMEM = pl.BlockSpec(memory_space=pltpu.VMEM)
SMEM = pl.BlockSpec(memory_space=pltpu.SMEM)
ANY = pl.BlockSpec(memory_space=pl.ANY)
PACK_ROWS = 256
EXTRA = 8
UNPACK, PACK, NEAR, FAR, BACKWARD, FOLD, HOLD, LAST, RELAY, FINISH, RIDE = 0.01, 0.01, 3, 0.01, 0.01, 0.01, 0.01, 3, 1.5, 0.01, 0.01


def params(mib):
    return pltpu.CompilerParams(vmem_limit_bytes=mib * 1024 * 1024)


def cost(gigaflops):
    return pl.CostEstimate(flops=int(gigaflops * 1e9), bytes_accessed=0, transcendentals=0)


def unpack(hidden):
    frames, positions, width = hidden.shape
    chunk = PACK_ROWS // positions
    rows = chunk * positions
    steps = frames // chunk

    def body(hidden_ref, *refs):
        outs, (stage, sems) = refs[:-2], refs[-2:]
        copies = [
            pltpu.make_async_copy(
                hidden_ref.at[pl.ds(i * chunk, chunk)], stage.at[pl.ds(i * chunk, chunk)], sems.at[i]
            )
            for i in range(steps)
        ]
        for copy in copies:
            copy.start()
        me = lax.axis_index("fsdp")
        r = lax.broadcasted_iota(jnp.int32, (rows, rows), 0)
        c = lax.broadcasted_iota(jnp.int32, (rows, rows), 1)
        pick = (lax.rem(r, chunk) == lax.div(c, positions)) & (
            lax.rem(c, positions) == (lax.div(r, chunk) ^ me)
        )
        pick = pick.astype(HALF)
        for i in range(steps):
            copies[i].wait()
            here = slice(i * chunk, (i + 1) * chunk)
            flat = stage[here].reshape(rows, width)
            moved = jnp.dot(pick, flat, preferred_element_type=WIDE).astype(HALF)
            for j in range(positions):
                part = moved[j * chunk : (j + 1) * chunk]
                outs[j][here, :] = part
        outs[-1][...] = jnp.zeros_like(outs[-1])

    return pl.pallas_call(
        body,
        in_specs=[ANY],
        out_specs=[VMEM] * (positions + 1),
        out_shape=[jax.ShapeDtypeStruct((frames, width), HALF)] * positions
        + [jax.ShapeDtypeStruct((8, 128), WIDE)],
        scratch_shapes=[pltpu.VMEM(hidden.shape, HALF), pltpu.SemaphoreType.DMA((steps,))],
        cost_estimate=cost(UNPACK),
        compiler_params=params(58),
        name="unpack",
    )(hidden)


def pack(parts):
    frames, width = parts[0].shape
    positions = len(parts)
    chunk = PACK_ROWS // positions
    rows = chunk * positions

    def body(*refs):
        me = lax.axis_index("fsdp")
        r = lax.broadcasted_iota(jnp.int32, (rows, rows), 0)
        c = lax.broadcasted_iota(jnp.int32, (rows, rows), 1)
        pick = (lax.rem(c, chunk) == lax.div(r, positions)) & (
            lax.rem(r, positions) == (lax.div(c, chunk) ^ me)
        )
        flat = jnp.concatenate([ref[...] for ref in refs[:-2]], axis=0)
        moved = jnp.dot(pick.astype(HALF), flat, preferred_element_type=WIDE).astype(HALF)
        refs[-2][...] = moved.reshape(chunk, positions, width)
        refs[-1][...] = jnp.zeros_like(refs[-1])

    return pl.pallas_call(
        body,
        grid=(frames // chunk,),
        in_specs=[pl.BlockSpec((chunk, width), lambda i: (i, 0))] * positions,
        out_specs=[pl.BlockSpec((chunk, positions, width), lambda i: (i, 0, 0)), pl.BlockSpec((8, 128), lambda i: (0, 0))],
        out_shape=[jax.ShapeDtypeStruct((frames, positions, width), HALF), jax.ShapeDtypeStruct((8, 128), WIDE)],
        cost_estimate=cost(PACK),
        compiler_params=params(24),
        name="pack",
    )(*parts)


def split_rows(value, classes):
    high = value.astype(HALF).astype(WIDE)
    middle = (value - high).astype(HALF).astype(WIDE)
    low = value - high - middle
    row = lax.broadcasted_iota(jnp.int32, (EXTRA, classes), 0)
    terms = jnp.where(row == 0, high, jnp.where(row == 1, middle, jnp.where(row == 2, low, 0.0)))
    return terms.astype(HALF)


def softmax_rows(normed, weights, label_ref, block, length):
    height, classes = normed.shape[0], weights.shape[1]
    logits = jnp.dot(normed, weights, preferred_element_type=WIDE)
    if label_ref.shape[0] == 1:
        label_row = label_ref[:, pl.ds(pl.multiple_of(block * height, height), height)]
    else:
        label_row = label_ref[pl.ds(block, 1), :]
    label = jnp.broadcast_to(label_row, (8, height)).T[:, :1]
    slot = block * height + lax.broadcasted_iota(jnp.int32, (height, 1), 0)
    valid = jnp.where(slot < length, 1.0, 0.0).astype(WIDE)
    top = jnp.max(logits, axis=1, keepdims=True)
    shifted = logits - top
    powers = jnp.exp(shifted)
    total = jnp.sum(powers, axis=1, keepdims=True)
    hit = lax.broadcasted_iota(jnp.int32, (height, classes), 1) == label
    picked = jnp.sum(jnp.where(hit, shifted, 0.0), axis=1, keepdims=True)
    loss = jnp.sum(valid * (jnp.log(total) - picked), axis=0, keepdims=True)
    probs = powers * (1.0 / total)
    return (valid * jnp.where(hit, probs - 1.0, probs)).astype(HALF), loss


def norm_rows(values, gain):
    values = values.astype(WIDE)
    inverse = lax.rsqrt(jnp.mean(values * values, axis=1, keepdims=True) + EPS)
    return (values * inverse * gain).astype(HALF)


def forward_near(lengths, labels, gains, rows, pieces):
    height, width = rows[0].shape
    depth, classes = pieces[0].shape
    n_dp, n_gain, n = len(pieces), len(gains), len(rows)

    def body(*refs):
        length_ref, label_ref = refs[:2]
        gain_refs, refs = refs[2 : 2 + n_gain], refs[2 + n_gain :]
        row_refs, refs = refs[:n], refs[n:]
        piece_refs, refs = refs[:n_dp], refs[n_dp:]
        loss_ref, gain_out, weight_ref, normed_ref, slope_ref, sems = refs
        me, dp = lax.axis_index("fsdp"), lax.axis_index("dp")

        def span(i):
            return pl.ds(pl.multiple_of((dp ^ i) * depth, depth), depth)

        copies = [pltpu.make_async_copy(piece_refs[i], weight_ref.at[span(i)], sems.at[i]) for i in range(n_dp)]
        for copy in copies:
            copy.start()
        if gains[0].shape[1] == width:
            gain_out[...] = gain_refs[0][...].astype(WIDE)
        else:
            lines = jnp.concatenate([ref[...].astype(WIDE) for ref in gain_refs], axis=0)
            for i in range(n_dp):
                gain_out[:, span(i)] = lines[i : i + 1]
        gain = gain_out[...]
        for j in range(n):
            normed_ref[j] = norm_rows(row_refs[j][...], gain)
        for copy in copies:
            copy.wait()
        weights = weight_ref[...]
        loss = jnp.zeros((1, 1), WIDE)
        for j in range(n):
            slopes, part = softmax_rows(normed_ref[j], weights, label_ref, me ^ j, length_ref[dp])
            slope_ref[j] = slopes
            loss = loss + part
        loss_ref[...] = jnp.broadcast_to(loss, loss_ref.shape)

    return pl.pallas_call(
        body,
        in_specs=[SMEM] + [VMEM] * (1 + n_gain + n) + [ANY] * n_dp,
        out_specs=[VMEM] * 5,
        out_shape=[
            jax.ShapeDtypeStruct((8, 128), WIDE),
            jax.ShapeDtypeStruct((1, width), WIDE),
            jax.ShapeDtypeStruct((width, classes), HALF),
            jax.ShapeDtypeStruct((n, height, width), HALF),
            jax.ShapeDtypeStruct((n, height, classes), HALF),
        ],
        scratch_shapes=[pltpu.SemaphoreType.DMA((n_dp,))],
        cost_estimate=cost(NEAR),
        compiler_params=params(20),
        name="forward_near",
    )(lengths, labels, *gains, *rows, *pieces)


def forward_far(lengths, labels, gain, weights, rows, normed, slopes, loss, n_dp):
    n = len(rows)
    n_near, height, width = normed.shape
    classes = weights.shape[1]
    depth = width // n_dp
    blocks = n_near + n

    def body(*refs):
        length_ref, label_ref, gain_ref, weight_ref = refs[:4]
        row_refs, refs = refs[4 : 4 + n], refs[4 + n :]
        near_normed, near_slopes, near_loss, loss_ref, slope_ref = refs[:5]
        part_refs, (normed_ref, slopes_ref, partial_ref) = refs[5:-3], refs[-3:]
        me, dp = lax.axis_index("fsdp"), lax.axis_index("dp")
        gain, weights = gain_ref[...], weight_ref[...]
        count = length_ref[0]
        for d in range(1, n_dp):
            count = count + length_ref[d]
        for j in range(n_near):
            normed_ref[j * height : (j + 1) * height, :] = near_normed[j]
            slopes_ref[j * height : (j + 1) * height, :] = near_slopes[j]
        loss = near_loss[:1, :1]
        for j in range(n):
            at = slice((n_near + j) * height, (n_near + j + 1) * height)
            normed_ref[at, :] = norm_rows(row_refs[j][...], gain)
        for j in range(n):
            at = slice((n_near + j) * height, (n_near + j + 1) * height)
            new, part = softmax_rows(normed_ref[at, :], weights, label_ref, me ^ (n_near + j), length_ref[dp])
            slope_ref[j] = new
            slopes_ref[at, :] = new
            loss = loss + part
        loss = jnp.broadcast_to(loss / (count.astype(WIDE) * blocks), (1, classes))
        loss_ref[...] = jnp.broadcast_to(loss, loss_ref.shape)
        step = min(256, width)
        for at in range(0, width, step):
            partial_ref[at : at + step, :] = lax.dot_general(
                normed_ref[:, at : at + step],
                slopes_ref[...],
                (((0,), (0,)), ((), ())),
                preferred_element_type=WIDE,
            ).astype(HALF)
        for i in range(n_dp):
            start = pl.multiple_of((dp ^ i) * depth, depth)
            part_refs[i][:depth, :] = partial_ref[pl.ds(start, depth), :]
        part_refs[n_dp - 1][depth:, :] = split_rows(loss, classes)

    out = pl.pallas_call(
        body,
        in_specs=[SMEM] + [VMEM] * (6 + n),
        out_specs=[VMEM] * (2 + n_dp),
        out_shape=[
            jax.ShapeDtypeStruct((8, classes), WIDE),
            jax.ShapeDtypeStruct((n, height, classes), HALF),
        ]
        + [jax.ShapeDtypeStruct((depth, classes), HALF)] * (n_dp - 1)
        + [jax.ShapeDtypeStruct((depth + EXTRA, classes), HALF)],
        scratch_shapes=[
            pltpu.VMEM((blocks * height, width), HALF),
            pltpu.VMEM((blocks * height, classes), HALF),
            pltpu.VMEM((width, classes), HALF),
        ],
        cost_estimate=cost(FAR),
        compiler_params=params(24),
        name="forward_far",
    )(lengths, labels, gain, weights, *rows, normed, slopes, loss)
    return out[0], out[1], out[2:]


def grad_rows(values, slopes, weights, gain):
    values = values.astype(WIDE)
    inverse = lax.rsqrt(jnp.mean(values * values, axis=1, keepdims=True) + EPS)
    back = lax.dot_general(slopes, weights, (((1,), (1,)), ((), ())), preferred_element_type=WIDE)
    weighted = back * gain
    scale = inverse * inverse * inverse * jnp.mean(weighted * values, axis=1, keepdims=True)
    return (inverse * weighted - values * scale).astype(HALF)


def backward(gain, weights, rows, slopes, after=(), held=()):
    n = len(rows)

    def body(gain_ref, weight_ref, slope_ref, *refs):
        for j in range(n):
            refs[n + len(after) + len(held) + j][...] = grad_rows(refs[j][...], slope_ref[j], weight_ref[...], gain_ref[...])

    return pl.pallas_call(
        body,
        in_specs=[VMEM] * (3 + n) + [ANY] * (len(after) + len(held)),
        out_specs=[VMEM] * n + [ANY] * len(held),
        out_shape=[jax.ShapeDtypeStruct(rows[0].shape, HALF)] * n
        + [jax.ShapeDtypeStruct(h.shape, h.dtype) for h in held],
        input_output_aliases={3 + n + len(after) + i: n + i for i in range(len(held))},
        cost_estimate=cost(BACKWARD),
        compiler_params=params(20),
        name="backward",
    )(gain, weights, slopes, *rows, *after, *held)


def fold(terms, loss=None, held=(), after=(), last=False):
    depth, classes = terms[0].shape
    n = len(terms)
    n_loss = 0 if loss is None else 1
    carries = n_loss and not last

    def body(*refs):
        ins, loss_in = refs[:n], refs[n : n + n_loss]
        outs = refs[n + n_loss + len(held) + len(after) :]
        total = ins[0][...].astype(WIDE)
        for ref in ins[1:]:
            total = total + ref[:depth, :].astype(WIDE)
        outs[0][:depth, :] = total.astype(outs[0].dtype)
        if n_loss:
            extra = ins[-1][depth:, :].astype(WIDE)
            value = loss_in[0][:1, :] + (extra[:1] + extra[1:2] + extra[2:3])
            outs[1][...] = jnp.broadcast_to(value[:, : outs[1].shape[1]], outs[1].shape)
            if carries:
                outs[0][depth:, :] = split_rows(value, classes)

    shapes = [jax.ShapeDtypeStruct((depth + (EXTRA if carries else 0), classes), WIDE if last else HALF)]
    if n_loss:
        shapes.append(jax.ShapeDtypeStruct((8, 128) if last else loss.shape, WIDE))
    out = pl.pallas_call(
        body,
        in_specs=[VMEM] * (n + n_loss) + [ANY] * (len(held) + len(after)),
        out_specs=[VMEM] * (1 + n_loss) + [ANY] * len(held),
        out_shape=shapes + [jax.ShapeDtypeStruct(h.shape, h.dtype) for h in held],
        input_output_aliases={n + n_loss + i: 1 + n_loss + i for i in range(len(held))},
        cost_estimate=cost(LAST if last else RIDE if n_loss else FOLD),
        compiler_params=params(8),
        name="fold",
    )(*terms, *([loss] if n_loss else []), *held, *after)
    return out[0], (out[1] if n_loss else None), out[1 + n_loss :]


def hold(gains, piece, after, claim=None):
    rows = sum(g.shape[0] for g in gains)

    def body(*refs):
        if gains:
            refs[-2][...] = jnp.concatenate([ref[...] for ref in refs[: len(gains)]], axis=0)

    out = pl.pallas_call(
        body,
        in_specs=[VMEM] * len(gains) + [ANY] * (1 + len(after)),
        out_specs=[VMEM] * bool(gains) + [ANY],
        out_shape=[jax.ShapeDtypeStruct((rows, g.shape[1]), HALF) for g in gains[:1]]
        + [jax.ShapeDtypeStruct(piece.shape, HALF)],
        input_output_aliases={len(gains): len(gains[:1])},
        cost_estimate=cost(claim or HOLD),
        compiler_params=params(8),
        name="hold",
    )(*gains, piece, *after)
    return out[0], out[-1]


def finish(parts, after):
    def body(*refs):
        total = refs[0][...]
        for ref in refs[1 : len(parts)]:
            total = total + ref[...]
        refs[-1][...] = total[:1, :1]

    return pl.pallas_call(
        body,
        in_specs=[VMEM] * len(parts) + [ANY] * len(after),
        out_specs=VMEM,
        out_shape=jax.ShapeDtypeStruct((1, 1), WIDE),
        cost_estimate=cost(FINISH),
        compiler_params=params(4),
        name="finish",
    )(*parts, *after)


def per_device(n_dp, n_fsdp, hidden, head, gain, targets, lengths):
    inner = 2
    line = n_dp // inner

    def swap(value, axis, offset):
        size = n_dp if axis == "dp" else n_fsdp
        return lax.ppermute(value, axis, [(i, i ^ offset) for i in range(size)])

    def exchange(blocks, after, claim=None):
        came = [swap(block, "fsdp", j + 2 & ~1) for j, block in reversed(list(enumerate(blocks)))][::-1]
        return [
            swap(hold([], block, [came[j - 1], *after], claim)[1], "fsdp", 1) if j % 2 else block
            for j, block in enumerate(came)
        ]

    small = gain.shape[1] % 128 == 0 and line == 4
    gains = [gain, swap(gain, "dp", 1)] if small else [gain]
    pieces = [None] * n_dp
    pieces[0] = head[0]
    for o in sorted(range(1, line), key=lambda o: (bin(o).count("1"), -o)):
        bit = o & -o
        if small and o == 3:
            break
        pieces[o * inner] = swap(pieces[(o ^ bit) * inner], "dp", bit * inner)
    own, side, *away, unpacked = unpack(hidden)
    for o in range(line):
        if small and o == 2:
            pieces[4] = hold([], pieces[4], [unpacked])[1]
        if small and o == 1:
            gain, pieces[2] = hold(gains, pieces[2], [pieces[1]])
        if pieces[o * inner] is not None:
            pieces[o * inner + 1] = swap(pieces[o * inner], "dp", 1)
    if small:
        gains = [gain, swap(gain, "dp", 2)]
        gain, side = hold(gains, side, [pieces[4]])
        gains = [gain, swap(gain, "dp", 4)]
        pieces[6] = hold([], swap(pieces[4], "dp", 2), [pieces[3], pieces[5]])[1]
        pieces[7] = swap(pieces[6], "dp", 1)
    else:
        gains = [lax.all_gather(gain, "dp", axis=1, tiled=True)]
    side = swap(side, "fsdp", 1)
    far = exchange(away, gains[1:], RELAY)

    height = targets.shape[0] // n_fsdp
    labels = targets.T if height % 128 == 0 else targets.reshape(n_fsdp, height)
    loss, gain_row, weights, normed, near_slopes = forward_near(lengths, labels, gains, [own, side], pieces)
    loss, far_slopes, parts = forward_far(
        lengths, labels, gain_row, weights, far, normed, near_slopes, loss, n_dp
    )

    far = backward(gain_row, weights, far, far_slopes)
    near = None
    across = [None] * line
    waiting = list(range(line - 1, -1, -1))
    for o in (waiting.pop(0), waiting.pop(0)):
        across[o] = swap(parts[o * inner + 1], "dp", 1)
    came = [[] for _ in range(line)]
    rides = line - 1
    order = far[-1:]
    for o in range(line - 1, 0, -1):
        held = [parts[waiting[0] * inner + 1]] if waiting else []
        if near is None and line > 2:
            held, later = [], held
        if o == rides:
            piece, loss, held = fold([parts[o * inner], across[o], *came[o]], loss, held, order)
        else:
            piece, _, held = fold([parts[o * inner], *came[o], across[o]], None, held, order)
        bit, order = o & -o, [piece]
        if near is None:
            near = backward(gain_row, weights, [own, side], near_slopes, [loss], later if line > 2 else [])
            near, held = near[:2], near[2:] or held
            beside = swap(near[1], "fsdp", 1)
        moved = swap(piece, "dp", bit * inner)
        if o == rides:
            rides = o ^ bit
            came[rides] = [*came[rides], moved]
        else:
            came[o ^ bit] = [moved, *came[o ^ bit]]
        if held:
            across[waiting.pop(0)] = swap(held[0], "dp", 1)
    grad_head, loss, _ = fold([parts[0], across[0], *came[0]], loss, last=True)

    grad_hidden, packed = pack([near[0], beside, *exchange(far, order)])

    parts = [loss] + [swap(loss, "fsdp", j) for j in range(1, n_fsdp)]
    return finish(parts, [packed])[0, 0], grad_hidden, grad_head[None]


def solution(mesh):
    n_dp, n_fsdp = mesh.shape["dp"], mesh.shape["fsdp"]
    placed = (
        P(("dp", "fsdp"), None, None),
        P("fsdp", "dp", None),
        P("fsdp", "dp"),
        P("dp", "fsdp"),
        P(),
    )
    return jax.shard_map(
        lambda *args: per_device(n_dp, n_fsdp, *args),
        mesh=mesh,
        in_specs=placed,
        out_specs=(P(), P(("dp", "fsdp"), None, None), P("fsdp", "dp", None)),
        check_vma=False,
    )
```

```python
import jax
import jax.numpy as jnp
from jax import lax
from jax.experimental import pallas as pl
from jax.experimental.pallas import tpu as pltpu
from jax.sharding import PartitionSpec as P

EPS = 1e-05
WIDE = jnp.float32
HALF = jnp.bfloat16
VMEM = pl.BlockSpec(memory_space=pltpu.VMEM)
SMEM = pl.BlockSpec(memory_space=pltpu.SMEM)
ANY = pl.BlockSpec(memory_space=pl.ANY)
PACK_ROWS = 256
EXTRA = 8
UNPACK, PACK, NEAR, FAR, BACKWARD, FOLD, HOLD, LAST, RELAY, FINISH, RIDE = 0.01, 0.01, 3, 0.01, 0.01, 0.01, 0.01, 3, 1.5, 0.01, 0.01


def params(mib):
    return pltpu.CompilerParams(vmem_limit_bytes=mib * 1024 * 1024)


def cost(gigaflops):
    return pl.CostEstimate(flops=int(gigaflops * 1e9), bytes_accessed=0, transcendentals=0)


def unpack(hidden):
    frames, positions, width = hidden.shape
    chunk = PACK_ROWS // positions
    rows = chunk * positions
    steps = frames // chunk

    def body(hidden_ref, *refs):
        outs, (stage, sems) = refs[:-2], refs[-2:]
        copies = [
            pltpu.make_async_copy(
                hidden_ref.at[pl.ds(i * chunk, chunk)], stage.at[pl.ds(i * chunk, chunk)], sems.at[i]
            )
            for i in range(steps)
        ]
        for copy in copies:
            copy.start()
        me = lax.axis_index("fsdp")
        r = lax.broadcasted_iota(jnp.int32, (rows, rows), 0)
        c = lax.broadcasted_iota(jnp.int32, (rows, rows), 1)
        pick = (lax.rem(r, chunk) == lax.div(c, positions)) & (
            lax.rem(c, positions) == (lax.div(r, chunk) ^ me)
        )
        pick = pick.astype(HALF)
        for i in range(steps):
            copies[i].wait()
            here = slice(i * chunk, (i + 1) * chunk)
            flat = stage[here].reshape(rows, width)
            moved = jnp.dot(pick, flat, preferred_element_type=WIDE).astype(HALF)
            for j in range(positions):
                part = moved[j * chunk : (j + 1) * chunk]
                outs[j][here, :] = part
        outs[-1][...] = jnp.zeros_like(outs[-1])

    return pl.pallas_call(
        body,
        in_specs=[ANY],
        out_specs=[VMEM] * (positions + 1),
        out_shape=[jax.ShapeDtypeStruct((frames, width), HALF)] * positions
        + [jax.ShapeDtypeStruct((8, 128), WIDE)],
        scratch_shapes=[pltpu.VMEM(hidden.shape, HALF), pltpu.SemaphoreType.DMA((steps,))],
        cost_estimate=cost(UNPACK),
        compiler_params=params(58),
        name="unpack",
    )(hidden)


def pack(parts):
    frames, width = parts[0].shape
    positions = len(parts)
    chunk = PACK_ROWS // positions
    rows = chunk * positions

    def body(*refs):
        me = lax.axis_index("fsdp")
        r = lax.broadcasted_iota(jnp.int32, (rows, rows), 0)
        c = lax.broadcasted_iota(jnp.int32, (rows, rows), 1)
        pick = (lax.rem(c, chunk) == lax.div(r, positions)) & (
            lax.rem(r, positions) == (lax.div(c, chunk) ^ me)
        )
        flat = jnp.concatenate([ref[...] for ref in refs[:-2]], axis=0)
        moved = jnp.dot(pick.astype(HALF), flat, preferred_element_type=WIDE).astype(HALF)
        refs[-2][...] = moved.reshape(chunk, positions, width)
        refs[-1][...] = jnp.zeros_like(refs[-1])

    return pl.pallas_call(
        body,
        grid=(frames // chunk,),
        in_specs=[pl.BlockSpec((chunk, width), lambda i: (i, 0))] * positions,
        out_specs=[pl.BlockSpec((chunk, positions, width), lambda i: (i, 0, 0)), pl.BlockSpec((8, 128), lambda i: (0, 0))],
        out_shape=[jax.ShapeDtypeStruct((frames, positions, width), HALF), jax.ShapeDtypeStruct((8, 128), WIDE)],
        cost_estimate=cost(PACK),
        compiler_params=params(24),
        name="pack",
    )(*parts)


def split_rows(value, classes):
    high = value.astype(HALF).astype(WIDE)
    middle = (value - high).astype(HALF).astype(WIDE)
    low = value - high - middle
    row = lax.broadcasted_iota(jnp.int32, (EXTRA, classes), 0)
    terms = jnp.where(row == 0, high, jnp.where(row == 1, middle, jnp.where(row == 2, low, 0.0)))
    return terms.astype(HALF)


def softmax_rows(normed, weights, label_ref, block, length):
    height, classes = normed.shape[0], weights.shape[1]
    logits = jnp.dot(normed, weights, preferred_element_type=WIDE)
    if label_ref.shape[0] == 1:
        label_row = label_ref[:, pl.ds(pl.multiple_of(block * height, height), height)]
    else:
        label_row = label_ref[pl.ds(block, 1), :]
    label = jnp.broadcast_to(label_row, (8, height)).T[:, :1]
    slot = block * height + lax.broadcasted_iota(jnp.int32, (height, 1), 0)
    valid = jnp.where(slot < length, 1.0, 0.0).astype(WIDE)
    top = jnp.max(logits, axis=1, keepdims=True)
    shifted = logits - top
    powers = jnp.exp(shifted)
    total = jnp.sum(powers, axis=1, keepdims=True)
    hit = lax.broadcasted_iota(jnp.int32, (height, classes), 1) == label
    picked = jnp.sum(jnp.where(hit, shifted, 0.0), axis=1, keepdims=True)
    loss = jnp.sum(valid * (jnp.log(total) - picked), axis=0, keepdims=True)
    probs = powers * (1.0 / total)
    return (valid * jnp.where(hit, probs - 1.0, probs)).astype(HALF), loss


def norm_rows(values, gain):
    values = values.astype(WIDE)
    inverse = lax.rsqrt(jnp.mean(values * values, axis=1, keepdims=True) + EPS)
    return (values * inverse * gain).astype(HALF)


def forward_near(lengths, labels, gains, rows, pieces):
    height, width = rows[0].shape
    depth, classes = pieces[0].shape
    n_dp, n_gain, n = len(pieces), len(gains), len(rows)

    def body(*refs):
        length_ref, label_ref = refs[:2]
        gain_refs, refs = refs[2 : 2 + n_gain], refs[2 + n_gain :]
        row_refs, refs = refs[:n], refs[n:]
        piece_refs, refs = refs[:n_dp], refs[n_dp:]
        loss_ref, gain_out, weight_ref, normed_ref, slope_ref, sems = refs
        me, dp = lax.axis_index("fsdp"), lax.axis_index("dp")

        def span(i):
            return pl.ds(pl.multiple_of((dp ^ i) * depth, depth), depth)

        copies = [pltpu.make_async_copy(piece_refs[i], weight_ref.at[span(i)], sems.at[i]) for i in range(n_dp)]
        for copy in copies:
            copy.start()
        if gains[0].shape[1] == width:
            gain_out[...] = gain_refs[0][...].astype(WIDE)
        else:
            lines = jnp.concatenate([ref[...].astype(WIDE) for ref in gain_refs], axis=0)
            for i in range(n_dp):
                gain_out[:, span(i)] = lines[i : i + 1]
        gain = gain_out[...]
        for j in range(n):
            normed_ref[j] = norm_rows(row_refs[j][...], gain)
        for copy in copies:
            copy.wait()
        weights = weight_ref[...]
        loss = jnp.zeros((1, 1), WIDE)
        for j in range(n):
            slopes, part = softmax_rows(normed_ref[j], weights, label_ref, me ^ j, length_ref[dp])
            slope_ref[j] = slopes
            loss = loss + part
        loss_ref[...] = jnp.broadcast_to(loss, loss_ref.shape)

    return pl.pallas_call(
        body,
        in_specs=[SMEM] + [VMEM] * (1 + n_gain + n) + [ANY] * n_dp,
        out_specs=[VMEM] * 5,
        out_shape=[
            jax.ShapeDtypeStruct((8, 128), WIDE),
            jax.ShapeDtypeStruct((1, width), WIDE),
            jax.ShapeDtypeStruct((width, classes), HALF),
            jax.ShapeDtypeStruct((n, height, width), HALF),
            jax.ShapeDtypeStruct((n, height, classes), HALF),
        ],
        scratch_shapes=[pltpu.SemaphoreType.DMA((n_dp,))],
        cost_estimate=cost(NEAR),
        compiler_params=params(20),
        name="forward_near",
    )(lengths, labels, *gains, *rows, *pieces)


def forward_far(lengths, labels, gain, weights, rows, normed, slopes, loss, n_dp):
    n = len(rows)
    n_near, height, width = normed.shape
    classes = weights.shape[1]
    depth = width // n_dp
    blocks = n_near + n

    def body(*refs):
        length_ref, label_ref, gain_ref, weight_ref = refs[:4]
        row_refs, refs = refs[4 : 4 + n], refs[4 + n :]
        near_normed, near_slopes, near_loss, loss_ref, slope_ref = refs[:5]
        part_refs, (normed_ref, slopes_ref, partial_ref) = refs[5:-3], refs[-3:]
        me, dp = lax.axis_index("fsdp"), lax.axis_index("dp")
        gain, weights = gain_ref[...], weight_ref[...]
        count = length_ref[0]
        for d in range(1, n_dp):
            count = count + length_ref[d]
        for j in range(n_near):
            normed_ref[j * height : (j + 1) * height, :] = near_normed[j]
            slopes_ref[j * height : (j + 1) * height, :] = near_slopes[j]
        loss = near_loss[:1, :1]
        for j in range(n):
            at = slice((n_near + j) * height, (n_near + j + 1) * height)
            normed_ref[at, :] = norm_rows(row_refs[j][...], gain)
        for j in range(n):
            at = slice((n_near + j) * height, (n_near + j + 1) * height)
            new, part = softmax_rows(normed_ref[at, :], weights, label_ref, me ^ (n_near + j), length_ref[dp])
            slope_ref[j] = new
            slopes_ref[at, :] = new
            loss = loss + part
        loss = jnp.broadcast_to(loss / (count.astype(WIDE) * blocks), (1, classes))
        loss_ref[...] = jnp.broadcast_to(loss, loss_ref.shape)
        step = min(256, width)
        for at in range(0, width, step):
            partial_ref[at : at + step, :] = lax.dot_general(
                normed_ref[:, at : at + step],
                slopes_ref[...],
                (((0,), (0,)), ((), ())),
                preferred_element_type=WIDE,
            ).astype(HALF)
        for i in range(n_dp):
            start = pl.multiple_of((dp ^ i) * depth, depth)
            part_refs[i][:depth, :] = partial_ref[pl.ds(start, depth), :]
        part_refs[n_dp - 1][depth:, :] = split_rows(loss, classes)

    out = pl.pallas_call(
        body,
        in_specs=[SMEM] + [VMEM] * (6 + n),
        out_specs=[VMEM] * (2 + n_dp),
        out_shape=[
            jax.ShapeDtypeStruct((8, classes), WIDE),
            jax.ShapeDtypeStruct((n, height, classes), HALF),
        ]
        + [jax.ShapeDtypeStruct((depth, classes), HALF)] * (n_dp - 1)
        + [jax.ShapeDtypeStruct((depth + EXTRA, classes), HALF)],
        scratch_shapes=[
            pltpu.VMEM((blocks * height, width), HALF),
            pltpu.VMEM((blocks * height, classes), HALF),
            pltpu.VMEM((width, classes), HALF),
        ],
        cost_estimate=cost(FAR),
        compiler_params=params(24),
        name="forward_far",
    )(lengths, labels, gain, weights, *rows, normed, slopes, loss)
    return out[0], out[1], out[2:]


def grad_rows(values, slopes, weights, gain):
    values = values.astype(WIDE)
    inverse = lax.rsqrt(jnp.mean(values * values, axis=1, keepdims=True) + EPS)
    back = lax.dot_general(slopes, weights, (((1,), (1,)), ((), ())), preferred_element_type=WIDE)
    weighted = back * gain
    scale = inverse * inverse * inverse * jnp.mean(weighted * values, axis=1, keepdims=True)
    return (inverse * weighted - values * scale).astype(HALF)


def backward(gain, weights, rows, slopes, after=(), held=()):
    n = len(rows)

    def body(gain_ref, weight_ref, slope_ref, *refs):
        for j in range(n):
            refs[n + len(after) + len(held) + j][...] = grad_rows(refs[j][...], slope_ref[j], weight_ref[...], gain_ref[...])

    return pl.pallas_call(
        body,
        in_specs=[VMEM] * (3 + n) + [ANY] * (len(after) + len(held)),
        out_specs=[VMEM] * n + [ANY] * len(held),
        out_shape=[jax.ShapeDtypeStruct(rows[0].shape, HALF)] * n
        + [jax.ShapeDtypeStruct(h.shape, h.dtype) for h in held],
        input_output_aliases={3 + n + len(after) + i: n + i for i in range(len(held))},
        cost_estimate=cost(BACKWARD),
        compiler_params=params(20),
        name="backward",
    )(gain, weights, slopes, *rows, *after, *held)


def fold(terms, loss=None, held=(), after=(), last=False):
    depth, classes = terms[0].shape
    n = len(terms)
    n_loss = 0 if loss is None else 1
    carries = n_loss and not last

    def body(*refs):
        ins, loss_in = refs[:n], refs[n : n + n_loss]
        outs = refs[n + n_loss + len(held) + len(after) :]
        total = ins[0][...].astype(WIDE)
        for ref in ins[1:]:
            total = total + ref[:depth, :].astype(WIDE)
        outs[0][:depth, :] = total.astype(outs[0].dtype)
        if n_loss:
            extra = ins[-1][depth:, :].astype(WIDE)
            value = loss_in[0][:1, :] + (extra[:1] + extra[1:2] + extra[2:3])
            outs[1][...] = jnp.broadcast_to(value[:, : outs[1].shape[1]], outs[1].shape)
            if carries:
                outs[0][depth:, :] = split_rows(value, classes)

    shapes = [jax.ShapeDtypeStruct((depth + (EXTRA if carries else 0), classes), WIDE if last else HALF)]
    if n_loss:
        shapes.append(jax.ShapeDtypeStruct((8, 128) if last else loss.shape, WIDE))
    out = pl.pallas_call(
        body,
        in_specs=[VMEM] * (n + n_loss) + [ANY] * (len(held) + len(after)),
        out_specs=[VMEM] * (1 + n_loss) + [ANY] * len(held),
        out_shape=shapes + [jax.ShapeDtypeStruct(h.shape, h.dtype) for h in held],
        input_output_aliases={n + n_loss + i: 1 + n_loss + i for i in range(len(held))},
        cost_estimate=cost(LAST if last else RIDE if n_loss else FOLD),
        compiler_params=params(8),
        name="fold",
    )(*terms, *([loss] if n_loss else []), *held, *after)
    return out[0], (out[1] if n_loss else None), out[1 + n_loss :]


def hold(gains, piece, after, claim=None):
    rows = sum(g.shape[0] for g in gains)

    def body(*refs):
        if gains:
            refs[-2][...] = jnp.concatenate([ref[...] for ref in refs[: len(gains)]], axis=0)

    out = pl.pallas_call(
        body,
        in_specs=[VMEM] * len(gains) + [ANY] * (1 + len(after)),
        out_specs=[VMEM] * bool(gains) + [ANY],
        out_shape=[jax.ShapeDtypeStruct((rows, g.shape[1]), HALF) for g in gains[:1]]
        + [jax.ShapeDtypeStruct(piece.shape, HALF)],
        input_output_aliases={len(gains): len(gains[:1])},
        cost_estimate=cost(claim or HOLD),
        compiler_params=params(8),
        name="hold",
    )(*gains, piece, *after)
    return out[0], out[-1]


def ride_end(loss, piece):
    def body(loss_ref, piece_ref, out_ref):
        extra = piece_ref[-EXTRA:, :128].astype(WIDE)
        out_ref[...] = loss_ref[:, :128] + (extra[:1] + extra[1:2] + extra[2:3])

    return pl.pallas_call(
        body,
        in_specs=[VMEM] * 2,
        out_specs=VMEM,
        out_shape=jax.ShapeDtypeStruct((8, 128), WIDE),
        cost_estimate=cost(HOLD),
        compiler_params=params(8),
        name="ride_end",
    )(loss, piece)


def finish(parts, after):
    def body(*refs):
        total = refs[0][...]
        for ref in refs[1 : len(parts)]:
            total = total + ref[...]
        refs[-1][...] = total[:1, :1]

    return pl.pallas_call(
        body,
        in_specs=[VMEM] * len(parts) + [ANY] * len(after),
        out_specs=VMEM,
        out_shape=jax.ShapeDtypeStruct((1, 1), WIDE),
        cost_estimate=cost(FINISH),
        compiler_params=params(4),
        name="finish",
    )(*parts, *after)


def per_device(n_dp, n_fsdp, hidden, head, gain, targets, lengths):
    inner = 2
    line = n_dp // inner

    def swap(value, axis, offset):
        size = n_dp if axis == "dp" else n_fsdp
        return lax.ppermute(value, axis, [(i, i ^ offset) for i in range(size)])

    def exchange(blocks, after, claim=None):
        came = [swap(block, "fsdp", j + 2 & ~1) for j, block in reversed(list(enumerate(blocks)))][::-1]
        return [
            swap(hold([], block, [came[j - 1], *after], claim)[1], "fsdp", 1) if j % 2 else block
            for j, block in enumerate(came)
        ]

    small = gain.shape[1] % 128 == 0 and line == 4
    gains = [gain, swap(gain, "dp", 1)] if small else [gain]
    pieces = [None] * n_dp
    pieces[0] = head[0]
    for o in sorted(range(1, line), key=lambda o: (bin(o).count("1"), -o)):
        bit = o & -o
        if small and o == 3:
            break
        pieces[o * inner] = swap(pieces[(o ^ bit) * inner], "dp", bit * inner)
    own, side, *away, unpacked = unpack(hidden)
    for o in range(line):
        if small and o == 2:
            pieces[4] = hold([], pieces[4], [unpacked])[1]
        if small and o == 1:
            gain, pieces[2] = hold(gains, pieces[2], [pieces[1]])
        if pieces[o * inner] is not None:
            pieces[o * inner + 1] = swap(pieces[o * inner], "dp", 1)
    if small:
        gains = [gain, swap(gain, "dp", 2)]
        gain, side = hold(gains, side, [pieces[4]])
        gains = [gain, swap(gain, "dp", 4)]
        pieces[6] = hold([], swap(pieces[4], "dp", 2), [pieces[3], pieces[5]])[1]
        pieces[7] = swap(pieces[6], "dp", 1)
    else:
        gains = [lax.all_gather(gain, "dp", axis=1, tiled=True)]
    side = swap(side, "fsdp", 1)
    far = exchange(away, gains[1:], RELAY)

    height = targets.shape[0] // n_fsdp
    labels = targets.T if height % 128 == 0 else targets.reshape(n_fsdp, height)
    loss, gain_row, weights, normed, near_slopes = forward_near(lengths, labels, gains, [own, side], pieces)
    loss, far_slopes, parts = forward_far(
        lengths, labels, gain_row, weights, far, normed, near_slopes, loss, n_dp
    )

    far = backward(gain_row, weights, far, far_slopes)
    near = None
    across = [None] * line
    waiting = list(range(line - 1, -1, -1))
    for o in (waiting.pop(0), waiting.pop(0)):
        across[o] = swap(parts[o * inner + 1], "dp", 1)
    came = [[] for _ in range(line)]
    rides = line - 1
    order = far[-1:]
    for o in range(line - 1, 0, -1):
        held = [parts[waiting[0] * inner + 1]] if waiting and (o > 2 or o == 1) else []
        if near is None and line > 2:
            held, later = [], held
        if o == rides:
            piece, loss, held = fold([parts[o * inner], across[o], *came[o]], loss, held, order)
        else:
            piece, _, held = fold([parts[o * inner], *came[o], across[o]], None, held, order)
        bit, order = o & -o, [piece]
        if near is None:
            near = backward(gain_row, weights, [own, side], near_slopes, [loss], later if line > 2 else [])
            near, held = near[:2], near[2:] or held
            beside = swap(near[1], "fsdp", 1)
        moved = swap(piece, "dp", bit * inner)
        if o == rides:
            rides = o ^ bit
            came[rides] = [*came[rides], moved]
        else:
            came[o ^ bit] = [moved, *came[o ^ bit]]
        if held:
            across[waiting.pop(0)] = swap(held[0], "dp", 1)
    loss = ride_end(loss, came[0][-1])

    grad_hidden, packed = pack([near[0], beside, *exchange(far, order)])

    grad_head = fold([parts[0], across[0], *came[0]], None, (), [], last=True)[0]

    parts = [loss] + [swap(loss, "fsdp", j) for j in range(1, n_fsdp)]
    return finish(parts, [packed])[0, 0], grad_hidden, grad_head[None]


def solution(mesh):
    n_dp, n_fsdp = mesh.shape["dp"], mesh.shape["fsdp"]
    placed = (
        P(("dp", "fsdp"), None, None),
        P("fsdp", "dp", None),
        P("fsdp", "dp"),
        P("dp", "fsdp"),
        P(),
    )
    return jax.shard_map(
        lambda *args: per_device(n_dp, n_fsdp, *args),
        mesh=mesh,
        in_specs=placed,
        out_specs=(P(), P(("dp", "fsdp"), None, None), P("fsdp", "dp", None)),
        check_vma=False,
    )
```

```python
import jax
import jax.numpy as jnp
from jax import lax
from jax.experimental import pallas as pl
from jax.experimental.pallas import tpu as pltpu
from jax.sharding import PartitionSpec as P

EPS = 1e-05
WIDE = jnp.float32
HALF = jnp.bfloat16
VMEM = pl.BlockSpec(memory_space=pltpu.VMEM)
SMEM = pl.BlockSpec(memory_space=pltpu.SMEM)
ANY = pl.BlockSpec(memory_space=pl.ANY)
PACK_ROWS = 256
EXTRA = 8
UNPACK, PACK, NEAR, FAR, BACKWARD, FOLD, HOLD, LAST, RELAY, FINISH, RIDE = 0.01, 0.01, 3, 0.01, 0.01, 0.01, 0.01, 3, 1.5, 0.01, 0.01


def params(mib):
    return pltpu.CompilerParams(vmem_limit_bytes=mib * 1024 * 1024)


def cost(gigaflops):
    return pl.CostEstimate(flops=int(gigaflops * 1e9), bytes_accessed=0, transcendentals=0)


def unpack(hidden):
    frames, positions, width = hidden.shape
    chunk = PACK_ROWS // positions
    rows = chunk * positions
    steps = frames // chunk

    def body(hidden_ref, *refs):
        outs, (stage, sems) = refs[:-2], refs[-2:]
        copies = [
            pltpu.make_async_copy(
                hidden_ref.at[pl.ds(i * chunk, chunk)], stage.at[pl.ds(i * chunk, chunk)], sems.at[i]
            )
            for i in range(steps)
        ]
        for copy in copies:
            copy.start()
        me = lax.axis_index("fsdp")
        r = lax.broadcasted_iota(jnp.int32, (rows, rows), 0)
        c = lax.broadcasted_iota(jnp.int32, (rows, rows), 1)
        pick = (lax.rem(r, chunk) == lax.div(c, positions)) & (
            lax.rem(c, positions) == (lax.div(r, chunk) ^ me)
        )
        pick = pick.astype(HALF)
        for i in range(steps):
            copies[i].wait()
            here = slice(i * chunk, (i + 1) * chunk)
            flat = stage[here].reshape(rows, width)
            moved = jnp.dot(pick, flat, preferred_element_type=WIDE).astype(HALF)
            for j in range(positions):
                part = moved[j * chunk : (j + 1) * chunk]
                outs[j][here, :] = part
        outs[-1][...] = jnp.zeros_like(outs[-1])

    return pl.pallas_call(
        body,
        in_specs=[ANY],
        out_specs=[VMEM] * (positions + 1),
        out_shape=[jax.ShapeDtypeStruct((frames, width), HALF)] * positions
        + [jax.ShapeDtypeStruct((8, 128), WIDE)],
        scratch_shapes=[pltpu.VMEM(hidden.shape, HALF), pltpu.SemaphoreType.DMA((steps,))],
        cost_estimate=cost(UNPACK),
        compiler_params=params(58),
        name="unpack",
    )(hidden)


def pack(parts):
    frames, width = parts[0].shape
    positions = len(parts)
    chunk = PACK_ROWS // positions
    rows = chunk * positions

    def body(*refs):
        me = lax.axis_index("fsdp")
        r = lax.broadcasted_iota(jnp.int32, (rows, rows), 0)
        c = lax.broadcasted_iota(jnp.int32, (rows, rows), 1)
        pick = (lax.rem(c, chunk) == lax.div(r, positions)) & (
            lax.rem(r, positions) == (lax.div(c, chunk) ^ me)
        )
        flat = jnp.concatenate([ref[...] for ref in refs[:-2]], axis=0)
        moved = jnp.dot(pick.astype(HALF), flat, preferred_element_type=WIDE).astype(HALF)
        refs[-2][...] = moved.reshape(chunk, positions, width)
        refs[-1][...] = jnp.zeros_like(refs[-1])

    return pl.pallas_call(
        body,
        grid=(frames // chunk,),
        in_specs=[pl.BlockSpec((chunk, width), lambda i: (i, 0))] * positions,
        out_specs=[pl.BlockSpec((chunk, positions, width), lambda i: (i, 0, 0)), pl.BlockSpec((8, 128), lambda i: (0, 0))],
        out_shape=[jax.ShapeDtypeStruct((frames, positions, width), HALF), jax.ShapeDtypeStruct((8, 128), WIDE)],
        cost_estimate=cost(PACK),
        compiler_params=params(24),
        name="pack",
    )(*parts)


def split_rows(value, classes):
    high = value.astype(HALF).astype(WIDE)
    middle = (value - high).astype(HALF).astype(WIDE)
    low = value - high - middle
    row = lax.broadcasted_iota(jnp.int32, (EXTRA, classes), 0)
    terms = jnp.where(row == 0, high, jnp.where(row == 1, middle, jnp.where(row == 2, low, 0.0)))
    return terms.astype(HALF)


def softmax_rows(normed, weights, label_ref, block, length):
    height, classes = normed.shape[0], weights.shape[1]
    logits = jnp.dot(normed, weights, preferred_element_type=WIDE)
    if label_ref.shape[0] == 1:
        label_row = label_ref[:, pl.ds(pl.multiple_of(block * height, height), height)]
    else:
        label_row = label_ref[pl.ds(block, 1), :]
    label = jnp.broadcast_to(label_row, (8, height)).T[:, :1]
    slot = block * height + lax.broadcasted_iota(jnp.int32, (height, 1), 0)
    valid = jnp.where(slot < length, 1.0, 0.0).astype(WIDE)
    top = jnp.max(logits, axis=1, keepdims=True)
    shifted = logits - top
    powers = jnp.exp(shifted)
    total = jnp.sum(powers, axis=1, keepdims=True)
    hit = lax.broadcasted_iota(jnp.int32, (height, classes), 1) == label
    picked = jnp.sum(jnp.where(hit, shifted, 0.0), axis=1, keepdims=True)
    loss = jnp.sum(valid * (jnp.log(total) - picked), axis=0, keepdims=True)
    probs = powers * (1.0 / total)
    return (valid * jnp.where(hit, probs - 1.0, probs)).astype(HALF), loss


def norm_rows(values, gain):
    values = values.astype(WIDE)
    inverse = lax.rsqrt(jnp.mean(values * values, axis=1, keepdims=True) + EPS)
    return (values * inverse * gain).astype(HALF)


def forward_near(lengths, labels, gains, rows, pieces):
    height, width = rows[0].shape
    depth, classes = pieces[0].shape
    n_dp, n_gain, n = len(pieces), len(gains), len(rows)

    def body(*refs):
        length_ref, label_ref = refs[:2]
        gain_refs, refs = refs[2 : 2 + n_gain], refs[2 + n_gain :]
        row_refs, refs = refs[:n], refs[n:]
        piece_refs, refs = refs[:n_dp], refs[n_dp:]
        loss_ref, gain_out, weight_ref, normed_ref, slope_ref, sems = refs
        me, dp = lax.axis_index("fsdp"), lax.axis_index("dp")

        def span(i):
            return pl.ds(pl.multiple_of((dp ^ i) * depth, depth), depth)

        copies = [pltpu.make_async_copy(piece_refs[i], weight_ref.at[span(i)], sems.at[i]) for i in range(n_dp)]
        for copy in copies:
            copy.start()
        if gains[0].shape[1] == width:
            gain_out[...] = gain_refs[0][...].astype(WIDE)
        else:
            lines = jnp.concatenate([ref[...].astype(WIDE) for ref in gain_refs], axis=0)
            for i in range(n_dp):
                gain_out[:, span(i)] = lines[i : i + 1]
        gain = gain_out[...]
        for j in range(n):
            normed_ref[j] = norm_rows(row_refs[j][...], gain)
        for copy in copies:
            copy.wait()
        weights = weight_ref[...]
        loss = jnp.zeros((1, 1), WIDE)
        for j in range(n):
            slopes, part = softmax_rows(normed_ref[j], weights, label_ref, me ^ j, length_ref[dp])
            slope_ref[j] = slopes
            loss = loss + part
        loss_ref[...] = jnp.broadcast_to(loss, loss_ref.shape)

    return pl.pallas_call(
        body,
        in_specs=[SMEM] + [VMEM] * (1 + n_gain + n) + [ANY] * n_dp,
        out_specs=[VMEM] * 5,
        out_shape=[
            jax.ShapeDtypeStruct((8, 128), WIDE),
            jax.ShapeDtypeStruct((1, width), WIDE),
            jax.ShapeDtypeStruct((width, classes), HALF),
            jax.ShapeDtypeStruct((n, height, width), HALF),
            jax.ShapeDtypeStruct((n, height, classes), HALF),
        ],
        scratch_shapes=[pltpu.SemaphoreType.DMA((n_dp,))],
        cost_estimate=cost(NEAR),
        compiler_params=params(20),
        name="forward_near",
    )(lengths, labels, *gains, *rows, *pieces)


def forward_far(lengths, labels, gain, weights, rows, normed, slopes, loss, n_dp):
    n = len(rows)
    n_near, height, width = normed.shape
    classes = weights.shape[1]
    depth = width // n_dp
    blocks = n_near + n

    def body(*refs):
        length_ref, label_ref, gain_ref, weight_ref = refs[:4]
        row_refs, refs = refs[4 : 4 + n], refs[4 + n :]
        near_normed, near_slopes, near_loss, loss_ref, slope_ref = refs[:5]
        part_refs, (normed_ref, slopes_ref, partial_ref) = refs[5:-3], refs[-3:]
        me, dp = lax.axis_index("fsdp"), lax.axis_index("dp")
        gain, weights = gain_ref[...], weight_ref[...]
        count = length_ref[0]
        for d in range(1, n_dp):
            count = count + length_ref[d]
        for j in range(n_near):
            normed_ref[j * height : (j + 1) * height, :] = near_normed[j]
            slopes_ref[j * height : (j + 1) * height, :] = near_slopes[j]
        loss = near_loss[:1, :1]
        for j in range(n):
            at = slice((n_near + j) * height, (n_near + j + 1) * height)
            normed_ref[at, :] = norm_rows(row_refs[j][...], gain)
        for j in range(n):
            at = slice((n_near + j) * height, (n_near + j + 1) * height)
            new, part = softmax_rows(normed_ref[at, :], weights, label_ref, me ^ (n_near + j), length_ref[dp])
            slope_ref[j] = new
            slopes_ref[at, :] = new
            loss = loss + part
        loss = jnp.broadcast_to(loss / (count.astype(WIDE) * blocks), (1, classes))
        loss_ref[...] = jnp.broadcast_to(loss, loss_ref.shape)
        step = min(256, width)
        for at in range(0, width, step):
            partial_ref[at : at + step, :] = lax.dot_general(
                normed_ref[:, at : at + step],
                slopes_ref[...],
                (((0,), (0,)), ((), ())),
                preferred_element_type=WIDE,
            ).astype(HALF)
        for i in range(n_dp):
            start = pl.multiple_of((dp ^ i) * depth, depth)
            part_refs[i][:depth, :] = partial_ref[pl.ds(start, depth), :]
        part_refs[n_dp - 1][depth:, :] = split_rows(loss, classes)

    out = pl.pallas_call(
        body,
        in_specs=[SMEM] + [VMEM] * (6 + n),
        out_specs=[VMEM] * (2 + n_dp),
        out_shape=[
            jax.ShapeDtypeStruct((8, classes), WIDE),
            jax.ShapeDtypeStruct((n, height, classes), HALF),
        ]
        + [jax.ShapeDtypeStruct((depth, classes), HALF)] * (n_dp - 1)
        + [jax.ShapeDtypeStruct((depth + EXTRA, classes), HALF)],
        scratch_shapes=[
            pltpu.VMEM((blocks * height, width), HALF),
            pltpu.VMEM((blocks * height, classes), HALF),
            pltpu.VMEM((width, classes), HALF),
        ],
        cost_estimate=cost(FAR),
        compiler_params=params(24),
        name="forward_far",
    )(lengths, labels, gain, weights, *rows, normed, slopes, loss)
    return out[0], out[1], out[2:]


def grad_rows(values, slopes, weights, gain):
    values = values.astype(WIDE)
    inverse = lax.rsqrt(jnp.mean(values * values, axis=1, keepdims=True) + EPS)
    back = lax.dot_general(slopes, weights, (((1,), (1,)), ((), ())), preferred_element_type=WIDE)
    weighted = back * gain
    scale = inverse * inverse * inverse * jnp.mean(weighted * values, axis=1, keepdims=True)
    return (inverse * weighted - values * scale).astype(HALF)


def backward(gain, weights, rows, slopes, after=(), held=()):
    n = len(rows)

    def body(gain_ref, weight_ref, slope_ref, *refs):
        for j in range(n):
            refs[n + len(after) + len(held) + j][...] = grad_rows(refs[j][...], slope_ref[j], weight_ref[...], gain_ref[...])

    return pl.pallas_call(
        body,
        in_specs=[VMEM] * (3 + n) + [ANY] * (len(after) + len(held)),
        out_specs=[VMEM] * n + [ANY] * len(held),
        out_shape=[jax.ShapeDtypeStruct(rows[0].shape, HALF)] * n
        + [jax.ShapeDtypeStruct(h.shape, h.dtype) for h in held],
        input_output_aliases={3 + n + len(after) + i: n + i for i in range(len(held))},
        cost_estimate=cost(BACKWARD),
        compiler_params=params(20),
        name="backward",
    )(gain, weights, slopes, *rows, *after, *held)


def fold(terms, loss=None, held=(), after=(), last=False):
    depth, classes = terms[0].shape
    n = len(terms)
    n_loss = 0 if loss is None else 1
    carries = n_loss and not last

    def body(*refs):
        ins, loss_in = refs[:n], refs[n : n + n_loss]
        outs = refs[n + n_loss + len(held) + len(after) :]
        total = ins[0][...].astype(WIDE)
        for ref in ins[1:]:
            total = total + ref[:depth, :].astype(WIDE)
        outs[0][:depth, :] = total.astype(outs[0].dtype)
        if n_loss:
            extra = ins[-1][depth:, :].astype(WIDE)
            value = loss_in[0][:1, :] + (extra[:1] + extra[1:2] + extra[2:3])
            outs[1][...] = jnp.broadcast_to(value[:, : outs[1].shape[1]], outs[1].shape)
            if carries:
                outs[0][depth:, :] = split_rows(value, classes)

    shapes = [jax.ShapeDtypeStruct((depth + (EXTRA if carries else 0), classes), WIDE if last else HALF)]
    if n_loss:
        shapes.append(jax.ShapeDtypeStruct((8, 128) if last else loss.shape, WIDE))
    out = pl.pallas_call(
        body,
        in_specs=[VMEM] * (n + n_loss) + [ANY] * (len(held) + len(after)),
        out_specs=[VMEM] * (1 + n_loss) + [ANY] * len(held),
        out_shape=shapes + [jax.ShapeDtypeStruct(h.shape, h.dtype) for h in held],
        input_output_aliases={n + n_loss + i: 1 + n_loss + i for i in range(len(held))},
        cost_estimate=cost(LAST if last else RIDE if n_loss else FOLD),
        compiler_params=params(8),
        name="fold",
    )(*terms, *([loss] if n_loss else []), *held, *after)
    return out[0], (out[1] if n_loss else None), out[1 + n_loss :]


def hold(gains, piece, after, claim=None):
    rows = sum(g.shape[0] for g in gains)

    def body(*refs):
        if gains:
            refs[-2][...] = jnp.concatenate([ref[...] for ref in refs[: len(gains)]], axis=0)

    out = pl.pallas_call(
        body,
        in_specs=[VMEM] * len(gains) + [ANY] * (1 + len(after)),
        out_specs=[VMEM] * bool(gains) + [ANY],
        out_shape=[jax.ShapeDtypeStruct((rows, g.shape[1]), HALF) for g in gains[:1]]
        + [jax.ShapeDtypeStruct(piece.shape, HALF)],
        input_output_aliases={len(gains): len(gains[:1])},
        cost_estimate=cost(claim or HOLD),
        compiler_params=params(8),
        name="hold",
    )(*gains, piece, *after)
    return out[0], out[-1]


def ride_end(loss, piece):
    def body(loss_ref, piece_ref, out_ref):
        extra = piece_ref[-EXTRA:, :128].astype(WIDE)
        out_ref[...] = loss_ref[:, :128] + (extra[:1] + extra[1:2] + extra[2:3])

    return pl.pallas_call(
        body,
        in_specs=[VMEM] * 2,
        out_specs=VMEM,
        out_shape=jax.ShapeDtypeStruct((8, 128), WIDE),
        cost_estimate=cost(HOLD),
        compiler_params=params(8),
        name="ride_end",
    )(loss, piece)


def finish(parts, after):
    def body(*refs):
        total = refs[0][...]
        for ref in refs[1 : len(parts)]:
            total = total + ref[...]
        refs[-1][...] = total[:1, :1]

    return pl.pallas_call(
        body,
        in_specs=[VMEM] * len(parts) + [ANY] * len(after),
        out_specs=VMEM,
        out_shape=jax.ShapeDtypeStruct((1, 1), WIDE),
        cost_estimate=cost(FINISH),
        compiler_params=params(4),
        name="finish",
    )(*parts, *after)


def per_device(n_dp, n_fsdp, hidden, head, gain, targets, lengths):
    inner = 2
    line = n_dp // inner

    def swap(value, axis, offset):
        size = n_dp if axis == "dp" else n_fsdp
        return lax.ppermute(value, axis, [(i, i ^ offset) for i in range(size)])

    def exchange(blocks, after, claim=None):
        came = [swap(block, "fsdp", j + 2 & ~1) for j, block in reversed(list(enumerate(blocks)))][::-1]
        return [
            swap(hold([], block, [came[j - 1], *after], claim)[1], "fsdp", 1) if j % 2 else block
            for j, block in enumerate(came)
        ]

    small = gain.shape[1] % 128 == 0 and line == 4
    gains = [gain, swap(gain, "dp", 1)] if small else [gain]
    pieces = [None] * n_dp
    pieces[0] = head[0]
    for o in sorted(range(1, line), key=lambda o: (bin(o).count("1"), -o)):
        bit = o & -o
        if small and o == 3:
            break
        pieces[o * inner] = swap(pieces[(o ^ bit) * inner], "dp", bit * inner)
    own, side, *away, unpacked = unpack(hidden)
    if not small:
        for o in range(line):
            pieces[o * inner + 1] = swap(pieces[o * inner], "dp", 1)
    if small:
        pieces[1] = swap(pieces[0], "dp", 1)
        gain, pieces[1] = hold(gains, pieces[1], [pieces[2]])
        pieces[3] = swap(pieces[1], "dp", 2)
        pieces[4] = hold([], pieces[4], [unpacked])[1]
        pieces[5] = swap(pieces[4], "dp", 1)
        gains = [gain, swap(gain, "dp", 2)]
        gain, side = hold(gains, side, [pieces[4]])
        gains = [gain, swap(gain, "dp", 4)]
        pieces[6] = hold([], swap(pieces[4], "dp", 2), [pieces[3], pieces[5]])[1]
        pieces[7] = swap(pieces[6], "dp", 1)
    else:
        gains = [lax.all_gather(gain, "dp", axis=1, tiled=True)]
    side = swap(side, "fsdp", 1)
    far = exchange(away, gains[1:], RELAY)

    height = targets.shape[0] // n_fsdp
    labels = targets.T if height % 128 == 0 else targets.reshape(n_fsdp, height)
    loss, gain_row, weights, normed, near_slopes = forward_near(lengths, labels, gains, [own, side], pieces)
    loss, far_slopes, parts = forward_far(
        lengths, labels, gain_row, weights, far, normed, near_slopes, loss, n_dp
    )

    far = backward(gain_row, weights, far, far_slopes)
    near = None
    first = [swap(parts[inner + 1], "dp", inner), swap(parts[inner], "dp", inner)]
    across = [None] * line
    waiting = list(range(line - 1, 1, -1))
    for o in waiting[:2]:
        across[o] = swap(parts[o * inner + 1], "dp", 1)
    waiting = waiting[2:]
    came = [[] for _ in range(line)]
    rides = line - 1
    order = [*far[-1:], first[0]]
    for o in range(line - 1, 1, -1):
        held = [parts[waiting[0] * inner + 1]] if waiting else []
        if o == rides:
            piece, loss, held = fold([parts[o * inner], across[o], *came[o]], loss, held, order)
        else:
            piece, _, held = fold([parts[o * inner], *came[o], across[o]], None, held, order)
        bit, order = o & -o, [piece]
        if near is None:
            near = backward(gain_row, weights, [own, side], near_slopes, [loss])
            beside = swap(near[1], "fsdp", 1)
        moved = swap(piece, "dp", bit * inner)
        if o == rides:
            rides = o ^ bit
            came[rides] = [*came[rides], moved]
        else:
            came[o ^ bit] = [moved, *came[o ^ bit]]
        if held:
            across[waiting.pop(0)] = swap(held[0], "dp", 1)
    both, _, _ = fold([parts[1], first[0]], None, (), near[-1:])
    across[0] = swap(both, "dp", 1)
    came[0] = [first[1], *came[0]]
    loss = ride_end(loss, came[0][-1])

    grad_hidden, packed = pack([near[0], beside, *exchange(far, order)])

    grad_head = fold([parts[0], across[0], *came[0]], None, (), [], last=True)[0]

    parts = [loss] + [swap(loss, "fsdp", j) for j in range(1, n_fsdp)]
    return finish(parts, [packed])[0, 0], grad_hidden, grad_head[None]


def solution(mesh):
    n_dp, n_fsdp = mesh.shape["dp"], mesh.shape["fsdp"]
    placed = (
        P(("dp", "fsdp"), None, None),
        P("fsdp", "dp", None),
        P("fsdp", "dp"),
        P("dp", "fsdp"),
        P(),
    )
    return jax.shard_map(
        lambda *args: per_device(n_dp, n_fsdp, *args),
        mesh=mesh,
        in_specs=placed,
        out_specs=(P(), P(("dp", "fsdp"), None, None), P("fsdp", "dp", None)),
        check_vma=False,
    )
```

```python
import jax
import jax.numpy as jnp
from jax import lax
from jax.experimental import pallas as pl
from jax.experimental.pallas import tpu as pltpu
from jax.sharding import PartitionSpec as P

EPS = 1e-05
WIDE = jnp.float32
HALF = jnp.bfloat16
VMEM = pl.BlockSpec(memory_space=pltpu.VMEM)
SMEM = pl.BlockSpec(memory_space=pltpu.SMEM)
ANY = pl.BlockSpec(memory_space=pl.ANY)
PACK_ROWS = 256
EXTRA = 8
UNPACK, PACK, NEAR, FAR, BACKWARD, FOLD, HOLD, LAST, RELAY, FINISH, RIDE = 0.01, 0.01, 3, 0.01, 0.01, 0.01, 0.01, 3, 1.5, 0.01, 0.01


def params(mib):
    return pltpu.CompilerParams(vmem_limit_bytes=mib * 1024 * 1024)


def cost(gigaflops):
    return pl.CostEstimate(flops=int(gigaflops * 1e9), bytes_accessed=0, transcendentals=0)


def unpack(hidden):
    frames, positions, width = hidden.shape
    chunk = PACK_ROWS // positions
    rows = chunk * positions
    steps = frames // chunk

    def body(hidden_ref, *refs):
        outs, (stage, sems) = refs[:-2], refs[-2:]
        copies = [
            pltpu.make_async_copy(
                hidden_ref.at[pl.ds(i * chunk, chunk)], stage.at[pl.ds(i * chunk, chunk)], sems.at[i]
            )
            for i in range(steps)
        ]
        for copy in copies:
            copy.start()
        me = lax.axis_index("fsdp")
        r = lax.broadcasted_iota(jnp.int32, (rows, rows), 0)
        c = lax.broadcasted_iota(jnp.int32, (rows, rows), 1)
        pick = (lax.rem(r, chunk) == lax.div(c, positions)) & (
            lax.rem(c, positions) == (lax.div(r, chunk) ^ me)
        )
        pick = pick.astype(HALF)
        for i in range(steps):
            copies[i].wait()
            here = slice(i * chunk, (i + 1) * chunk)
            flat = stage[here].reshape(rows, width)
            moved = jnp.dot(pick, flat, preferred_element_type=WIDE).astype(HALF)
            for j in range(positions):
                part = moved[j * chunk : (j + 1) * chunk]
                outs[j][here, :] = part
        outs[-1][...] = jnp.zeros_like(outs[-1])

    return pl.pallas_call(
        body,
        in_specs=[ANY],
        out_specs=[VMEM] * (positions + 1),
        out_shape=[jax.ShapeDtypeStruct((frames, width), HALF)] * positions
        + [jax.ShapeDtypeStruct((8, 128), WIDE)],
        scratch_shapes=[pltpu.VMEM(hidden.shape, HALF), pltpu.SemaphoreType.DMA((steps,))],
        cost_estimate=cost(UNPACK),
        compiler_params=params(58),
        name="unpack",
    )(hidden)


def pack(parts):
    frames, width = parts[0].shape
    positions = len(parts)
    chunk = PACK_ROWS // positions
    rows = chunk * positions

    def body(*refs):
        me = lax.axis_index("fsdp")
        r = lax.broadcasted_iota(jnp.int32, (rows, rows), 0)
        c = lax.broadcasted_iota(jnp.int32, (rows, rows), 1)
        pick = (lax.rem(c, chunk) == lax.div(r, positions)) & (
            lax.rem(r, positions) == (lax.div(c, chunk) ^ me)
        )
        flat = jnp.concatenate([ref[...] for ref in refs[:-2]], axis=0)
        moved = jnp.dot(pick.astype(HALF), flat, preferred_element_type=WIDE).astype(HALF)
        refs[-2][...] = moved.reshape(chunk, positions, width)
        refs[-1][...] = jnp.zeros_like(refs[-1])

    return pl.pallas_call(
        body,
        grid=(frames // chunk,),
        in_specs=[pl.BlockSpec((chunk, width), lambda i: (i, 0))] * positions,
        out_specs=[pl.BlockSpec((chunk, positions, width), lambda i: (i, 0, 0)), pl.BlockSpec((8, 128), lambda i: (0, 0))],
        out_shape=[jax.ShapeDtypeStruct((frames, positions, width), HALF), jax.ShapeDtypeStruct((8, 128), WIDE)],
        cost_estimate=cost(PACK),
        compiler_params=params(24),
        name="pack",
    )(*parts)


def split_rows(value, classes):
    high = value.astype(HALF).astype(WIDE)
    middle = (value - high).astype(HALF).astype(WIDE)
    low = value - high - middle
    row = lax.broadcasted_iota(jnp.int32, (EXTRA, classes), 0)
    terms = jnp.where(row == 0, high, jnp.where(row == 1, middle, jnp.where(row == 2, low, 0.0)))
    return terms.astype(HALF)


def softmax_rows(normed, weights, label_ref, block, length):
    height, classes = normed.shape[0], weights.shape[1]
    logits = jnp.dot(normed, weights, preferred_element_type=WIDE)
    if label_ref.shape[0] == 1:
        label_row = label_ref[:, pl.ds(pl.multiple_of(block * height, height), height)]
    else:
        label_row = label_ref[pl.ds(block, 1), :]
    label = jnp.broadcast_to(label_row, (8, height)).T[:, :1]
    slot = block * height + lax.broadcasted_iota(jnp.int32, (height, 1), 0)
    valid = jnp.where(slot < length, 1.0, 0.0).astype(WIDE)
    top = jnp.max(logits, axis=1, keepdims=True)
    shifted = logits - top
    powers = jnp.exp(shifted)
    total = jnp.sum(powers, axis=1, keepdims=True)
    hit = lax.broadcasted_iota(jnp.int32, (height, classes), 1) == label
    picked = jnp.sum(jnp.where(hit, shifted, 0.0), axis=1, keepdims=True)
    loss = jnp.sum(valid * (jnp.log(total) - picked), axis=0, keepdims=True)
    probs = powers * (1.0 / total)
    return (valid * jnp.where(hit, probs - 1.0, probs)).astype(HALF), loss


def norm_rows(values, gain):
    values = values.astype(WIDE)
    inverse = lax.rsqrt(jnp.mean(values * values, axis=1, keepdims=True) + EPS)
    return (values * inverse * gain).astype(HALF)


def forward_near(lengths, labels, gains, rows, pieces):
    height, width = rows[0].shape
    depth, classes = pieces[0].shape
    n_dp, n_gain, n = len(pieces), len(gains), len(rows)

    def body(*refs):
        length_ref, label_ref = refs[:2]
        gain_refs, refs = refs[2 : 2 + n_gain], refs[2 + n_gain :]
        row_refs, refs = refs[:n], refs[n:]
        piece_refs, refs = refs[:n_dp], refs[n_dp:]
        loss_ref, gain_out, weight_ref, normed_ref, slope_ref, sems = refs
        me, dp = lax.axis_index("fsdp"), lax.axis_index("dp")

        def span(i):
            return pl.ds(pl.multiple_of((dp ^ i) * depth, depth), depth)

        copies = [pltpu.make_async_copy(piece_refs[i], weight_ref.at[span(i)], sems.at[i]) for i in range(n_dp)]
        for copy in copies:
            copy.start()
        if gains[0].shape[1] == width:
            gain_out[...] = gain_refs[0][...].astype(WIDE)
        else:
            lines = jnp.concatenate([ref[...].astype(WIDE) for ref in gain_refs], axis=0)
            for i in range(n_dp):
                gain_out[:, span(i)] = lines[i : i + 1]
        gain = gain_out[...]
        for j in range(n):
            normed_ref[j] = norm_rows(row_refs[j][...], gain)
        for copy in copies:
            copy.wait()
        weights = weight_ref[...]
        loss = jnp.zeros((1, 1), WIDE)
        for j in range(n):
            slopes, part = softmax_rows(normed_ref[j], weights, label_ref, me ^ j, length_ref[dp])
            slope_ref[j] = slopes
            loss = loss + part
        loss_ref[...] = jnp.broadcast_to(loss, loss_ref.shape)

    return pl.pallas_call(
        body,
        in_specs=[SMEM] + [VMEM] * (1 + n_gain + n) + [ANY] * n_dp,
        out_specs=[VMEM] * 5,
        out_shape=[
            jax.ShapeDtypeStruct((8, 128), WIDE),
            jax.ShapeDtypeStruct((1, width), WIDE),
            jax.ShapeDtypeStruct((width, classes), HALF),
            jax.ShapeDtypeStruct((n, height, width), HALF),
            jax.ShapeDtypeStruct((n, height, classes), HALF),
        ],
        scratch_shapes=[pltpu.SemaphoreType.DMA((n_dp,))],
        cost_estimate=cost(NEAR),
        compiler_params=params(20),
        name="forward_near",
    )(lengths, labels, *gains, *rows, *pieces)


def forward_far(lengths, labels, gain, weights, rows, normed, slopes, loss, n_dp):
    n = len(rows)
    n_near, height, width = normed.shape
    classes = weights.shape[1]
    depth = width // n_dp
    blocks = n_near + n

    def body(*refs):
        length_ref, label_ref, gain_ref, weight_ref = refs[:4]
        row_refs, refs = refs[4 : 4 + n], refs[4 + n :]
        near_normed, near_slopes, near_loss, loss_ref, slope_ref = refs[:5]
        part_refs, (normed_ref, slopes_ref, partial_ref) = refs[5:-3], refs[-3:]
        me, dp = lax.axis_index("fsdp"), lax.axis_index("dp")
        gain, weights = gain_ref[...], weight_ref[...]
        count = length_ref[0]
        for d in range(1, n_dp):
            count = count + length_ref[d]
        for j in range(n_near):
            normed_ref[j * height : (j + 1) * height, :] = near_normed[j]
            slopes_ref[j * height : (j + 1) * height, :] = near_slopes[j]
        loss = near_loss[:1, :1]
        for j in range(n):
            at = slice((n_near + j) * height, (n_near + j + 1) * height)
            normed_ref[at, :] = norm_rows(row_refs[j][...], gain)
        for j in range(n):
            at = slice((n_near + j) * height, (n_near + j + 1) * height)
            new, part = softmax_rows(normed_ref[at, :], weights, label_ref, me ^ (n_near + j), length_ref[dp])
            slope_ref[j] = new
            slopes_ref[at, :] = new
            loss = loss + part
        loss = jnp.broadcast_to(loss / (count.astype(WIDE) * blocks), (1, classes))
        loss_ref[...] = jnp.broadcast_to(loss, loss_ref.shape)
        step = min(256, width)
        for at in range(0, width, step):
            partial_ref[at : at + step, :] = lax.dot_general(
                normed_ref[:, at : at + step],
                slopes_ref[...],
                (((0,), (0,)), ((), ())),
                preferred_element_type=WIDE,
            ).astype(HALF)
        for i in range(n_dp):
            start = pl.multiple_of((dp ^ i) * depth, depth)
            part_refs[i][:depth, :] = partial_ref[pl.ds(start, depth), :]
        part_refs[n_dp - 1][depth:, :] = split_rows(loss, classes)

    out = pl.pallas_call(
        body,
        in_specs=[SMEM] + [VMEM] * (6 + n),
        out_specs=[VMEM] * (2 + n_dp),
        out_shape=[
            jax.ShapeDtypeStruct((8, classes), WIDE),
            jax.ShapeDtypeStruct((n, height, classes), HALF),
        ]
        + [jax.ShapeDtypeStruct((depth, classes), HALF)] * (n_dp - 1)
        + [jax.ShapeDtypeStruct((depth + EXTRA, classes), HALF)],
        scratch_shapes=[
            pltpu.VMEM((blocks * height, width), HALF),
            pltpu.VMEM((blocks * height, classes), HALF),
            pltpu.VMEM((width, classes), HALF),
        ],
        cost_estimate=cost(FAR),
        compiler_params=params(24),
        name="forward_far",
    )(lengths, labels, gain, weights, *rows, normed, slopes, loss)
    return out[0], out[1], out[2:]


def grad_rows(values, slopes, weights, gain):
    values = values.astype(WIDE)
    inverse = lax.rsqrt(jnp.mean(values * values, axis=1, keepdims=True) + EPS)
    back = lax.dot_general(slopes, weights, (((1,), (1,)), ((), ())), preferred_element_type=WIDE)
    weighted = back * gain
    scale = inverse * inverse * inverse * jnp.mean(weighted * values, axis=1, keepdims=True)
    return (inverse * weighted - values * scale).astype(HALF)


def backward(gain, weights, rows, slopes, after=(), held=()):
    n = len(rows)

    def body(gain_ref, weight_ref, slope_ref, *refs):
        for j in range(n):
            refs[n + len(after) + len(held) + j][...] = grad_rows(refs[j][...], slope_ref[j], weight_ref[...], gain_ref[...])

    return pl.pallas_call(
        body,
        in_specs=[VMEM] * (3 + n) + [ANY] * (len(after) + len(held)),
        out_specs=[VMEM] * n + [ANY] * len(held),
        out_shape=[jax.ShapeDtypeStruct(rows[0].shape, HALF)] * n
        + [jax.ShapeDtypeStruct(h.shape, h.dtype) for h in held],
        input_output_aliases={3 + n + len(after) + i: n + i for i in range(len(held))},
        cost_estimate=cost(BACKWARD),
        compiler_params=params(20),
        name="backward",
    )(gain, weights, slopes, *rows, *after, *held)


def fold(terms, loss=None, held=(), after=(), last=False):
    depth, classes = terms[0].shape
    n = len(terms)
    n_loss = 0 if loss is None else 1
    carries = n_loss and not last

    def body(*refs):
        ins, loss_in = refs[:n], refs[n : n + n_loss]
        outs = refs[n + n_loss + len(held) + len(after) :]
        total = ins[0][...].astype(WIDE)
        for ref in ins[1:]:
            total = total + ref[:depth, :].astype(WIDE)
        outs[0][:depth, :] = total.astype(outs[0].dtype)
        if n_loss:
            extra = ins[-1][depth:, :].astype(WIDE)
            value = loss_in[0][:1, :] + (extra[:1] + extra[1:2] + extra[2:3])
            outs[1][...] = jnp.broadcast_to(value[:, : outs[1].shape[1]], outs[1].shape)
            if carries:
                outs[0][depth:, :] = split_rows(value, classes)

    shapes = [jax.ShapeDtypeStruct((depth + (EXTRA if carries else 0), classes), WIDE if last else HALF)]
    if n_loss:
        shapes.append(jax.ShapeDtypeStruct((8, 128) if last else loss.shape, WIDE))
    out = pl.pallas_call(
        body,
        in_specs=[VMEM] * (n + n_loss) + [ANY] * (len(held) + len(after)),
        out_specs=[VMEM] * (1 + n_loss) + [ANY] * len(held),
        out_shape=shapes + [jax.ShapeDtypeStruct(h.shape, h.dtype) for h in held],
        input_output_aliases={n + n_loss + i: 1 + n_loss + i for i in range(len(held))},
        cost_estimate=cost(LAST if last else RIDE if n_loss else FOLD),
        compiler_params=params(8),
        name="fold",
    )(*terms, *([loss] if n_loss else []), *held, *after)
    return out[0], (out[1] if n_loss else None), out[1 + n_loss :]


def hold(gains, piece, after, claim=None):
    rows = sum(g.shape[0] for g in gains)

    def body(*refs):
        if gains:
            refs[-2][...] = jnp.concatenate([ref[...] for ref in refs[: len(gains)]], axis=0)

    out = pl.pallas_call(
        body,
        in_specs=[VMEM] * len(gains) + [ANY] * (1 + len(after)),
        out_specs=[VMEM] * bool(gains) + [ANY],
        out_shape=[jax.ShapeDtypeStruct((rows, g.shape[1]), HALF) for g in gains[:1]]
        + [jax.ShapeDtypeStruct(piece.shape, HALF)],
        input_output_aliases={len(gains): len(gains[:1])},
        cost_estimate=cost(claim or HOLD),
        compiler_params=params(8),
        name="hold",
    )(*gains, piece, *after)
    return out[0], out[-1]


def ride_end(loss, piece):
    def body(loss_ref, piece_ref, out_ref):
        extra = piece_ref[-EXTRA:, :128].astype(WIDE)
        out_ref[...] = loss_ref[:, :128] + (extra[:1] + extra[1:2] + extra[2:3])

    return pl.pallas_call(
        body,
        in_specs=[VMEM] * 2,
        out_specs=VMEM,
        out_shape=jax.ShapeDtypeStruct((8, 128), WIDE),
        cost_estimate=cost(HOLD),
        compiler_params=params(8),
        name="ride_end",
    )(loss, piece)


def finish(parts, after):
    def body(*refs):
        total = refs[0][...]
        for ref in refs[1 : len(parts)]:
            total = total + ref[...]
        refs[-1][...] = total[:1, :1]

    return pl.pallas_call(
        body,
        in_specs=[VMEM] * len(parts) + [ANY] * len(after),
        out_specs=VMEM,
        out_shape=jax.ShapeDtypeStruct((1, 1), WIDE),
        cost_estimate=cost(FINISH),
        compiler_params=params(4),
        name="finish",
    )(*parts, *after)


def per_device(n_dp, n_fsdp, hidden, head, gain, targets, lengths):
    inner = 2
    line = n_dp // inner

    def swap(value, axis, offset):
        size = n_dp if axis == "dp" else n_fsdp
        return lax.ppermute(value, axis, [(i, i ^ offset) for i in range(size)])

    def exchange(blocks, after, claim=None):
        came = [swap(block, "fsdp", j + 2 & ~1) for j, block in reversed(list(enumerate(blocks)))][::-1]
        return [
            swap(hold([], block, [came[j - 1], *after], claim)[1], "fsdp", 1) if j % 2 else block
            for j, block in enumerate(came)
        ]

    small = gain.shape[1] % 128 == 0 and line == 4
    gains = [gain, swap(gain, "dp", 1)] if small else [gain]
    pieces = [None] * n_dp
    pieces[0] = head[0]
    for o in sorted(range(1, line), key=lambda o: (bin(o).count("1"), -o)):
        bit = o & -o
        if small and o == 3:
            break
        pieces[o * inner] = swap(pieces[(o ^ bit) * inner], "dp", bit * inner)
    own, side, *away, unpacked = unpack(hidden)
    if not small:
        for o in range(line):
            pieces[o * inner + 1] = swap(pieces[o * inner], "dp", 1)
    if small:
        pieces[1] = swap(pieces[0], "dp", 1)
        gain, pieces[1] = hold(gains, pieces[1], [pieces[2]])
        pieces[3] = swap(pieces[1], "dp", 2)
        pieces[4] = hold([], pieces[4], [unpacked])[1]
        pieces[5] = swap(pieces[4], "dp", 1)
        gains = [gain, swap(gain, "dp", 2)]
        gain, own = hold(gains, own, [pieces[4]])
        side = hold([], side, [pieces[3]])[1]
        gains = [gain, swap(gain, "dp", 4)]
        pieces[6] = hold([], swap(pieces[4], "dp", 2), [pieces[3], pieces[5]])[1]
        pieces[7] = swap(pieces[6], "dp", 1)
    else:
        gains = [lax.all_gather(gain, "dp", axis=1, tiled=True)]
    side = swap(side, "fsdp", 1)
    far = exchange(away, gains[1:], RELAY)

    height = targets.shape[0] // n_fsdp
    labels = targets.T if height % 128 == 0 else targets.reshape(n_fsdp, height)
    loss, gain_row, weights, normed, near_slopes = forward_near(lengths, labels, gains, [own, side], pieces)
    loss, far_slopes, parts = forward_far(
        lengths, labels, gain_row, weights, far, normed, near_slopes, loss, n_dp
    )

    far = backward(gain_row, weights, far, far_slopes)
    near = None
    first = [swap(parts[inner + 1], "dp", inner), swap(parts[inner], "dp", inner)]
    across = [None] * line
    waiting = list(range(line - 1, 1, -1))
    for o in waiting[:2]:
        across[o] = swap(parts[o * inner + 1], "dp", 1)
    waiting = waiting[2:]
    came = [[] for _ in range(line)]
    rides = line - 1
    order = [*far[-1:], first[0]]
    for o in range(line - 1, 1, -1):
        held = [parts[waiting[0] * inner + 1]] if waiting else []
        if o == rides:
            piece, loss, held = fold([parts[o * inner], across[o], *came[o]], loss, held, order)
        else:
            piece, _, held = fold([parts[o * inner], *came[o], across[o]], None, held, order)
        bit, order = o & -o, [piece]
        if near is None:
            near = backward(gain_row, weights, [own, side], near_slopes, [loss])
            beside = swap(near[1], "fsdp", 1)
        moved = swap(piece, "dp", bit * inner)
        if o == rides:
            rides = o ^ bit
            came[rides] = [*came[rides], moved]
        else:
            came[o ^ bit] = [moved, *came[o ^ bit]]
        if held:
            across[waiting.pop(0)] = swap(held[0], "dp", 1)
    both, _, _ = fold([parts[1], first[0]], None, (), near[-1:])
    across[0] = swap(both, "dp", 1)
    came[0] = [first[1], *came[0]]
    loss = ride_end(loss, came[0][-1])

    grad_hidden, packed = pack([near[0], beside, *exchange(far, order)])

    grad_head = fold([parts[0], across[0], *came[0]], None, (), [], last=True)[0]

    parts = [loss] + [swap(loss, "fsdp", j) for j in range(1, n_fsdp)]
    return finish(parts, [packed])[0, 0], grad_hidden, grad_head[None]


def solution(mesh):
    n_dp, n_fsdp = mesh.shape["dp"], mesh.shape["fsdp"]
    placed = (
        P(("dp", "fsdp"), None, None),
        P("fsdp", "dp", None),
        P("fsdp", "dp"),
        P("dp", "fsdp"),
        P(),
    )
    return jax.shard_map(
        lambda *args: per_device(n_dp, n_fsdp, *args),
        mesh=mesh,
        in_specs=placed,
        out_specs=(P(), P(("dp", "fsdp"), None, None), P("fsdp", "dp", None)),
        check_vma=False,
    )
```

```python
import jax
import jax.numpy as jnp
from jax import lax
from jax.experimental import pallas as pl
from jax.experimental.pallas import tpu as pltpu
from jax.sharding import PartitionSpec as P

EPS = 1e-05
WIDE = jnp.float32
HALF = jnp.bfloat16
VMEM = pl.BlockSpec(memory_space=pltpu.VMEM)
SMEM = pl.BlockSpec(memory_space=pltpu.SMEM)
ANY = pl.BlockSpec(memory_space=pl.ANY)
PACK_ROWS = 256
EXTRA = 8
UNPACK, PACK, NEAR, FAR, BACKWARD, FOLD, HOLD, LAST, RELAY, FINISH, RIDE = 0.01, 0.01, 3, 0.01, 0.01, 0.01, 0.01, 3, 1.5, 0.01, 0.01


def params(mib):
    return pltpu.CompilerParams(vmem_limit_bytes=mib * 1024 * 1024)


def cost(gigaflops):
    return pl.CostEstimate(flops=int(gigaflops * 1e9), bytes_accessed=0, transcendentals=0)


def unpack(hidden):
    frames, positions, width = hidden.shape
    chunk = PACK_ROWS // positions
    rows = chunk * positions
    steps = frames // chunk

    def body(hidden_ref, *refs):
        outs, (stage, sems) = refs[:-2], refs[-2:]
        copies = [
            pltpu.make_async_copy(
                hidden_ref.at[pl.ds(i * chunk, chunk)], stage.at[pl.ds(i * chunk, chunk)], sems.at[i]
            )
            for i in range(steps)
        ]
        for copy in copies:
            copy.start()
        me = lax.axis_index("fsdp")
        r = lax.broadcasted_iota(jnp.int32, (rows, rows), 0)
        c = lax.broadcasted_iota(jnp.int32, (rows, rows), 1)
        pick = (lax.rem(r, chunk) == lax.div(c, positions)) & (
            lax.rem(c, positions) == (lax.div(r, chunk) ^ me)
        )
        pick = pick.astype(HALF)
        for i in range(steps):
            copies[i].wait()
            here = slice(i * chunk, (i + 1) * chunk)
            flat = stage[here].reshape(rows, width)
            moved = jnp.dot(pick, flat, preferred_element_type=WIDE).astype(HALF)
            for j in range(positions):
                part = moved[j * chunk : (j + 1) * chunk]
                outs[j][here, :] = part
        outs[-1][...] = jnp.zeros_like(outs[-1])

    return pl.pallas_call(
        body,
        in_specs=[ANY],
        out_specs=[VMEM] * (positions + 1),
        out_shape=[jax.ShapeDtypeStruct((frames, width), HALF)] * positions
        + [jax.ShapeDtypeStruct((8, 128), WIDE)],
        scratch_shapes=[pltpu.VMEM(hidden.shape, HALF), pltpu.SemaphoreType.DMA((steps,))],
        cost_estimate=cost(UNPACK),
        compiler_params=params(58),
        name="unpack",
    )(hidden)


def pack(parts):
    frames, width = parts[0].shape
    positions = len(parts)
    chunk = PACK_ROWS // positions
    rows = chunk * positions

    def body(*refs):
        me = lax.axis_index("fsdp")
        r = lax.broadcasted_iota(jnp.int32, (rows, rows), 0)
        c = lax.broadcasted_iota(jnp.int32, (rows, rows), 1)
        pick = (lax.rem(c, chunk) == lax.div(r, positions)) & (
            lax.rem(r, positions) == (lax.div(c, chunk) ^ me)
        )
        flat = jnp.concatenate([ref[...] for ref in refs[:-2]], axis=0)
        moved = jnp.dot(pick.astype(HALF), flat, preferred_element_type=WIDE).astype(HALF)
        refs[-2][...] = moved.reshape(chunk, positions, width)
        refs[-1][...] = jnp.zeros_like(refs[-1])

    return pl.pallas_call(
        body,
        grid=(frames // chunk,),
        in_specs=[pl.BlockSpec((chunk, width), lambda i: (i, 0))] * positions,
        out_specs=[pl.BlockSpec((chunk, positions, width), lambda i: (i, 0, 0)), pl.BlockSpec((8, 128), lambda i: (0, 0))],
        out_shape=[jax.ShapeDtypeStruct((frames, positions, width), HALF), jax.ShapeDtypeStruct((8, 128), WIDE)],
        cost_estimate=cost(PACK),
        compiler_params=params(24),
        name="pack",
    )(*parts)


def split_rows(value, classes):
    high = value.astype(HALF).astype(WIDE)
    middle = (value - high).astype(HALF).astype(WIDE)
    low = value - high - middle
    row = lax.broadcasted_iota(jnp.int32, (EXTRA, classes), 0)
    terms = jnp.where(row == 0, high, jnp.where(row == 1, middle, jnp.where(row == 2, low, 0.0)))
    return terms.astype(HALF)


def softmax_rows(normed, weights, label_ref, block, length):
    height, classes = normed.shape[0], weights.shape[1]
    logits = jnp.dot(normed, weights, preferred_element_type=WIDE)
    if label_ref.shape[0] == 1:
        label_row = label_ref[:, pl.ds(pl.multiple_of(block * height, height), height)]
    else:
        label_row = label_ref[pl.ds(block, 1), :]
    label = jnp.broadcast_to(label_row, (8, height)).T[:, :1]
    slot = block * height + lax.broadcasted_iota(jnp.int32, (height, 1), 0)
    valid = jnp.where(slot < length, 1.0, 0.0).astype(WIDE)
    top = jnp.max(logits, axis=1, keepdims=True)
    shifted = logits - top
    powers = jnp.exp(shifted)
    total = jnp.sum(powers, axis=1, keepdims=True)
    hit = lax.broadcasted_iota(jnp.int32, (height, classes), 1) == label
    picked = jnp.sum(jnp.where(hit, shifted, 0.0), axis=1, keepdims=True)
    loss = jnp.sum(valid * (jnp.log(total) - picked), axis=0, keepdims=True)
    probs = powers * (1.0 / total)
    return (valid * jnp.where(hit, probs - 1.0, probs)).astype(HALF), loss


def norm_rows(values, gain):
    values = values.astype(WIDE)
    inverse = lax.rsqrt(jnp.mean(values * values, axis=1, keepdims=True) + EPS)
    return (values * inverse * gain).astype(HALF)


def forward_near(lengths, labels, gains, rows, pieces):
    height, width = rows[0].shape
    depth, classes = pieces[0].shape
    n_dp, n_gain, n = len(pieces), len(gains), len(rows)

    def body(*refs):
        length_ref, label_ref = refs[:2]
        gain_refs, refs = refs[2 : 2 + n_gain], refs[2 + n_gain :]
        row_refs, refs = refs[:n], refs[n:]
        piece_refs, refs = refs[:n_dp], refs[n_dp:]
        loss_ref, gain_out, weight_ref, normed_ref, slope_ref, sems = refs
        me, dp = lax.axis_index("fsdp"), lax.axis_index("dp")

        def span(i):
            return pl.ds(pl.multiple_of((dp ^ i) * depth, depth), depth)

        copies = [pltpu.make_async_copy(piece_refs[i], weight_ref.at[span(i)], sems.at[i]) for i in range(n_dp)]
        for copy in copies:
            copy.start()
        if gains[0].shape[1] == width:
            gain_out[...] = gain_refs[0][...].astype(WIDE)
        else:
            lines = jnp.concatenate([ref[...].astype(WIDE) for ref in gain_refs], axis=0)
            for i in range(n_dp):
                gain_out[:, span(i)] = lines[i : i + 1]
        gain = gain_out[...]
        for j in range(n):
            normed_ref[j] = norm_rows(row_refs[j][...], gain)
        for copy in copies:
            copy.wait()
        weights = weight_ref[...]
        loss = jnp.zeros((1, 1), WIDE)
        for j in range(n):
            slopes, part = softmax_rows(normed_ref[j], weights, label_ref, me ^ j, length_ref[dp])
            slope_ref[j] = slopes
            loss = loss + part
        loss_ref[...] = jnp.broadcast_to(loss, loss_ref.shape)

    return pl.pallas_call(
        body,
        in_specs=[SMEM] + [VMEM] * (1 + n_gain + n) + [ANY] * n_dp,
        out_specs=[VMEM] * 5,
        out_shape=[
            jax.ShapeDtypeStruct((8, 128), WIDE),
            jax.ShapeDtypeStruct((1, width), WIDE),
            jax.ShapeDtypeStruct((width, classes), HALF),
            jax.ShapeDtypeStruct((n, height, width), HALF),
            jax.ShapeDtypeStruct((n, height, classes), HALF),
        ],
        scratch_shapes=[pltpu.SemaphoreType.DMA((n_dp,))],
        cost_estimate=cost(NEAR),
        compiler_params=params(20),
        name="forward_near",
    )(lengths, labels, *gains, *rows, *pieces)


def forward_far(lengths, labels, gain, weights, rows, normed, slopes, loss, n_dp):
    n = len(rows)
    n_near, height, width = normed.shape
    classes = weights.shape[1]
    depth = width // n_dp
    blocks = n_near + n

    def body(*refs):
        length_ref, label_ref, gain_ref, weight_ref = refs[:4]
        row_refs, refs = refs[4 : 4 + n], refs[4 + n :]
        near_normed, near_slopes, near_loss, loss_ref, slope_ref = refs[:5]
        part_refs, (normed_ref, slopes_ref, partial_ref) = refs[5:-3], refs[-3:]
        me, dp = lax.axis_index("fsdp"), lax.axis_index("dp")
        gain, weights = gain_ref[...], weight_ref[...]
        count = length_ref[0]
        for d in range(1, n_dp):
            count = count + length_ref[d]
        for j in range(n_near):
            normed_ref[j * height : (j + 1) * height, :] = near_normed[j]
            slopes_ref[j * height : (j + 1) * height, :] = near_slopes[j]
        loss = near_loss[:1, :1]
        for j in range(n):
            at = slice((n_near + j) * height, (n_near + j + 1) * height)
            normed_ref[at, :] = norm_rows(row_refs[j][...], gain)
        for j in range(n):
            at = slice((n_near + j) * height, (n_near + j + 1) * height)
            new, part = softmax_rows(normed_ref[at, :], weights, label_ref, me ^ (n_near + j), length_ref[dp])
            slope_ref[j] = new
            slopes_ref[at, :] = new
            loss = loss + part
        loss = jnp.broadcast_to(loss / (count.astype(WIDE) * blocks), (1, classes))
        loss_ref[...] = jnp.broadcast_to(loss, loss_ref.shape)
        step = min(256, width)
        for at in range(0, width, step):
            partial_ref[at : at + step, :] = lax.dot_general(
                normed_ref[:, at : at + step],
                slopes_ref[...],
                (((0,), (0,)), ((), ())),
                preferred_element_type=WIDE,
            ).astype(HALF)
        for i in range(n_dp):
            start = pl.multiple_of((dp ^ i) * depth, depth)
            part_refs[i][:depth, :] = partial_ref[pl.ds(start, depth), :]
        part_refs[n_dp - 1][depth:, :] = split_rows(loss, classes)

    out = pl.pallas_call(
        body,
        in_specs=[SMEM] + [VMEM] * (6 + n),
        out_specs=[VMEM] * (2 + n_dp),
        out_shape=[
            jax.ShapeDtypeStruct((8, classes), WIDE),
            jax.ShapeDtypeStruct((n, height, classes), HALF),
        ]
        + [jax.ShapeDtypeStruct((depth, classes), HALF)] * (n_dp - 1)
        + [jax.ShapeDtypeStruct((depth + EXTRA, classes), HALF)],
        scratch_shapes=[
            pltpu.VMEM((blocks * height, width), HALF),
            pltpu.VMEM((blocks * height, classes), HALF),
            pltpu.VMEM((width, classes), HALF),
        ],
        cost_estimate=cost(FAR),
        compiler_params=params(24),
        name="forward_far",
    )(lengths, labels, gain, weights, *rows, normed, slopes, loss)
    return out[0], out[1], out[2:]


def grad_rows(values, slopes, weights, gain):
    values = values.astype(WIDE)
    inverse = lax.rsqrt(jnp.mean(values * values, axis=1, keepdims=True) + EPS)
    back = lax.dot_general(slopes, weights, (((1,), (1,)), ((), ())), preferred_element_type=WIDE)
    weighted = back * gain
    scale = inverse * inverse * inverse * jnp.mean(weighted * values, axis=1, keepdims=True)
    return (inverse * weighted - values * scale).astype(HALF)


def backward(gain, weights, rows, slopes, after=(), held=()):
    n = len(rows)

    def body(gain_ref, weight_ref, slope_ref, *refs):
        for j in range(n):
            refs[n + len(after) + len(held) + j][...] = grad_rows(refs[j][...], slope_ref[j], weight_ref[...], gain_ref[...])

    return pl.pallas_call(
        body,
        in_specs=[VMEM] * (3 + n) + [ANY] * (len(after) + len(held)),
        out_specs=[VMEM] * n + [ANY] * len(held),
        out_shape=[jax.ShapeDtypeStruct(rows[0].shape, HALF)] * n
        + [jax.ShapeDtypeStruct(h.shape, h.dtype) for h in held],
        input_output_aliases={3 + n + len(after) + i: n + i for i in range(len(held))},
        cost_estimate=cost(BACKWARD),
        compiler_params=params(20),
        name="backward",
    )(gain, weights, slopes, *rows, *after, *held)


def fold(terms, loss=None, held=(), after=(), last=False):
    depth, classes = terms[0].shape
    n = len(terms)
    n_loss = 0 if loss is None else 1
    carries = n_loss and not last

    def body(*refs):
        ins, loss_in = refs[:n], refs[n : n + n_loss]
        outs = refs[n + n_loss + len(held) + len(after) :]
        total = ins[0][...].astype(WIDE)
        for ref in ins[1:]:
            total = total + ref[:depth, :].astype(WIDE)
        outs[0][:depth, :] = total.astype(outs[0].dtype)
        if n_loss:
            extra = ins[-1][depth:, :].astype(WIDE)
            value = loss_in[0][:1, :] + (extra[:1] + extra[1:2] + extra[2:3])
            outs[1][...] = jnp.broadcast_to(value[:, : outs[1].shape[1]], outs[1].shape)
            if carries:
                outs[0][depth:, :] = split_rows(value, classes)

    shapes = [jax.ShapeDtypeStruct((depth + (EXTRA if carries else 0), classes), WIDE if last else HALF)]
    if n_loss:
        shapes.append(jax.ShapeDtypeStruct((8, 128) if last else loss.shape, WIDE))
    out = pl.pallas_call(
        body,
        in_specs=[VMEM] * (n + n_loss) + [ANY] * (len(held) + len(after)),
        out_specs=[VMEM] * (1 + n_loss) + [ANY] * len(held),
        out_shape=shapes + [jax.ShapeDtypeStruct(h.shape, h.dtype) for h in held],
        input_output_aliases={n + n_loss + i: 1 + n_loss + i for i in range(len(held))},
        cost_estimate=cost(LAST if last else RIDE if n_loss else FOLD),
        compiler_params=params(8),
        name="fold",
    )(*terms, *([loss] if n_loss else []), *held, *after)
    return out[0], (out[1] if n_loss else None), out[1 + n_loss :]


def hold(gains, piece, after, claim=None):
    rows = sum(g.shape[0] for g in gains)

    def body(*refs):
        if gains:
            refs[-2][...] = jnp.concatenate([ref[...] for ref in refs[: len(gains)]], axis=0)

    out = pl.pallas_call(
        body,
        in_specs=[VMEM] * len(gains) + [ANY] * (1 + len(after)),
        out_specs=[VMEM] * bool(gains) + [ANY],
        out_shape=[jax.ShapeDtypeStruct((rows, g.shape[1]), HALF) for g in gains[:1]]
        + [jax.ShapeDtypeStruct(piece.shape, HALF)],
        input_output_aliases={len(gains): len(gains[:1])},
        cost_estimate=cost(claim or HOLD),
        compiler_params=params(8),
        name="hold",
    )(*gains, piece, *after)
    return out[0], out[-1]


def ride_end(loss, piece):
    def body(loss_ref, piece_ref, out_ref):
        extra = piece_ref[-EXTRA:, :128].astype(WIDE)
        out_ref[...] = loss_ref[:, :128] + (extra[:1] + extra[1:2] + extra[2:3])

    return pl.pallas_call(
        body,
        in_specs=[VMEM] * 2,
        out_specs=VMEM,
        out_shape=jax.ShapeDtypeStruct((8, 128), WIDE),
        cost_estimate=cost(HOLD),
        compiler_params=params(8),
        name="ride_end",
    )(loss, piece)


def finish(parts, after):
    def body(*refs):
        total = refs[0][...]
        for ref in refs[1 : len(parts)]:
            total = total + ref[...]
        refs[-1][...] = total[:1, :1]

    return pl.pallas_call(
        body,
        in_specs=[VMEM] * len(parts) + [ANY] * len(after),
        out_specs=VMEM,
        out_shape=jax.ShapeDtypeStruct((1, 1), WIDE),
        cost_estimate=cost(FINISH),
        compiler_params=params(4),
        name="finish",
    )(*parts, *after)


def per_device(n_dp, n_fsdp, hidden, head, gain, targets, lengths):
    inner = 2
    line = n_dp // inner

    def swap(value, axis, offset):
        size = n_dp if axis == "dp" else n_fsdp
        return lax.ppermute(value, axis, [(i, i ^ offset) for i in range(size)])

    def exchange(blocks, after, claim=None):
        came = [swap(block, "fsdp", j + 2 & ~1) for j, block in reversed(list(enumerate(blocks)))][::-1]
        return [
            swap(hold([], block, [came[j - 1], *after], claim)[1], "fsdp", 1) if j % 2 else block
            for j, block in enumerate(came)
        ]

    small = gain.shape[1] % 128 == 0 and line == 4
    gains = [gain, swap(gain, "dp", 1)] if small else [gain]
    pieces = [None] * n_dp
    pieces[0] = head[0]
    for o in sorted(range(1, line), key=lambda o: (bin(o).count("1"), -o)):
        bit = o & -o
        if small and o == 3:
            break
        pieces[o * inner] = swap(pieces[(o ^ bit) * inner], "dp", bit * inner)
    own, side, *away, unpacked = unpack(hidden)
    for o in range(line):
        if small and o == 2:
            pieces[4] = hold([], pieces[4], [unpacked])[1]
        if small and o == 1:
            gain, pieces[2] = hold(gains, pieces[2], [pieces[1]])
        if pieces[o * inner] is not None:
            pieces[o * inner + 1] = swap(pieces[o * inner], "dp", 1)
    if small:
        gains = [gain, swap(gain, "dp", 2)]
        gain, side = hold(gains, side, [pieces[4]])
        gains = [gain, swap(gain, "dp", 4)]
        pieces[6] = hold([], swap(pieces[4], "dp", 2), [pieces[3], pieces[5]])[1]
        pieces[7] = swap(pieces[6], "dp", 1)
    else:
        gains = [lax.all_gather(gain, "dp", axis=1, tiled=True)]
    side = swap(side, "fsdp", 1)
    far = exchange(away, gains[1:], RELAY)

    height = targets.shape[0] // n_fsdp
    labels = targets.T if height % 128 == 0 else targets.reshape(n_fsdp, height)
    loss, gain_row, weights, normed, near_slopes = forward_near(lengths, labels, gains, [own, side], pieces)
    loss, far_slopes, parts = forward_far(
        lengths, labels, gain_row, weights, far, normed, near_slopes, loss, n_dp
    )

    far = backward(gain_row, weights, far, far_slopes)
    near = None
    first = [swap(parts[inner + 1], "dp", inner), swap(parts[inner], "dp", inner)]
    across = [None] * line
    waiting = list(range(line - 1, 1, -1))
    for o in waiting[:2]:
        across[o] = swap(parts[o * inner + 1], "dp", 1)
    waiting = waiting[2:]
    came = [[] for _ in range(line)]
    rides = line - 1
    order = [*far[-1:], first[0]]
    for o in range(line - 1, 1, -1):
        held = [parts[waiting[0] * inner + 1]] if waiting else []
        if o == rides:
            piece, loss, held = fold([parts[o * inner], across[o], *came[o]], loss, held, order)
        else:
            piece, _, held = fold([parts[o * inner], *came[o], across[o]], None, held, order)
        bit, order = o & -o, [piece]
        if near is None:
            near = backward(gain_row, weights, [own, side], near_slopes, [loss])
            beside = swap(near[1], "fsdp", 1)
        moved = swap(piece, "dp", bit * inner)
        if o == rides:
            rides = o ^ bit
            came[rides] = [*came[rides], moved]
        else:
            came[o ^ bit] = [moved, *came[o ^ bit]]
        if held:
            across[waiting.pop(0)] = swap(held[0], "dp", 1)
    both, _, _ = fold([parts[1], first[0]], None, (), near[-1:])
    across[0] = swap(both, "dp", 1)
    came[0] = [first[1], *came[0]]
    loss = ride_end(loss, came[0][-1])

    grad_hidden, packed = pack([near[0], beside, *exchange(far, order)])

    grad_head = fold([parts[0], across[0], *came[0]], None, (), [], last=True)[0]

    parts = [loss] + [swap(loss, "fsdp", j) for j in range(1, n_fsdp)]
    return finish(parts, [packed])[0, 0], grad_hidden, grad_head[None]


def solution(mesh):
    n_dp, n_fsdp = mesh.shape["dp"], mesh.shape["fsdp"]
    placed = (
        P(("dp", "fsdp"), None, None),
        P("fsdp", "dp", None),
        P("fsdp", "dp"),
        P("dp", "fsdp"),
        P(),
    )
    return jax.shard_map(
        lambda *args: per_device(n_dp, n_fsdp, *args),
        mesh=mesh,
        in_specs=placed,
        out_specs=(P(), P(("dp", "fsdp"), None, None), P("fsdp", "dp", None)),
        check_vma=False,
    )
```

```python
import jax
import jax.numpy as jnp
from jax import lax
from jax.experimental import pallas as pl
from jax.experimental.pallas import tpu as pltpu
from jax.sharding import PartitionSpec as P

EPS = 1e-05
WIDE = jnp.float32
HALF = jnp.bfloat16
VMEM = pl.BlockSpec(memory_space=pltpu.VMEM)
SMEM = pl.BlockSpec(memory_space=pltpu.SMEM)
ANY = pl.BlockSpec(memory_space=pl.ANY)
PACK_ROWS = 256
EXTRA = 8
UNPACK, PACK, NEAR, FAR, BACKWARD, FOLD, HOLD, LAST, RELAY, FINISH, RIDE = 0.01, 0.01, 3, 0.01, 0.01, 0.01, 0.01, 3, 1.5, 0.01, 0.01


def params(mib):
    return pltpu.CompilerParams(vmem_limit_bytes=mib * 1024 * 1024)


def cost(gigaflops):
    return pl.CostEstimate(flops=int(gigaflops * 1e9), bytes_accessed=0, transcendentals=0)


def unpack(hidden):
    frames, positions, width = hidden.shape
    chunk = PACK_ROWS // positions
    rows = chunk * positions
    steps = frames // chunk

    def body(hidden_ref, *refs):
        outs, (stage, sems) = refs[:-2], refs[-2:]
        copies = [
            pltpu.make_async_copy(
                hidden_ref.at[pl.ds(i * chunk, chunk)], stage.at[pl.ds(i * chunk, chunk)], sems.at[i]
            )
            for i in range(steps)
        ]
        for copy in copies:
            copy.start()
        me = lax.axis_index("fsdp")
        r = lax.broadcasted_iota(jnp.int32, (rows, rows), 0)
        c = lax.broadcasted_iota(jnp.int32, (rows, rows), 1)
        pick = (lax.rem(r, chunk) == lax.div(c, positions)) & (
            lax.rem(c, positions) == (lax.div(r, chunk) ^ me)
        )
        pick = pick.astype(HALF)
        for i in range(steps):
            copies[i].wait()
            here = slice(i * chunk, (i + 1) * chunk)
            flat = stage[here].reshape(rows, width)
            moved = jnp.dot(pick, flat, preferred_element_type=WIDE).astype(HALF)
            for j in range(positions):
                part = moved[j * chunk : (j + 1) * chunk]
                outs[j][here, :] = part
        outs[-1][...] = jnp.zeros_like(outs[-1])

    return pl.pallas_call(
        body,
        in_specs=[ANY],
        out_specs=[VMEM] * (positions + 1),
        out_shape=[jax.ShapeDtypeStruct((frames, width), HALF)] * positions
        + [jax.ShapeDtypeStruct((8, 128), WIDE)],
        scratch_shapes=[pltpu.VMEM(hidden.shape, HALF), pltpu.SemaphoreType.DMA((steps,))],
        cost_estimate=cost(UNPACK),
        compiler_params=params(58),
        name="unpack",
    )(hidden)


def pack(parts):
    frames, width = parts[0].shape
    positions = len(parts)
    chunk = PACK_ROWS // positions
    rows = chunk * positions

    def body(*refs):
        me = lax.axis_index("fsdp")
        r = lax.broadcasted_iota(jnp.int32, (rows, rows), 0)
        c = lax.broadcasted_iota(jnp.int32, (rows, rows), 1)
        pick = (lax.rem(c, chunk) == lax.div(r, positions)) & (
            lax.rem(r, positions) == (lax.div(c, chunk) ^ me)
        )
        flat = jnp.concatenate([ref[...] for ref in refs[:-2]], axis=0)
        moved = jnp.dot(pick.astype(HALF), flat, preferred_element_type=WIDE).astype(HALF)
        refs[-2][...] = moved.reshape(chunk, positions, width)
        refs[-1][...] = jnp.zeros_like(refs[-1])

    return pl.pallas_call(
        body,
        grid=(frames // chunk,),
        in_specs=[pl.BlockSpec((chunk, width), lambda i: (i, 0))] * positions,
        out_specs=[pl.BlockSpec((chunk, positions, width), lambda i: (i, 0, 0)), pl.BlockSpec((8, 128), lambda i: (0, 0))],
        out_shape=[jax.ShapeDtypeStruct((frames, positions, width), HALF), jax.ShapeDtypeStruct((8, 128), WIDE)],
        cost_estimate=cost(PACK),
        compiler_params=params(24),
        name="pack",
    )(*parts)


def split_rows(value, classes):
    high = value.astype(HALF).astype(WIDE)
    middle = (value - high).astype(HALF).astype(WIDE)
    low = value - high - middle
    row = lax.broadcasted_iota(jnp.int32, (EXTRA, classes), 0)
    terms = jnp.where(row == 0, high, jnp.where(row == 1, middle, jnp.where(row == 2, low, 0.0)))
    return terms.astype(HALF)


def softmax_rows(normed, weights, label_ref, block, length):
    height, classes = normed.shape[0], weights.shape[1]
    logits = jnp.dot(normed, weights, preferred_element_type=WIDE)
    if label_ref.shape[0] == 1:
        label_row = label_ref[:, pl.ds(pl.multiple_of(block * height, height), height)]
    else:
        label_row = label_ref[pl.ds(block, 1), :]
    label = jnp.broadcast_to(label_row, (8, height)).T[:, :1]
    slot = block * height + lax.broadcasted_iota(jnp.int32, (height, 1), 0)
    valid = jnp.where(slot < length, 1.0, 0.0).astype(WIDE)
    top = jnp.max(logits, axis=1, keepdims=True)
    shifted = logits - top
    powers = jnp.exp(shifted)
    total = jnp.sum(powers, axis=1, keepdims=True)
    hit = lax.broadcasted_iota(jnp.int32, (height, classes), 1) == label
    picked = jnp.sum(jnp.where(hit, shifted, 0.0), axis=1, keepdims=True)
    loss = jnp.sum(valid * (jnp.log(total) - picked), axis=0, keepdims=True)
    probs = powers * (1.0 / total)
    return (valid * jnp.where(hit, probs - 1.0, probs)).astype(HALF), loss


def norm_rows(values, gain):
    values = values.astype(WIDE)
    inverse = lax.rsqrt(jnp.mean(values * values, axis=1, keepdims=True) + EPS)
    return (values * inverse * gain).astype(HALF)


def forward_near(lengths, labels, gains, rows, pieces):
    height, width = rows[0].shape
    depth, classes = pieces[0].shape
    n_dp, n_gain, n = len(pieces), len(gains), len(rows)

    def body(*refs):
        length_ref, label_ref = refs[:2]
        gain_refs, refs = refs[2 : 2 + n_gain], refs[2 + n_gain :]
        row_refs, refs = refs[:n], refs[n:]
        piece_refs, refs = refs[:n_dp], refs[n_dp:]
        loss_ref, gain_out, weight_ref, normed_ref, slope_ref, sems = refs
        me, dp = lax.axis_index("fsdp"), lax.axis_index("dp")

        def span(i):
            return pl.ds(pl.multiple_of((dp ^ i) * depth, depth), depth)

        copies = [pltpu.make_async_copy(piece_refs[i], weight_ref.at[span(i)], sems.at[i]) for i in range(n_dp)]
        for copy in copies:
            copy.start()
        if gains[0].shape[1] == width:
            gain_out[...] = gain_refs[0][...].astype(WIDE)
        else:
            lines = jnp.concatenate([ref[...].astype(WIDE) for ref in gain_refs], axis=0)
            for i in range(n_dp):
                gain_out[:, span(i)] = lines[i : i + 1]
        gain = gain_out[...]
        for j in range(n):
            normed_ref[j] = norm_rows(row_refs[j][...], gain)
        for copy in copies:
            copy.wait()
        weights = weight_ref[...]
        loss = jnp.zeros((1, 1), WIDE)
        for j in range(n):
            slopes, part = softmax_rows(normed_ref[j], weights, label_ref, me ^ j, length_ref[dp])
            slope_ref[j] = slopes
            loss = loss + part
        loss_ref[...] = jnp.broadcast_to(loss, loss_ref.shape)

    return pl.pallas_call(
        body,
        in_specs=[SMEM] + [VMEM] * (1 + n_gain + n) + [ANY] * n_dp,
        out_specs=[VMEM] * 5,
        out_shape=[
            jax.ShapeDtypeStruct((8, 128), WIDE),
            jax.ShapeDtypeStruct((1, width), WIDE),
            jax.ShapeDtypeStruct((width, classes), HALF),
            jax.ShapeDtypeStruct((n, height, width), HALF),
            jax.ShapeDtypeStruct((n, height, classes), HALF),
        ],
        scratch_shapes=[pltpu.SemaphoreType.DMA((n_dp,))],
        cost_estimate=cost(NEAR),
        compiler_params=params(20),
        name="forward_near",
    )(lengths, labels, *gains, *rows, *pieces)


def forward_far(lengths, labels, gain, weights, rows, normed, slopes, loss, n_dp):
    n = len(rows)
    n_near, height, width = normed.shape
    classes = weights.shape[1]
    depth = width // n_dp
    blocks = n_near + n

    def body(*refs):
        length_ref, label_ref, gain_ref, weight_ref = refs[:4]
        row_refs, refs = refs[4 : 4 + n], refs[4 + n :]
        near_normed, near_slopes, near_loss, loss_ref, slope_ref = refs[:5]
        part_refs, (normed_ref, slopes_ref, partial_ref) = refs[5:-3], refs[-3:]
        me, dp = lax.axis_index("fsdp"), lax.axis_index("dp")
        gain, weights = gain_ref[...], weight_ref[...]
        count = length_ref[0]
        for d in range(1, n_dp):
            count = count + length_ref[d]
        for j in range(n_near):
            normed_ref[j * height : (j + 1) * height, :] = near_normed[j]
            slopes_ref[j * height : (j + 1) * height, :] = near_slopes[j]
        loss = near_loss[:1, :1]
        for j in range(n):
            at = slice((n_near + j) * height, (n_near + j + 1) * height)
            normed_ref[at, :] = norm_rows(row_refs[j][...], gain)
        for j in range(n):
            at = slice((n_near + j) * height, (n_near + j + 1) * height)
            new, part = softmax_rows(normed_ref[at, :], weights, label_ref, me ^ (n_near + j), length_ref[dp])
            slope_ref[j] = new
            slopes_ref[at, :] = new
            loss = loss + part
        loss = jnp.broadcast_to(loss / (count.astype(WIDE) * blocks), (1, classes))
        loss_ref[...] = jnp.broadcast_to(loss, loss_ref.shape)
        step = min(256, width)
        for at in range(0, width, step):
            partial_ref[at : at + step, :] = lax.dot_general(
                normed_ref[:, at : at + step],
                slopes_ref[...],
                (((0,), (0,)), ((), ())),
                preferred_element_type=WIDE,
            ).astype(HALF)
        for i in range(n_dp):
            start = pl.multiple_of((dp ^ i) * depth, depth)
            part_refs[i][:depth, :] = partial_ref[pl.ds(start, depth), :]
        part_refs[n_dp - 1][depth:, :] = split_rows(loss, classes)

    out = pl.pallas_call(
        body,
        in_specs=[SMEM] + [VMEM] * (6 + n),
        out_specs=[VMEM] * (2 + n_dp),
        out_shape=[
            jax.ShapeDtypeStruct((8, classes), WIDE),
            jax.ShapeDtypeStruct((n, height, classes), HALF),
        ]
        + [jax.ShapeDtypeStruct((depth, classes), HALF)] * (n_dp - 1)
        + [jax.ShapeDtypeStruct((depth + EXTRA, classes), HALF)],
        scratch_shapes=[
            pltpu.VMEM((blocks * height, width), HALF),
            pltpu.VMEM((blocks * height, classes), HALF),
            pltpu.VMEM((width, classes), HALF),
        ],
        cost_estimate=cost(FAR),
        compiler_params=params(24),
        name="forward_far",
    )(lengths, labels, gain, weights, *rows, normed, slopes, loss)
    return out[0], out[1], out[2:]


def grad_rows(values, slopes, weights, gain):
    values = values.astype(WIDE)
    inverse = lax.rsqrt(jnp.mean(values * values, axis=1, keepdims=True) + EPS)
    back = lax.dot_general(slopes, weights, (((1,), (1,)), ((), ())), preferred_element_type=WIDE)
    weighted = back * gain
    scale = inverse * inverse * inverse * jnp.mean(weighted * values, axis=1, keepdims=True)
    return (inverse * weighted - values * scale).astype(HALF)


def backward(gain, weights, rows, slopes, after=(), held=()):
    n = len(rows)

    def body(gain_ref, weight_ref, slope_ref, *refs):
        for j in range(n):
            refs[n + len(after) + len(held) + j][...] = grad_rows(refs[j][...], slope_ref[j], weight_ref[...], gain_ref[...])

    return pl.pallas_call(
        body,
        in_specs=[VMEM] * (3 + n) + [ANY] * (len(after) + len(held)),
        out_specs=[VMEM] * n + [ANY] * len(held),
        out_shape=[jax.ShapeDtypeStruct(rows[0].shape, HALF)] * n
        + [jax.ShapeDtypeStruct(h.shape, h.dtype) for h in held],
        input_output_aliases={3 + n + len(after) + i: n + i for i in range(len(held))},
        cost_estimate=cost(BACKWARD),
        compiler_params=params(20),
        name="backward",
    )(gain, weights, slopes, *rows, *after, *held)


def fold(terms, loss=None, held=(), after=(), last=False):
    depth, classes = terms[0].shape
    n = len(terms)
    n_loss = 0 if loss is None else 1
    carries = n_loss and not last

    def body(*refs):
        ins, loss_in = refs[:n], refs[n : n + n_loss]
        outs = refs[n + n_loss + len(held) + len(after) :]
        total = ins[0][...].astype(WIDE)
        for ref in ins[1:]:
            total = total + ref[:depth, :].astype(WIDE)
        outs[0][:depth, :] = total.astype(outs[0].dtype)
        if n_loss:
            extra = ins[-1][depth:, :].astype(WIDE)
            value = loss_in[0][:1, :] + (extra[:1] + extra[1:2] + extra[2:3])
            outs[1][...] = jnp.broadcast_to(value[:, : outs[1].shape[1]], outs[1].shape)
            if carries:
                outs[0][depth:, :] = split_rows(value, classes)

    shapes = [jax.ShapeDtypeStruct((depth + (EXTRA if carries else 0), classes), WIDE if last else HALF)]
    if n_loss:
        shapes.append(jax.ShapeDtypeStruct((8, 128) if last else loss.shape, WIDE))
    out = pl.pallas_call(
        body,
        in_specs=[VMEM] * (n + n_loss) + [ANY] * (len(held) + len(after)),
        out_specs=[VMEM] * (1 + n_loss) + [ANY] * len(held),
        out_shape=shapes + [jax.ShapeDtypeStruct(h.shape, h.dtype) for h in held],
        input_output_aliases={n + n_loss + i: 1 + n_loss + i for i in range(len(held))},
        cost_estimate=cost(LAST if last else RIDE if n_loss else FOLD),
        compiler_params=params(8),
        name="fold",
    )(*terms, *([loss] if n_loss else []), *held, *after)
    return out[0], (out[1] if n_loss else None), out[1 + n_loss :]


def hold(gains, piece, after, claim=None):
    rows = sum(g.shape[0] for g in gains)

    def body(*refs):
        if gains:
            refs[-2][...] = jnp.concatenate([ref[...] for ref in refs[: len(gains)]], axis=0)

    out = pl.pallas_call(
        body,
        in_specs=[VMEM] * len(gains) + [ANY] * (1 + len(after)),
        out_specs=[VMEM] * bool(gains) + [ANY],
        out_shape=[jax.ShapeDtypeStruct((rows, g.shape[1]), HALF) for g in gains[:1]]
        + [jax.ShapeDtypeStruct(piece.shape, HALF)],
        input_output_aliases={len(gains): len(gains[:1])},
        cost_estimate=cost(claim or HOLD),
        compiler_params=params(8),
        name="hold",
    )(*gains, piece, *after)
    return out[0], out[-1]


def ride_end(loss, piece):
    def body(loss_ref, piece_ref, out_ref):
        extra = piece_ref[-EXTRA:, :128].astype(WIDE)
        out_ref[...] = loss_ref[:, :128] + (extra[:1] + extra[1:2] + extra[2:3])

    return pl.pallas_call(
        body,
        in_specs=[VMEM] * 2,
        out_specs=VMEM,
        out_shape=jax.ShapeDtypeStruct((8, 128), WIDE),
        cost_estimate=cost(HOLD),
        compiler_params=params(8),
        name="ride_end",
    )(loss, piece)


def finish(parts, after):
    def body(*refs):
        total = refs[0][...]
        for ref in refs[1 : len(parts)]:
            total = total + ref[...]
        refs[-1][...] = total[:1, :1]

    return pl.pallas_call(
        body,
        in_specs=[VMEM] * len(parts) + [ANY] * len(after),
        out_specs=VMEM,
        out_shape=jax.ShapeDtypeStruct((1, 1), WIDE),
        cost_estimate=cost(FINISH),
        compiler_params=params(4),
        name="finish",
    )(*parts, *after)


def per_device(n_dp, n_fsdp, hidden, head, gain, targets, lengths):
    inner = 2
    line = n_dp // inner

    def swap(value, axis, offset):
        size = n_dp if axis == "dp" else n_fsdp
        return lax.ppermute(value, axis, [(i, i ^ offset) for i in range(size)])

    def exchange(blocks, after, claim=None):
        came = [swap(block, "fsdp", j + 2 & ~1) for j, block in reversed(list(enumerate(blocks)))][::-1]
        return [
            swap(hold([], block, [came[j - 1], *after], claim)[1], "fsdp", 1) if j % 2 else block
            for j, block in enumerate(came)
        ]

    small = gain.shape[1] % 128 == 0 and line == 4
    gains = [gain, swap(gain, "dp", 1)] if small else [gain]
    pieces = [None] * n_dp
    pieces[0] = head[0]
    for o in sorted(range(1, line), key=lambda o: (bin(o).count("1"), -o)):
        bit = o & -o
        if small and o == 3:
            break
        pieces[o * inner] = swap(pieces[(o ^ bit) * inner], "dp", bit * inner)
    own, side, *away, unpacked = unpack(hidden)
    for o in range(line):
        if small and o == 2:
            pieces[4] = hold([], pieces[4], [unpacked])[1]
        if small and o == 1:
            gain, pieces[2] = hold(gains, pieces[2], [pieces[1]])
        if pieces[o * inner] is not None:
            pieces[o * inner + 1] = swap(pieces[o * inner], "dp", 1)
    if small:
        gains = [gain, swap(gain, "dp", 2)]
        gain, side = hold(gains, side, [pieces[4]])
        gains = [gain, swap(gain, "dp", 4)]
        pieces[6] = hold([], swap(pieces[4], "dp", 2), [pieces[3], pieces[5]])[1]
        pieces[7] = swap(pieces[6], "dp", 1)
    else:
        gains = [lax.all_gather(gain, "dp", axis=1, tiled=True)]
    side = swap(side, "fsdp", 1)
    far = exchange(away, gains[1:], RELAY)

    height = targets.shape[0] // n_fsdp
    labels = targets.T if height % 128 == 0 else targets.reshape(n_fsdp, height)
    loss, gain_row, weights, normed, near_slopes = forward_near(lengths, labels, gains, [own, side], pieces)
    loss, far_slopes, parts = forward_far(
        lengths, labels, gain_row, weights, far, normed, near_slopes, loss, n_dp
    )

    far = backward(gain_row, weights, far, far_slopes)
    near = None
    first = [swap(parts[inner + 1], "dp", inner), swap(parts[inner], "dp", inner)]
    across = [None] * line
    waiting = list(range(line - 1, 1, -1))
    for o in waiting[:2]:
        across[o] = swap(parts[o * inner + 1], "dp", 1)
    waiting = waiting[2:]
    came = [[] for _ in range(line)]
    rides = line - 1
    order = [*far[-1:], first[0]]
    for o in range(line - 1, 1, -1):
        held = [parts[waiting[0] * inner + 1]] if waiting else []
        if o == rides:
            piece, loss, held = fold([parts[o * inner], across[o], *came[o]], loss, held, order)
        else:
            piece, _, held = fold([parts[o * inner], *came[o], across[o]], None, held, order)
        bit, order = o & -o, [piece]
        if near is None:
            near = backward(gain_row, weights, [own, side], near_slopes, [loss])
            beside = swap(near[1], "fsdp", 1)
        moved = swap(piece, "dp", bit * inner)
        if o == rides:
            rides = o ^ bit
            came[rides] = [*came[rides], moved]
        else:
            came[o ^ bit] = [moved, *came[o ^ bit]]
        if held:
            across[waiting.pop(0)] = swap(held[0], "dp", 1)
    both, _, _ = fold([parts[1], first[0]], None, (), near[-1:])
    across[0] = swap(both, "dp", 1)
    came[0] = [first[1], *came[0]]
    loss = ride_end(loss, came[0][-1])

    grad_hidden, packed = pack([near[0], beside, *exchange(far, order)])

    grad_head = fold([parts[0], across[0], *came[0]], None, (), [], last=True)[0]

    bit = n_fsdp // 2
    while bit > 1:
        loss = loss + swap(loss, "fsdp", bit)
        bit //= 2
    parts = [loss, swap(loss, "fsdp", bit)]
    return finish(parts, [packed])[0, 0], grad_hidden, grad_head[None]


def solution(mesh):
    n_dp, n_fsdp = mesh.shape["dp"], mesh.shape["fsdp"]
    placed = (
        P(("dp", "fsdp"), None, None),
        P("fsdp", "dp", None),
        P("fsdp", "dp"),
        P("dp", "fsdp"),
        P(),
    )
    return jax.shard_map(
        lambda *args: per_device(n_dp, n_fsdp, *args),
        mesh=mesh,
        in_specs=placed,
        out_specs=(P(), P(("dp", "fsdp"), None, None), P("fsdp", "dp", None)),
        check_vma=False,
    )
```
